32 devices in a mesh: span: 8 (over z, x), elem: 4 (over y, core).
Axes of the slice: x: 2, y: 2, z: 4, core: 2. Of those that a mesh axis runs over, the one named last changes fastest.
Arguments:
- species: float32 [81, 3, 512, 512], P(None, None, 'span', 'elem'), may hold values from 0.02 to 0.3
- laplacian: float32 [81, 3, 512, 512], P(None, None, 'span', 'elem'), may hold values from -6 to 6
- binary: float32 [3, 4], replicated, may hold values from 0.3 to 3
- dref: float32 [3], replicated, may hold values from 0.5 to 2
- stiff_eig: float32 [9], replicated, may hold values from 0.02 to 3
- basis: float32 [9, 9], replicated, may hold values from -1 to 1, as said below
- rounds: int32 [256], replicated, may hold values from 1 to 4
- adjacency: int32 [512, 4], P('elem'), may hold values from 0 to 511, as said below
- edge_map: int32 [512, 4], P('elem'), may hold values from 0 to 3
Outputs:
- updated: float32 [81, 3, 512, 512], P(None, None, 'span', 'elem')
The draws below stay inside these ranges and needn't reach their ends.
Inputs may be any that keep to these rules, and one draw needn't show every extreme that they name: basis is an orthogonal matrix. The elements form a periodic mesh of 16 columns and 8 * 4 rows; each index of elem holds 8 whole rows in some order. adjacency is symmetric: element e lies across edge edge_map[e, j] of element adjacency[e, j]. The element across an edge lies on the same index of elem or on the one just before or after it, cyclically; exactly 16 elements of each index have an edge facing the next index and 16 one facing the previous, one such edge each.
All inputs are finite; a program needn't handle non-finite values.
Results may differ from the reference program's by a relative error of at most 0.0001.
Values sent between devices are 32-bit elements; how exact they have to be, the bound alone decides.
No kernel may reach another device: no remote copies, remote signals or barrier semaphores. Data moves between devices by JAX's collectives and lax.ppermute only.
A program may use at most 128 MiB of HBM per device.

```python
import math
import jax
import jax.numpy as jnp
import numpy as np
from jax import lax

NP = 9
NN = 81
SPECIES = 3
NZ = 512
MODES = 256
MESH_X = 16
ROWS_DEV = 8
ELEM_DEV = 128
ELEM = 512
N_ELEM = 4


def draw_basis(key, part):
    raw_draw = jax.random.normal(key, (NP, NP), jnp.float32)
    columns = []
    for index in range(NP):
        vector = raw_draw[:, index]
        for repeat in range(2):
            for other in columns:
                vector = vector - jnp.dot(other, vector) * other
        columns.append(vector / jnp.sqrt(jnp.sum(vector * vector)))
    return jnp.stack(columns, axis=1)


def draw_rounds(key, part):
    mode_ids = jnp.arange(MODES, dtype=jnp.int32)
    baseline = 4 - 4 * mode_ids // MODES
    jitter = jax.random.randint(jax.random.fold_in(key, 3), (MODES,), -1, 2)
    return jnp.clip(baseline + jitter, 1, 4).astype(jnp.int32)


def mesh_tables(key):
    base_key = jax.random.fold_in(key, 5)
    mesh_rows = ROWS_DEV * N_ELEM
    device_keys = jax.random.split(jax.random.fold_in(base_key, 1), N_ELEM)
    orders = jax.vmap(lambda device_key: jax.random.permutation(device_key, ELEM_DEV))(device_keys).astype(jnp.int32)
    rotations = jax.random.randint(jax.random.fold_in(base_key, 2), (mesh_rows, MESH_X), 0, 4)
    row_ids = jnp.arange(mesh_rows, dtype=jnp.int32)[:, None]
    col_ids = jnp.arange(MESH_X, dtype=jnp.int32)[None, :]
    device_ids = row_ids // ROWS_DEV
    within = row_ids % ROWS_DEV * MESH_X + col_ids
    identity = device_ids * ELEM_DEV + orders[device_ids, within]
    adjacency = jnp.zeros((ELEM_DEV * N_ELEM, 4), jnp.int32)
    edge_map = jnp.zeros((ELEM_DEV * N_ELEM, 4), jnp.int32)
    for local_edge in range(4):
        direction = (local_edge + rotations) % 4
        row_step = jnp.where(direction == 0, -1, jnp.where(direction == 2, 1, 0))
        col_step = jnp.where(direction == 1, 1, jnp.where(direction == 3, -1, 0))
        next_row = (row_ids + row_step) % mesh_rows
        next_col = (col_ids + col_step) % MESH_X
        neighbour = identity[next_row, next_col]
        back_edge = (direction + 2 - rotations[next_row, next_col]) % 4
        adjacency = adjacency.at[identity.reshape(-1), local_edge].set(neighbour.reshape(-1).astype(jnp.int32))
        edge_map = edge_map.at[identity.reshape(-1), local_edge].set(back_edge.reshape(-1).astype(jnp.int32))
    return (adjacency, edge_map)


def draw_adjacency(key, part):
    return mesh_tables(key)[0]


def draw_edge_map(key, part):
    return mesh_tables(key)[1]


def block_levels(rng, extent, cuts, least, top_value):
    level = 1.0
    for dim, parts in cuts:
        steps = jax.random.uniform(jax.random.fold_in(jax.random.fold_in(rng, 6), dim), (parts,), jnp.float32, least / len(cuts), top_value / len(cuts))
        level = level * jnp.repeat(jnp.exp(steps), extent[dim] // parts).reshape((-1,) + (1,) * (len(extent) - 1 - dim))
    return level


def noise(rng, extent, width, reach, cuts=(), kind=jnp.bfloat16):
    values = jax.random.normal(rng, extent, jnp.float32) * width
    if len(cuts) > 0:
        values = block_levels(rng, extent, cuts, -0.22, 0.18) * values
    return jnp.clip(values, min=-reach, max=reach).astype(kind)


def setup_inputs(seed: int = 0) -> dict:
    key_list = jax.random.split(jax.random.key(seed), 10)
    return {
        "species": jnp.clip(0.02 + 0.28 * jax.random.uniform(key_list[0], (NN, SPECIES, NZ, ELEM), jnp.float32) ** block_levels(key_list[0], (NN, SPECIES, NZ, ELEM), ((2, 8), (3, 4)), -0.2, 0.2), 0.02, 0.3),
        "laplacian": noise(key_list[1], (NN, SPECIES, NZ, ELEM), 1.0, 6.0, ((2, 8), (3, 4)), jnp.float32),
        "binary": jnp.clip(jnp.exp(jax.random.uniform(key_list[2], (SPECIES, SPECIES + 1), jnp.float32, math.log(0.3), math.log(3.0))), 0.3, 3.0),
        "dref": jnp.clip(jnp.exp(jax.random.uniform(key_list[3], (SPECIES,), jnp.float32, math.log(0.5), math.log(2.0))), 0.5, 2.0),
        "stiff_eig": jnp.clip(jnp.exp(jax.random.uniform(key_list[4], (NP,), jnp.float32, math.log(0.02), math.log(3.0))), 0.02, 3.0),
        "basis": draw_basis(jax.random.fold_in(key_list[9], 71), 0),
        "rounds": draw_rounds(jax.random.fold_in(key_list[9], 71), 0),
        "adjacency": draw_adjacency(jax.random.fold_in(key_list[9], 71), 0),
        "edge_map": draw_edge_map(jax.random.fold_in(key_list[9], 71), 0),
    }


coupling = 0.2
highest = lax.Precision.HIGHEST


def edge_lists(per_side):
    last_node = per_side - 1
    bottom = [i for i in range(per_side)]
    right_edge = [i * per_side + last_node for i in range(per_side)]
    top_edge = [last_node * per_side + last_node - i for i in range(per_side)]
    left_edge = [(last_node - i) * per_side for i in range(per_side)]
    return [bottom, right_edge, top_edge, left_edge]


def edge_matrix(per_side):
    edge_table = np.zeros((4, per_side, per_side * per_side), np.float32)
    for edge_id, node_list in enumerate(edge_lists(per_side)):
        for i, node_id in enumerate(node_list):
            edge_table[edge_id, i, node_id] = 1.0
    return edge_table


def mixture_source(species, laplacian, binary, dref):
    n_species = species.shape[1]
    bath_share = 1.0 - jnp.sum(species, axis=1)
    source_parts = []
    for s in range(n_species):
        resistance = bath_share / binary[s, n_species]
        for j in range(n_species):
            if j != s:
                resistance = resistance + species[:, j] / binary[s, j]
        mixture = (1.0 - species[:, s]) / resistance
        source_parts.append((species[:, s] + (mixture - dref[s]) * laplacian[:, s]) / dref[s])
    return jnp.stack(source_parts, axis=1)


def block_inverse(values, kron_basis, inverse_diag):
    n_nodes = values.shape[0]
    inner_part = jnp.dot(kron_basis.T, values.reshape(n_nodes, -1), precision=highest).reshape(values.shape) * inverse_diag
    return jnp.dot(kron_basis, inner_part.reshape(n_nodes, -1), precision=highest).reshape(values.shape)


def reference(species, laplacian, binary, dref, stiff_eig, basis, rounds, adjacency, edge_map):
    per_side = basis.shape[0]
    n_nodes = per_side * per_side
    species = jnp.transpose(species, (0, 1, 3, 2))
    laplacian = jnp.transpose(laplacian, (0, 1, 3, 2))
    source = mixture_source(species, laplacian, binary, dref)
    spectrum = jnp.fft.rfft(source, axis=3)[..., :MODES] / NZ
    modal_rhs = jnp.stack([jnp.real(spectrum), jnp.imag(spectrum)], axis=3)
    wavenumber = jnp.arange(MODES).astype(source.dtype) * (8.0 / NZ)
    shifts = 1.0 / dref[:, None] + (wavenumber * wavenumber)[None, :]
    eig_sum = (stiff_eig[:, None] + stiff_eig[None, :]).reshape(n_nodes)
    inverse_diag = 1.0 / (shifts[None, :, None, None, :] + eig_sum[:, None, None, None, None])
    kron_basis = (basis[:, None, :, None] * basis[None, :, None, :]).reshape(n_nodes, n_nodes)
    flat_index = np.array(edge_lists(per_side)).reshape(-1)
    scatter_table = edge_matrix(per_side)

    def couple(modal_field):
        traces = modal_field[flat_index].reshape((4, per_side) + modal_field.shape[1:])
        across = traces[edge_map, :, :, adjacency][:, :, ::-1]
        return jnp.einsum("jtn,ejtsrm->nserm", scatter_table, across, precision=highest)

    modal = block_inverse(modal_rhs, kron_basis, inverse_diag)
    for sweep_id in range(1, 4):
        proposal = block_inverse(modal_rhs + coupling * couple(modal), kron_basis, inverse_diag)
        modal = jnp.where(sweep_id < rounds, proposal, modal)
    complex_modes = modal[:, :, :, 0] + 1j * modal[:, :, :, 1]
    padded = jnp.concatenate([complex_modes, jnp.zeros_like(complex_modes[..., :1])], axis=3)
    result = jnp.fft.irfft(padded, n=NZ, axis=3) * NZ
    return jnp.transpose(result, (0, 1, 3, 2))
```

```python
import functools

import jax
import jax.numpy as jnp
import numpy as np
from jax import lax
from jax.experimental import pallas as pl
from jax.experimental.pallas import tpu as pltpu
from jax.sharding import PartitionSpec as P

MESH_X = 16
LANES = 128
VMEM_BYTES = 48 * 1024 * 1024


coupling = 0.2
highest = lax.Precision.HIGHEST
two_pi = 6.283185307179586
f32 = jnp.float32
bf16 = jnp.bfloat16


def edge_lists(per_side):
    last_node = per_side - 1
    bottom = [i for i in range(per_side)]
    right_edge = [i * per_side + last_node for i in range(per_side)]
    top_edge = [last_node * per_side + last_node - i for i in range(per_side)]
    left_edge = [(last_node - i) * per_side for i in range(per_side)]
    return [bottom, right_edge, top_edge, left_edge]


def row_orders(n_span):
    even = [r ^ (r >> 1 & 1) for r in range(n_span)]
    odd = [r ^ int(2 * r >= n_span) for r in range(n_span)][::-1]
    return [even, odd]


def ring_route(n_span, n_elem, step):
    orders = row_orders(n_span)
    places = [orders[p % 2][r] * n_elem + p for p in range(n_elem) for r in range(n_span)]
    count = len(places)
    return [(places[g], places[(g + step) % count]) for g in range(count)]


def split_terms(values):
    top = values.astype(bf16)
    return top, (values - top.astype(f32)).astype(bf16)


def half_swap(first, second):
    low = lax.broadcasted_iota(jnp.int32, first.shape, 1) < LANES // 2
    left = jnp.where(low, first, pltpu.roll(second, LANES // 2, 1))
    right = jnp.where(low, pltpu.roll(first, LANES // 2, 1), second)
    return left, right


def tables_kernel(n_span, n_elem, place_ref, adj_ref, map_ref, perm_ref, perm2_ref, link_ref):
    own = adj_ref.shape[0]
    span_id, elem_id = place_ref[0], place_ref[1]
    lane = lax.broadcasted_iota(jnp.int32, (own, own), 1).astype(f32)
    sub = lax.broadcasted_iota(jnp.int32, (own, own), 0).astype(f32)
    eye = (lane == sub).astype(f32)
    first_own = (elem_id * own).astype(f32)
    first_next = (lax.rem(elem_id + 1, n_elem) * own).astype(f32)
    first_prev = (lax.rem(elem_id + n_elem - 1, n_elem) * own).astype(f32)

    def wide(ref, j):
        return jnp.broadcast_to(ref[:, j : j + 1].astype(f32), (own, own))

    def turned(column):
        return jnp.sum(eye * column, axis=0, keepdims=True)

    def inside(ids, first):
        return (ids >= first) & (ids < first + own)

    adj_col = [wide(adj_ref, j) for j in range(4)]
    adj_row = [turned(c) for c in adj_col]
    map_row = [turned(wide(map_ref, j)) for j in range(4)]
    near = eye
    for j in range(4):
        near = near + (adj_col[j] - first_own == lane).astype(f32)
    near = near.astype(bf16)
    prev_col = jnp.zeros((own, own), f32)
    next_col = jnp.zeros((own, own), f32)
    for j in range(4):
        prev_col = prev_col + jnp.where(inside(adj_col[j], first_prev), adj_col[j] + 1.0, 0.0)
        next_col = next_col + jnp.where(inside(adj_col[j], first_next), adj_col[j] + 1.0, 0.0)
    reached = (prev_col > 0).astype(f32)
    row_col = 1.0 - reached
    for _ in range(n_span - 2):
        reached = jnp.minimum(
            jnp.dot(near, reached.astype(bf16), preferred_element_type=f32), 1.0
        )
        row_col = row_col + 1.0 - reached
    row_row = turned(row_col)
    same = row_col == row_row
    pos_col = jnp.sum((same & (lane < sub)).astype(f32), axis=1, keepdims=True)
    pos_row = jnp.sum((same & (sub < lane)).astype(f32), axis=0, keepdims=True)
    odd = lax.rem(elem_id, 2) == 1
    orders = row_orders(n_span)
    slot_row = jnp.zeros_like(row_row)
    for r in range(n_span):
        slot = jnp.where(odd, orders[1][r], orders[0][r]).astype(f32)
        slot_row = jnp.where(row_row == float(r), slot, slot_row)
    new_row = slot_row * float(MESH_X) + pos_row
    perm = (sub == new_row).astype(f32).astype(bf16)
    perm_ref[:, :own] = perm
    perm_ref[:, own:] = perm
    perm2_ref[:own] = perm
    perm2_ref[own:] = perm

    rank_prev = jnp.sum(
        ((prev_col > 0) & (prev_col < turned(prev_col))).astype(f32), axis=0, keepdims=True
    )
    rank_next = jnp.sum(
        ((next_col > 0) & (next_col < turned(next_col))).astype(f32), axis=0, keepdims=True
    )
    spot = lax.broadcasted_iota(jnp.int32, (MESH_X, own), 0).astype(f32)
    here = new_row == spot + (span_id * MESH_X).astype(f32)
    spot_lane = lax.broadcasted_iota(jnp.int32, (MESH_X, own), 1).astype(f32)
    edge_up = jnp.zeros_like(row_row)
    edge_down = jnp.zeros_like(row_row)

    def chosen(values):
        return jnp.sum(jnp.where(here, values, 0.0), axis=1, keepdims=True)

    for j in range(4):
        meets = (sub == adj_row[j] - first_own).astype(f32)
        its_pos = jnp.sum(meets * pos_col, axis=0, keepdims=True)
        its_row = jnp.sum(meets * row_col, axis=0, keepdims=True)
        inner = inside(adj_row[j], first_own)
        ahead = inside(adj_row[j], first_next)
        behind = inside(adj_row[j], first_prev)
        up = ahead | (inner & (its_row == row_row + 1.0))
        down = behind | (inner & (its_row == row_row - 1.0))
        its_pos = jnp.where(ahead, rank_next, jnp.where(behind, rank_prev, its_pos))
        base = jnp.where(up, 4.0 * MESH_X, jnp.where(down, 5.0 * MESH_X, map_row[j] * MESH_X))
        edge_up = jnp.where(up, float(j), edge_up)
        edge_down = jnp.where(down, float(j), edge_down)
        row = (spot_lane == chosen(base + its_pos)).astype(f32).astype(bf16)
        link_ref[j * MESH_X : (j + 1) * MESH_X, :own] = row
        link_ref[j * MESH_X : (j + 1) * MESH_X, own:] = row
    for place, edge in ((4, edge_up), (5, edge_down)):
        row = (spot_lane == chosen(edge * MESH_X) + spot).astype(f32).astype(bf16)
        link_ref[place * MESH_X : (place + 1) * MESH_X, :own] = row
        link_ref[place * MESH_X : (place + 1) * MESH_X, own:] = row


def mesh_tables(adjacency, edge_map, n_span, n_elem):
    own = adjacency.shape[0]
    place = jnp.stack([lax.axis_index("span"), lax.axis_index("elem")]).astype(jnp.int32)
    return pl.pallas_call(
        functools.partial(tables_kernel, n_span, n_elem),
        out_shape=(
            jax.ShapeDtypeStruct((own, 2 * own), bf16),
            jax.ShapeDtypeStruct((2 * own, own), bf16),
            jax.ShapeDtypeStruct((6 * MESH_X, 2 * own), bf16),
        ),
        in_specs=[
            pl.BlockSpec(memory_space=pltpu.SMEM),
            pl.BlockSpec(memory_space=pltpu.VMEM),
            pl.BlockSpec(memory_space=pltpu.VMEM),
        ],
        out_specs=[pl.BlockSpec(memory_space=pltpu.VMEM)] * 3,
        name="mesh_tables",
    )(place, adjacency, edge_map)


def source_kernel(s, n_nodes, inv_ref, dref_ref, species_ref, lap_ref, perm_ref, out_ref):
    n_species = species_ref.shape[1]
    per_step = species_ref.shape[0]
    zl = species_ref.shape[2]
    n_span = out_ref.shape[0]
    perm = perm_ref[...]

    def source(n):
        parts = [species_ref[n, j] for j in range(n_species)]
        bath = 1.0 - sum(parts[1:], parts[0])
        resistance = bath * inv_ref[s, n_species]
        for j in range(n_species):
            if j != s:
                resistance = resistance + parts[j] * inv_ref[s, j]
        mixture = (1.0 - parts[s]) / resistance
        return (parts[s] + (mixture - dref_ref[s]) * lap_ref[n, 0]) / dref_ref[s]

    def turned(first, second):
        top, rest = split_terms(jnp.concatenate([first, second], axis=0))
        both = jnp.concatenate([top, rest], axis=1)
        return lax.dot_general(
            perm, both, (((1,), (1,)), ((), ())), preferred_element_type=f32
        )

    def pair(k, carry):
        tile = turned(source(2 * k), source(2 * k + 1))
        row = pl.multiple_of(k * MESH_X, MESH_X)
        for q in range(n_span):
            out_ref[q, pl.ds(row, MESH_X), :] = tile[q * MESH_X : (q + 1) * MESH_X]
        return carry

    last_step = pl.num_programs(0) - 1

    @pl.when(pl.program_id(0) < last_step)
    def _():
        lax.fori_loop(0, per_step // 2, pair, 0, unroll=2)

    @pl.when(pl.program_id(0) == last_step)
    def _():
        value = source(0)
        tile = turned(value, value)
        half = MESH_X // 2
        low = lax.broadcasted_iota(jnp.int32, (half, 2 * zl), 1) < zl
        for q in range(n_span):
            block = tile[q * MESH_X : (q + 1) * MESH_X]
            out_ref[q, :half, :] = jnp.where(low, block[:half], block[half:])


def packed_source(s, species, laplacian, inv_binary, dref, perm, n_span):
    n_nodes, n_species, zl, own = species.shape
    step = MESH_X
    steps = n_nodes // step + 1
    rows = n_nodes * MESH_X // 2
    return pl.pallas_call(
        functools.partial(source_kernel, s, n_nodes),
        grid=(steps,),
        out_shape=jax.ShapeDtypeStruct((n_span, rows, 2 * zl), f32),
        in_specs=[
            pl.BlockSpec(memory_space=pltpu.SMEM),
            pl.BlockSpec(memory_space=pltpu.SMEM),
            pl.BlockSpec((step, n_species, zl, own), lambda g: (g, 0, 0, 0)),
            pl.BlockSpec((step, 1, zl, own), lambda g: (g, s, 0, 0)),
            pl.BlockSpec((own, 2 * own), lambda g: (0, 0)),
        ],
        out_specs=pl.BlockSpec((n_span, step * MESH_X // 2, 2 * zl), lambda g: (0, g, 0)),
        compiler_params=pltpu.CompilerParams(vmem_limit_bytes=VMEM_BYTES),
        cost_estimate=pl.CostEstimate(
            flops=int(species.size) * 60, bytes_accessed=int(species.size) * 7, transcendentals=0
        ),
        name="packed_source",
    )(inv_binary, dref, species, laplacian, perm)


def unpack_kernel(recv_ref, perm_ref, *refs):
    out_ref = refs[-1]
    n_span = recv_ref.shape[0]
    per_step, _, zl, _ = out_ref.shape
    perm = perm_ref[...]

    def turned(tile):
        top, rest = split_terms(tile)
        both = jnp.concatenate([top, rest], axis=0)
        return lax.dot_general(
            both, perm, (((0,), (0,)), ((), ())), preferred_element_type=f32
        )

    def pair(k, carry):
        row = pl.multiple_of(k * MESH_X, MESH_X)
        tile = jnp.concatenate(
            [recv_ref[q, pl.ds(row, MESH_X), :] for q in range(n_span)], axis=0
        )
        result = turned(tile)
        out_ref[2 * k, 0] = result[:zl]
        out_ref[2 * k + 1, 0] = result[zl:]
        return carry

    last_step = pl.num_programs(0) - 1

    @pl.when(pl.program_id(0) < last_step)
    def _():
        lax.fori_loop(0, per_step // 2, pair, 0, unroll=2)

    @pl.when(pl.program_id(0) == last_step)
    def _():
        half = MESH_X // 2
        blocks = []
        for q in range(n_span):
            block = recv_ref[q, :half, :]
            blocks += [block, pltpu.roll(block, zl, 1)]
        out_ref[0, 0] = turned(jnp.concatenate(blocks, axis=0))[:zl]


def unpacked(s, recv, perm2, shape, before):
    n_nodes, n_species, zl, own = shape
    n_span, rows, width = recv.shape
    step = MESH_X
    steps = n_nodes // step + 1
    operands = [recv, perm2] + ([] if before is None else [before])
    return pl.pallas_call(
        unpack_kernel,
        grid=(steps,),
        out_shape=jax.ShapeDtypeStruct(shape, f32),
        in_specs=[
            pl.BlockSpec((n_span, step * MESH_X // 2, width), lambda g: (0, g, 0)),
            pl.BlockSpec((2 * own, own), lambda g: (0, 0)),
        ]
        + ([] if before is None else [pl.BlockSpec(memory_space=pl.ANY)]),
        out_specs=pl.BlockSpec((step, 1, zl, own), lambda g: (g, s, 0, 0)),
        input_output_aliases={} if before is None else {2: 0},
        compiler_params=pltpu.CompilerParams(vmem_limit_bytes=VMEM_BYTES),
        cost_estimate=pl.CostEstimate(
            flops=int(recv.size) * 512, bytes_accessed=int(recv.size) * 8, transcendentals=0
        ),
        name="unpacked",
    )(*operands)


def node_places(per_side):
    places = {}
    for edge, nodes in enumerate(edge_lists(per_side)):
        for t, node in enumerate(nodes):
            places.setdefault(node, []).append((edge, t))
    return places


def mix(values, weights):
    total = values[0] * weights[0]
    for value, weight in zip(values[1:], weights[1:]):
        total = total + value * weight
    return total


def to_eigen(src, dst, basis_ref, m, cols):
    def body(a, carry):
        xs = [src[a * m + b, :, cols] for b in range(m)]
        for j in range(m):
            dst[a * m + j, :, cols] = mix(xs, [basis_ref[b, j] for b in range(m)])
        return carry

    lax.fori_loop(0, m, body, 0)


def edges_to_eigen(field, dst, basis_ref, m, cols):
    for a in range(m):
        ends = range(m) if a in (0, m - 1) else (0, m - 1)
        xs = [field(a * m + b) for b in ends]
        for j in range(m):
            dst[a * m + j, :, cols] = mix(xs, [basis_ref[b, j] for b in ends])


def columns_to_eigen(src, store, basis_ref, m, cols):
    def body(b, carry):
        xs = [src[a * m + b, :, cols] for a in range(m)]
        for i in range(m):
            store(i * m + b, mix(xs, [basis_ref[a, i] for a in range(m)]))
        return carry

    lax.fori_loop(0, m, body, 0)


def columns_from_eigen(load, dst, basis_ref, m, cols):
    def body(b, carry):
        xs = [load(a * m + b) for a in range(m)]
        for i in range(m):
            dst[i * m + b, :, cols] = mix(xs, [basis_ref[i, a] for a in range(m)])
        return carry

    lax.fori_loop(0, m, body, 0)


def rows_from_eigen(src, store, basis_ref, m, cols):
    def body(i, carry):
        xs = [src[i * m + b, :, cols] for b in range(m)]
        for j in range(m):
            store(i * m + j, mix(xs, [basis_ref[j, b] for b in range(m)]))
        return carry

    lax.fori_loop(0, m, body, 0)


def edge_traces(src, trace_ref, basis_ref, m, cols):
    places = node_places(m)
    for i in range(m):
        xs = [src[i * m + b, :, cols] for b in range(m)]
        for j in range(m) if i in (0, m - 1) else (0, m - 1):
            value = mix(xs, [basis_ref[j, b] for b in range(m)])
            for edge, t in places[i * m + j]:
                trace_ref[t, edge * MESH_X : (edge + 1) * MESH_X, cols] = value


def picked(link, blocks):
    pad = link.shape[1] // 2 - sum(block.shape[0] for block in blocks)
    blocks = blocks + [jnp.zeros((pad, blocks[0].shape[1]), f32)]
    top, rest = split_terms(jnp.concatenate(blocks, axis=0))
    return jnp.dot(link, jnp.concatenate([top, rest], axis=0), preferred_element_type=f32)


def send_traces(trace_ref, link_ref, up_ref, down_ref, m):
    link = link_ref[4 * MESH_X : 6 * MESH_X, :]
    for t in range(m):
        out = picked(link, [trace_ref[t]])
        up_ref[t] = out[:MESH_X]
        down_ref[t] = out[MESH_X:]


def column_blocks(width, block):
    return [slice(c, c + block) for c in range(0, width, block)]


BLOCK = 256


def start_kernel(
    m, basis_ref, recv_ref, top_ref, rest_ref, diag_ref, link_ref,
    w_ref, trace_ref, up_ref, down_ref, xt, xr, y,
):
    n_span, rows, width = recv_ref.shape
    n_nodes = m * m
    planes = top_ref.shape[0]

    def place(node, first, second, tile):
        lanes = slice(tile * LANES, (tile + 1) * LANES)
        for offset, value in ((0, first), (1, second)):
            top, rest = split_terms(value)
            row = pl.multiple_of((node + offset) * MESH_X, MESH_X)
            xt[pl.ds(row, MESH_X), lanes] = top
            xr[pl.ds(row, MESH_X), lanes] = rest

    def pair(k, carry):
        row = pl.multiple_of(k * MESH_X, MESH_X)
        for tile in range(n_span // 2):
            left, right = half_swap(
                recv_ref[2 * tile, pl.ds(row, MESH_X), :],
                recv_ref[2 * tile + 1, pl.ds(row, MESH_X), :],
            )
            place(2 * k, left, right, tile)
        return carry

    lax.fori_loop(0, n_nodes // 2, pair, 0)
    half = MESH_X // 2
    last = n_nodes // 2 * MESH_X
    for tile in range(n_span // 2):
        left, right = half_swap(
            recv_ref[2 * tile, last : last + half, :],
            recv_ref[2 * tile + 1, last : last + half, :],
        )
        lanes = slice(tile * LANES, (tile + 1) * LANES)
        top, rest = split_terms(jnp.concatenate([left, right], axis=0))
        xt[2 * last :, lanes] = top
        xr[2 * last :, lanes] = rest

    chunk = m * MESH_X

    def transform(c, carry):
        rows_c = pl.ds(pl.multiple_of(c * chunk, chunk), chunk)
        top, rest = xt[rows_c, :], xr[rows_c, :]
        out = jnp.dot(top, top_ref[...], preferred_element_type=f32)
        out = out + jnp.dot(rest, top_ref[...], preferred_element_type=f32)
        out = out + jnp.dot(top, rest_ref[...], preferred_element_type=f32)
        y[pl.ds(c * m, m)] = out.reshape(m, MESH_X, planes)
        return carry

    lax.fori_loop(0, m, transform, 0)

    for cols in column_blocks(planes, BLOCK):
        to_eigen(y, y, basis_ref, m, cols)

        def store(n, value, cols=cols):
            w_ref[n, :, cols] = value

        columns_to_eigen(y, store, basis_ref, m, cols)

        def load(n, cols=cols):
            return w_ref[n, :, cols] * diag_ref[n, :, cols]

        columns_from_eigen(load, y, basis_ref, m, cols)
        edge_traces(y, trace_ref, basis_ref, m, cols)
    send_traces(trace_ref, link_ref, up_ref, down_ref, m)


def coupled_values(m, trace_ref, above_ref, below_ref, link_ref, g):
    link = link_ref[: 4 * MESH_X, :]
    for t in range(m):
        back = m - 1 - t
        g[t] = picked(link, [trace_ref[back], above_ref[back], below_ref[back]])


def sweep_values(m, sweep_id, basis_ref, rounds_ref, w_ref, v_ref, diag_ref, g, y, vout, cols):
    places = node_places(m)

    def field(node):
        total = None
        for edge, t in places[node]:
            value = g[t, edge * MESH_X : (edge + 1) * MESH_X, cols]
            total = value if total is None else total + value
        return total * coupling

    edges_to_eigen(field, y, basis_ref, m, cols)
    going = rounds_ref[:, cols] > sweep_id

    def store(n, value):
        vout[n, :, cols] = jnp.where(going, w_ref[n, :, cols] + value, v_ref[n, :, cols])

    columns_to_eigen(y, store, basis_ref, m, cols)

    def load(n):
        return vout[n, :, cols] * diag_ref[n, :, cols]

    columns_from_eigen(load, y, basis_ref, m, cols)


def sweep_kernel(
    m, sweep_id, basis_ref, rounds_ref, w_ref, v_ref, diag_ref, link_ref, trace_ref, above_ref,
    below_ref, vout_ref, tout_ref, up_ref, down_ref, g, y,
):
    width = w_ref.shape[2]
    coupled_values(m, trace_ref, above_ref, below_ref, link_ref, g)
    for cols in column_blocks(width, min(BLOCK, width)):
        sweep_values(
            m, sweep_id, basis_ref, rounds_ref, w_ref, v_ref, diag_ref, g, y, vout_ref, cols
        )
        edge_traces(y, tout_ref, basis_ref, m, cols)
    send_traces(tout_ref, link_ref, up_ref, down_ref, m)


def finish_kernel(
    m, sweep_id, basis_ref, rounds_ref, w_ref, v_ref, diag_ref, link_ref, trace_ref, above_ref,
    below_ref, top_ref, rest_ref, out_ref, g, y, vout, mt, mr,
):
    n_nodes = m * m
    n_span = out_ref.shape[0]
    planes = top_ref.shape[0]
    coupled_values(m, trace_ref, above_ref, below_ref, link_ref, g)
    for cols in column_blocks(planes, BLOCK):
        sweep_values(m, sweep_id, basis_ref, rounds_ref, w_ref, v_ref, diag_ref, g, y, vout, cols)

        def store(n, value, cols=cols):
            row = pl.multiple_of(n * MESH_X, MESH_X)
            top, rest = split_terms(value)
            mt[pl.ds(row, MESH_X), cols] = top
            mr[pl.ds(row, MESH_X), cols] = rest

        rows_from_eigen(y, store, basis_ref, m, cols)

    chunk = m * MESH_X

    def transform(c, carry):
        rows_c = pl.ds(pl.multiple_of(c * chunk, chunk), chunk)
        top, rest = mt[rows_c, :], mr[rows_c, :]
        out = jnp.dot(top, top_ref[...], preferred_element_type=f32)
        out = out + jnp.dot(rest, top_ref[...], preferred_element_type=f32)
        out = out + jnp.dot(top, rest_ref[...], preferred_element_type=f32)
        y[pl.ds(c * m, m)] = out.reshape(m, MESH_X, planes)
        return carry

    lax.fori_loop(0, m, transform, 0)

    def pair(k, carry):
        row = pl.multiple_of(k * MESH_X, MESH_X)
        for tile in range(n_span // 2):
            lanes = slice(tile * LANES, (tile + 1) * LANES)
            left, right = half_swap(y[2 * k, :, lanes], y[2 * k + 1, :, lanes])
            out_ref[2 * tile, pl.ds(row, MESH_X), :] = left
            out_ref[2 * tile + 1, pl.ds(row, MESH_X), :] = right
        return carry

    lax.fori_loop(0, n_nodes // 2, pair, 0)
    half = MESH_X // 2
    last = n_nodes // 2 * MESH_X
    for tile in range(n_span // 2):
        lanes = slice(tile * LANES, (tile + 1) * LANES)
        left, right = half_swap(y[n_nodes - 1, :half, lanes], y[n_nodes - 1, half:, lanes])
        out_ref[2 * tile, last : last + half, :] = left
        out_ref[2 * tile + 1, last : last + half, :] = right


def vmem_call(kernel, name, out_shape, scratch, flops, operands):
    bytes_moved = sum(int(x.size) * x.dtype.itemsize for x in list(operands) + list(out_shape))
    smem = pl.BlockSpec(memory_space=pltpu.SMEM)
    vmem = pl.BlockSpec(memory_space=pltpu.VMEM)
    return pl.pallas_call(
        kernel,
        out_shape=tuple(out_shape),
        in_specs=[smem] + [vmem] * (len(operands) - 1),
        out_specs=tuple([vmem] * len(out_shape)),
        scratch_shapes=scratch,
        compiler_params=pltpu.CompilerParams(vmem_limit_bytes=VMEM_BYTES),
        cost_estimate=pl.CostEstimate(
            flops=flops, bytes_accessed=bytes_moved, transcendentals=0
        ),
        name=name,
    )(*operands)


def solve_species(recv, basis, rounds_row, diag, link, forward, backward, n_span, n_elem):
    m = basis.shape[0]
    n_nodes = m * m
    planes = forward[0].shape[0]
    field = jax.ShapeDtypeStruct((n_nodes, MESH_X, planes), f32)
    trace = jax.ShapeDtypeStruct((m, 4 * MESH_X, planes), f32)
    side = jax.ShapeDtypeStruct((m, MESH_X, planes), f32)
    terms = pltpu.VMEM((n_nodes * MESH_X, planes), bf16)
    work = pltpu.VMEM(field.shape, f32)
    gathered = pltpu.VMEM(trace.shape, f32)
    transform_flops = 6 * n_nodes * MESH_X * planes * planes
    mix_flops = 600 * n_nodes * MESH_X * planes
    axes = ("span", "elem")
    to_next = ring_route(n_span, n_elem, 1)
    to_prev = ring_route(n_span, n_elem, -1)

    def exchange(up, down):
        below = lax.ppermute(up, axes, to_next)
        above = lax.ppermute(down, axes, to_prev)
        return above, below

    w, traces, up, down = vmem_call(
        functools.partial(start_kernel, m),
        "start_solve",
        [field, trace, side, side],
        [terms, terms, work],
        transform_flops + mix_flops,
        [basis, recv, forward[0], forward[1], diag, link],
    )
    v = w
    for sweep_id in (1, 2):
        above, below = exchange(up, down)
        v, traces, up, down = vmem_call(
            functools.partial(sweep_kernel, m, sweep_id),
            "sweep_solve",
            [field, trace, side, side],
            [gathered, work],
            mix_flops,
            [basis, rounds_row, w, v, diag, link, traces, above, below],
        )
    above, below = exchange(up, down)
    (result,) = vmem_call(
        functools.partial(finish_kernel, m, 3),
        "finish_solve",
        [jax.ShapeDtypeStruct(recv.shape, f32)],
        [gathered, work, work, terms, terms],
        transform_flops + mix_flops,
        [basis, rounds_row, w, v, diag, link, traces, above, below, backward[0], backward[1]],
    )
    return result


def outer_split(values):
    top = lax.reduce_precision(values, exponent_bits=8, mantissa_bits=7)
    return top.astype(bf16), (values - top).astype(bf16)


def row_body(species, laplacian, binary, dref, stiff_eig, basis, rounds, adjacency, edge_map):
    n_nodes, n_species, zl, own = species.shape
    n_span = lax.axis_size("span")
    n_elem = lax.axis_size("elem")
    planes = zl * n_span
    n_modes = planes // 2
    perm, perm2, link = mesh_tables(adjacency, edge_map, n_span, n_elem)
    inv_binary = 1.0 / binary
    arrived = []
    for s in range(n_species):
        sent = packed_source(s, species, laplacian, inv_binary, dref, perm, n_span)
        arrived.append(lax.all_to_all(sent, "span", split_axis=0, concat_axis=0, tiled=True))

    col_mode = jnp.tile(jnp.arange(n_modes, dtype=jnp.int32), 2)
    col_part = jnp.repeat(jnp.arange(2, dtype=jnp.int32), n_modes)
    table_in, table_out = transform_tables(col_mode, col_part, planes)
    forward = outer_split(table_in)
    backward = outer_split(table_out)
    wavenumber = col_mode.astype(f32) * (8.0 / planes)
    shifts = 1.0 / dref[:, None] + (wavenumber * wavenumber)[None, :]
    eig_sum = (stiff_eig[:, None] + stiff_eig[None, :]).reshape(n_nodes)
    diag = 1.0 / (shifts[:, None, None, :] + eig_sum[None, :, None, None])
    rounds_row = jnp.tile(rounds, 2).reshape(1, planes)

    updated = None
    for s in range(n_species):
        result = solve_species(
            arrived[s], basis, rounds_row, diag[s], link, forward, backward, n_span, n_elem
        )
        back = lax.all_to_all(result, "span", split_axis=0, concat_axis=0, tiled=True)
        updated = unpacked(s, back, perm2, species.shape, updated)
    return updated


def from_behind(block, axis, distance):
    devices = range(lax.axis_size(axis))
    route = [((i - distance) % len(devices), i) for i in devices]
    return lax.ppermute(block, axis, route)


def edge_matrix(per_side):
    edge_table = np.zeros((4, per_side, per_side * per_side), np.float32)
    for edge_id, node_list in enumerate(edge_lists(per_side)):
        for i, node_id in enumerate(node_list):
            edge_table[edge_id, i, node_id] = 1.0
    return edge_table


def mixture_source(species, laplacian, binary, dref):
    n_species = species.shape[1]
    bath_share = 1.0 - jnp.sum(species, axis=1)
    source_parts = []
    for s in range(n_species):
        resistance = bath_share / binary[s, n_species]
        for j in range(n_species):
            if j != s:
                resistance = resistance + species[:, j] / binary[s, j]
        mixture = (1.0 - species[:, s]) / resistance
        source_parts.append((species[:, s] + (mixture - dref[s]) * laplacian[:, s]) / dref[s])
    return jnp.stack(source_parts, axis=1)


def block_inverse(values, kron_basis, inverse_diag):
    n_nodes = values.shape[0]
    inner_part = (
        jnp.dot(kron_basis.T, values.reshape(n_nodes, -1), precision=highest).reshape(values.shape)
        * inverse_diag
    )
    return jnp.dot(kron_basis, inner_part.reshape(n_nodes, -1), precision=highest).reshape(
        values.shape
    )


def transform_tables(col_mode, col_part, planes):
    plane_ids = jnp.arange(planes, dtype=jnp.int32)
    phase_id = plane_ids[:, None] * col_mode[None, :] % planes
    angles = phase_id.astype(jnp.float32) * (two_pi / planes)
    trig_table = jnp.where(col_part[None, :] == 0, jnp.cos(angles), -jnp.sin(angles))
    weights = jnp.where(col_mode == 0, 1.0, 2.0).astype(jnp.float32)
    return (trig_table / planes, (trig_table * weights[None, :]).T)


def body(species, laplacian, binary, dref, stiff_eig, basis, rounds, adjacency, edge_map):
    per_side = basis.shape[0]
    n_nodes = per_side * per_side
    n_span = lax.axis_size("span")
    n_elem = lax.axis_size("elem")
    planes = species.shape[2] * n_span
    n_modes = planes // 2
    per_device = n_modes // n_span
    half_tile = per_device // 2
    own_count = adjacency.shape[0]
    source = mixture_source(species, laplacian, binary, dref)
    assign = jnp.arange(n_modes, dtype=jnp.int32).reshape(n_span, per_device)
    tile_count = 1
    col_mode = jnp.broadcast_to(
        assign.reshape(n_span, 2, 1, half_tile), (n_span, 2, 2, half_tile)
    ).reshape(planes)
    col_part = jnp.broadcast_to(
        jnp.arange(2, dtype=jnp.int32).reshape(1, 1, 2, 1), (n_span, 2, 2, half_tile)
    ).reshape(planes)
    forward, backward = transform_tables(col_mode, col_part, planes)
    source_swapped = jnp.transpose(source, (0, 1, 3, 2))
    coeffs = jnp.einsum(
        "nsez,zr->nser",
        lax.all_to_all(source_swapped, "span", split_axis=2, concat_axis=3, tiled=True),
        forward,
        precision=highest,
    )
    exchanged = lax.all_to_all(coeffs, "span", split_axis=3, concat_axis=2, tiled=True)
    modal_rhs = jnp.transpose(exchanged, (0, 1, 3, 2))
    columns = 2 * per_device
    my_modes = lax.dynamic_slice_in_dim(col_mode, lax.axis_index("span") * columns, columns)
    my_rounds = rounds[my_modes]
    wavenumber = my_modes.astype(jnp.float32) * (8.0 / planes)
    shifts = 1.0 / dref[:, None] + (wavenumber * wavenumber)[None, :]
    eig_sum = (stiff_eig[:, None] + stiff_eig[None, :]).reshape(n_nodes)
    inverse_diag = 1.0 / (shifts[None, :, :, None] + eig_sum[:, None, None, None])
    kron_basis = (basis[:, None, :, None] * basis[None, :, None, :]).reshape(n_nodes, n_nodes)
    flat_index = np.array(edge_lists(per_side)).reshape(-1)
    scatter_table = jnp.asarray(edge_matrix(per_side))
    owners = adjacency // own_count
    offset = (owners - lax.axis_index("elem") + n_elem) % n_elem
    local_id = adjacency % own_count
    flat_adj = adjacency.reshape(-1)
    flat_offset = offset.reshape(-1)
    earlier = flat_adj[None, :] < flat_adj[:, None]
    from_prev = flat_offset == n_elem - 1
    from_next = flat_offset == 1
    rank_prev = jnp.sum((earlier & from_prev[None, :]).astype(jnp.int32), axis=1)
    rank_next = jnp.sum((earlier & from_next[None, :]).astype(jnp.int32), axis=1)
    position = jnp.where(
        from_prev,
        own_count + rank_prev,
        jnp.where(from_next, own_count + MESH_X + rank_next, local_id.reshape(-1)),
    ).reshape(adjacency.shape)
    slot_ids = jnp.arange(MESH_X, dtype=jnp.int32)
    faces_next = jnp.any(offset == 1, axis=1)
    faces_prev = jnp.any(offset == n_elem - 1, axis=1)
    slot_next = jnp.cumsum(faces_next.astype(jnp.int32)) - 1
    slot_prev = jnp.cumsum(faces_prev.astype(jnp.int32)) - 1
    pick_next = (faces_next[:, None] & (slot_next[:, None] == slot_ids[None, :])).astype(
        jnp.float32
    )
    pick_prev = (faces_prev[:, None] & (slot_prev[:, None] == slot_ids[None, :])).astype(
        jnp.float32
    )

    def gather_pool(traces):
        send_up = jnp.einsum("ktsce,ea->ktsca", traces, pick_next, precision=highest)
        send_down = jnp.einsum("ktsce,ea->ktsca", traces, pick_prev, precision=highest)
        from_before = from_behind(send_up, "elem", 1)
        from_after = from_behind(send_down, "elem", -1)
        return jnp.concatenate([traces, from_before, from_after], axis=4)

    def couple(modal_field):
        traces = modal_field[flat_index].reshape((4, per_side) + modal_field.shape[1:])
        across = gather_pool(traces)[edge_map, :, :, :, position][:, :, ::-1]
        return jnp.einsum("jtn,ejtsc->nsce", scatter_table, across, precision=highest)

    tile_modes = assign.reshape(n_span, tile_count, per_device // tile_count)
    sweep_bound = jnp.max(rounds[tile_modes[:, 0].reshape(-1)])
    initial = block_inverse(modal_rhs, kron_basis, inverse_diag)

    def sweep_once(sweep_id, modal_field):
        proposal = block_inverse(
            modal_rhs + coupling * couple(modal_field), kron_basis, inverse_diag
        )
        return jnp.where(sweep_id < my_rounds[:, None], proposal, modal_field)

    solved = lax.fori_loop(1, sweep_bound, sweep_once, initial)
    solution_swapped = jnp.transpose(solved, (0, 1, 3, 2))
    values = jnp.einsum(
        "nser,rz->nsez",
        lax.all_to_all(solution_swapped, "span", split_axis=2, concat_axis=3, tiled=True),
        backward,
        precision=highest,
    )
    returned = lax.all_to_all(values, "span", split_axis=3, concat_axis=2, tiled=True)
    return jnp.transpose(returned, (0, 1, 3, 2))


def solution(mesh):
    n_span, n_elem = mesh.shape["span"], mesh.shape["elem"]

    def chosen_body(species, *rest):
        zl, own = species.shape[2:]
        by_rows = n_span * MESH_X == own and 2 * zl == LANES == own and n_elem > 2
        return (row_body if by_rows else body)(species, *rest)

    return jax.shard_map(
        chosen_body,
        mesh=mesh,
        in_specs=(
            P(None, None, "span", "elem"),
            P(None, None, "span", "elem"),
            P(),
            P(),
            P(),
            P(),
            P(),
            P("elem", None),
            P("elem", None),
        ),
        out_specs=P(None, None, "span", "elem"),
        check_vma=False,
    )
```

```python
import functools

import jax
import jax.numpy as jnp
import numpy as np
from jax import lax
from jax.experimental import pallas as pl
from jax.experimental.pallas import tpu as pltpu
from jax.sharding import PartitionSpec as P

MESH_X = 16
LANES = 128
SIDE = 9
PAIRS = 8
QUAD = 4
NODE_ROWS = 88
TRACE_ROWS = 40
N_SWEEPS = 3
WHOLE = 2
COST_SCALE = 5
FIRST_WHOLE = True
DONE = jax.ShapeDtypeStruct((8, LANES), jnp.float32)
VMEM_BYTES = 48 * 1024 * 1024


coupling = 0.2
highest = lax.Precision.HIGHEST
two_pi = 6.283185307179586
f32 = jnp.float32
bf16 = jnp.bfloat16


def edge_lists(per_side):
    last_node = per_side - 1
    bottom = [i for i in range(per_side)]
    right_edge = [i * per_side + last_node for i in range(per_side)]
    top_edge = [last_node * per_side + last_node - i for i in range(per_side)]
    left_edge = [(last_node - i) * per_side for i in range(per_side)]
    return [bottom, right_edge, top_edge, left_edge]


def row_orders(n_span):
    even = [r ^ (r >> 1 & 1) for r in range(n_span)]
    odd = [r ^ int(2 * r >= n_span) for r in range(n_span)][::-1]
    return [even, odd]


def ring_route(n_span, n_elem, step):
    orders = row_orders(n_span)
    places = [orders[p % 2][r] * n_elem + p for p in range(n_elem) for r in range(n_span)]
    count = len(places)
    return [(places[g], places[(g + step) % count]) for g in range(count)]


def lasting(micros):
    return pl.CostEstimate(flops=int(micros * COST_SCALE * 1150000000), bytes_accessed=0, transcendentals=0)


def split_terms(values):
    top = values.astype(bf16)
    return top, (values - top.astype(f32)).astype(bf16)


def half_swap(first, second):
    low = lax.broadcasted_iota(jnp.int32, first.shape, 1) < LANES // 2
    left = jnp.where(low, first, pltpu.roll(second, LANES // 2, 1))
    right = jnp.where(low, pltpu.roll(first, LANES // 2, 1), second)
    return left, right


def tables_kernel(
    n_span, n_elem, place_ref, adj_ref, map_ref, perm_ref, perm2_ref, base_ref, step_ref, send_ref
):
    own = adj_ref.shape[1]
    span_id, elem_id = place_ref[0], place_ref[1]
    lane = lax.broadcasted_iota(jnp.int32, (own, own), 1).astype(f32)
    sub = lax.broadcasted_iota(jnp.int32, (own, own), 0).astype(f32)
    eye = (lane == sub).astype(f32)
    first_own = (elem_id * own).astype(f32)
    first_next = (lax.rem(elem_id + 1, n_elem) * own).astype(f32)
    first_prev = (lax.rem(elem_id + n_elem - 1, n_elem) * own).astype(f32)

    def column(row):
        return jnp.sum(eye * row, axis=1, keepdims=True)

    def inside(ids, first):
        return (ids >= first) & (ids < first + own)

    adj_row = [adj_ref[j : j + 1, :].astype(f32) for j in range(4)]
    map_row = [map_ref[j : j + 1, :].astype(f32) for j in range(4)]
    meets = [(sub == adj_row[j] - first_own).astype(f32) for j in range(4)]
    near = (eye + meets[0] + meets[1] + meets[2] + meets[3]).astype(bf16)
    prev_row = jnp.zeros((1, own), f32)
    next_row = jnp.zeros((1, own), f32)
    for j in range(4):
        prev_row = prev_row + jnp.where(inside(adj_row[j], first_prev), adj_row[j] + 1.0, 0.0)
        next_row = next_row + jnp.where(inside(adj_row[j], first_next), adj_row[j] + 1.0, 0.0)
    prev_col, next_col = column(prev_row), column(next_row)
    reached = jnp.broadcast_to((prev_col > 0).astype(f32), (own, own))
    row_col = 1.0 - reached
    for _ in range(n_span - 2):
        reached = jnp.minimum(
            jnp.dot(near, reached.astype(bf16), preferred_element_type=f32), 1.0
        )
        row_col = row_col + 1.0 - reached
    row_row = jnp.sum(eye * row_col, axis=0, keepdims=True)
    same = row_col == row_row
    pos_col = jnp.sum((same & (lane < sub)).astype(f32), axis=1, keepdims=True)
    pos_row = jnp.sum((same & (sub < lane)).astype(f32), axis=0, keepdims=True)
    odd = lax.rem(elem_id, 2) == 1
    orders = row_orders(n_span)
    slot_row = jnp.zeros_like(row_row)
    for r in range(n_span):
        slot = jnp.where(odd, orders[1][r], orders[0][r]).astype(f32)
        slot_row = jnp.where(row_row == float(r), slot, slot_row)
    new_row = slot_row * float(MESH_X) + pos_row
    perm = (sub == new_row).astype(f32).astype(bf16)
    perm_ref[:, :own] = perm
    perm_ref[:, own:] = perm
    perm2_ref[:own] = perm
    perm2_ref[own:] = perm

    def rank(col, row):
        return jnp.sum(((col > 0) & (col < row)).astype(f32), axis=0, keepdims=True)

    rank_prev, rank_next = rank(prev_col, prev_row), rank(next_col, next_row)
    spot = lax.broadcasted_iota(jnp.int32, (MESH_X, own), 0).astype(f32)
    here = new_row == spot + (span_id * MESH_X).astype(f32)
    edge_up = jnp.zeros_like(row_row)
    edge_down = jnp.zeros_like(row_row)

    def chosen(values):
        picks = jnp.sum(jnp.where(here, values, 0.0), axis=1, keepdims=True)
        return jnp.broadcast_to(picks, (MESH_X, own))

    per_elem = float(TRACE_ROWS)
    per_row = MESH_X * per_elem
    side_rows = float(MESH_X * SIDE)
    for j in range(4):
        its_pos = jnp.sum(meets[j] * pos_col, axis=0, keepdims=True)
        its_row = jnp.sum(meets[j] * row_col, axis=0, keepdims=True)
        inner = inside(adj_row[j], first_own)
        ahead = inside(adj_row[j], first_next)
        behind = inside(adj_row[j], first_prev)
        up = ahead | (inner & (its_row == row_row + 1.0))
        down = behind | (inner & (its_row == row_row - 1.0))
        its_pos = jnp.where(ahead, rank_next, jnp.where(behind, rank_prev, its_pos))
        base = jnp.where(
            up,
            per_row + its_pos,
            jnp.where(down, per_row + side_rows + its_pos, its_pos * per_elem + map_row[j]),
        )
        edge_up = jnp.where(up, float(j), edge_up)
        edge_down = jnp.where(down, float(j), edge_down)
        rows = slice(j * MESH_X, (j + 1) * MESH_X)
        base_ref[rows] = chosen(base)
        step_ref[rows] = chosen(jnp.where(up | down, float(MESH_X), 4.0))
    send_ref[:MESH_X] = chosen(edge_up) + spot * per_elem
    send_ref[MESH_X:] = chosen(edge_down) + spot * per_elem


def mesh_tables(adjacency, edge_map, n_span, n_elem):
    own = adjacency.shape[0]
    place = jnp.stack([lax.axis_index("span"), lax.axis_index("elem")]).astype(jnp.int32)
    return pl.pallas_call(
        functools.partial(tables_kernel, n_span, n_elem),
        out_shape=(
            jax.ShapeDtypeStruct((own, 2 * own), bf16),
            jax.ShapeDtypeStruct((2 * own, own), bf16),
            jax.ShapeDtypeStruct((4 * MESH_X, own), f32),
            jax.ShapeDtypeStruct((4 * MESH_X, own), f32),
            jax.ShapeDtypeStruct((2 * MESH_X, own), f32),
        ),
        in_specs=[
            pl.BlockSpec(memory_space=pltpu.SMEM),
            pl.BlockSpec(memory_space=pltpu.VMEM),
            pl.BlockSpec(memory_space=pltpu.VMEM),
        ],
        out_specs=[pl.BlockSpec(memory_space=pltpu.VMEM)] * 5,
        cost_estimate=lasting(3),
        name="mesh_tables",
    )(place, adjacency.T, edge_map.T)


def link_kernel(
    base_ref, step_ref, send_ref, from_ref, turn_ref, skip_ref, out_ref, move_ref, link_ref, pick_ref
):
    def spread(table, values):
        return jnp.dot(table[...], values[...], precision=highest, preferred_element_type=f32)

    def fill(ref, wanted):
        for c in range(0, ref.shape[1], LANES):
            width = min(LANES, ref.shape[1] - c)
            lane = lax.broadcasted_iota(jnp.int32, wanted.shape, 1).astype(f32) + float(c)
            ref[:, c : c + width] = (wanted == lane).astype(f32).astype(bf16)[:, :width]

    fill(link_ref, spread(from_ref, base_ref) + turn_ref[...] * spread(from_ref, step_ref) + skip_ref[...])
    fill(pick_ref, spread(out_ref, send_ref) + move_ref[...])


def link_matrices(base, step, send, own):
    rows = MESH_X * TRACE_ROWS
    from_edge = np.zeros((rows, 4 * MESH_X), np.float32)
    turn = np.zeros((rows, own), np.float32)
    skip = np.full((rows, own), -1.0, np.float32)
    for i in range(MESH_X):
        for t in range(SIDE):
            for j in range(4):
                row = i * TRACE_ROWS + t * 4 + j
                from_edge[row, j * MESH_X + i] = 1.0
                turn[row] = SIDE - 1 - t
                skip[row] = 0.0
    side_rows = SIDE * MESH_X
    out_edge = np.zeros((2 * side_rows, 2 * MESH_X), np.float32)
    move = np.zeros((2 * side_rows, own), np.float32)
    for way in range(2):
        for t in range(SIDE):
            for i in range(MESH_X):
                row = way * side_rows + t * MESH_X + i
                out_edge[row, way * MESH_X + i] = 1.0
                move[row] = 4 * t
    vmem = pl.BlockSpec(memory_space=pltpu.VMEM)
    return pl.pallas_call(
        link_kernel,
        out_shape=(
            jax.ShapeDtypeStruct((rows, rows + 2 * side_rows), bf16),
            jax.ShapeDtypeStruct((2 * side_rows, rows), bf16),
        ),
        in_specs=[vmem] * 8,
        out_specs=[vmem] * 2,
        cost_estimate=lasting(4),
        name="link_matrices",
    )(base, step, send, from_edge, turn, skip, out_edge, move)


def source_kernel(s, has_tail, binary_ref, dref_ref, species_ref, lap_ref, perm_ref, *refs):
    out_ref, done_ref = refs[-2:]
    done_ref[...] = jnp.zeros_like(done_ref)
    per_step, n_species, zl, own = species_ref.shape
    n_span = out_ref.shape[0]
    perm = perm_ref[...]

    def inverse(value):
        return 1.0 / jnp.full((8, own), value, f32)

    def wide(row):
        return jnp.broadcast_to(row[:1], (zl, own))

    inv = [wide(inverse(binary_ref[s, j])) for j in range(n_species + 1)]
    inv_dref = wide(inverse(dref_ref[s]))

    def source(n):
        parts = [species_ref[n, j] for j in range(n_species)]
        bath = 1.0 - sum(parts[1:], parts[0])
        resistance = bath * inv[n_species]
        for j in range(n_species):
            if j != s:
                resistance = resistance + parts[j] * inv[j]
        mixture = (1.0 - parts[s]) / resistance
        return (parts[s] + (mixture - dref_ref[s]) * lap_ref[n, 0]) * inv_dref

    def turned(first, second):
        top, rest = split_terms(jnp.concatenate([first, second], axis=0))
        both = jnp.concatenate([top, rest], axis=1)
        return lax.dot_general(
            perm, both, (((1,), (1,)), ((), ())), preferred_element_type=f32
        )

    def blocks():
        pairs = per_step // 2
        for k in range(pairs):
            tile = turned(source(2 * k), source(2 * k + 1))
            for q in range(n_span):
                out_ref[q, pl.ds(k, MESH_X, stride=pairs), :] = tile[
                    q * MESH_X : (q + 1) * MESH_X
                ]

    def tail():
        value = source(0)
        tile = turned(value, value)
        half = MESH_X // 2
        low = lax.broadcasted_iota(jnp.int32, (half, 2 * zl), 1) < zl
        for q in range(n_span):
            block = tile[q * MESH_X : (q + 1) * MESH_X]
            out_ref[q, :half, :] = jnp.where(low, block[:half], block[half:])

    by_step(has_tail, blocks, tail)


def by_step(has_tail, blocks, tail):
    if not has_tail:
        blocks()
        return
    last_step = pl.num_programs(0) - 1
    pl.when(pl.program_id(0) < last_step)(blocks)
    pl.when(pl.program_id(0) == last_step)(tail)


def part_blocks(n_nodes, part):
    groups = n_nodes // (2 * PAIRS)
    rows = MESH_X * PAIRS
    first = groups // 2
    if part == 0:
        return 0, first, first * rows
    if part == WHOLE:
        return 0, groups + 1, groups * rows + MESH_X // 2
    return first, groups - first + 1, (groups - first) * rows + MESH_X // 2


def packed_source(s, part, species, laplacian, binary, dref, perm, n_span, after):
    n_nodes, n_species, zl, own = species.shape
    step = 2 * PAIRS
    begin, steps, rows = part_blocks(n_nodes, part)
    return pl.pallas_call(
        functools.partial(source_kernel, s, part > 0),
        grid=(steps,),
        out_shape=(jax.ShapeDtypeStruct((n_span, rows, 2 * zl), f32), DONE),
        in_specs=[
            pl.BlockSpec(memory_space=pltpu.SMEM),
            pl.BlockSpec(memory_space=pltpu.SMEM),
            pl.BlockSpec((step, n_species, zl, own), lambda g: (g + begin, 0, 0, 0)),
            pl.BlockSpec((step, 1, zl, own), lambda g: (g + begin, s, 0, 0)),
            pl.BlockSpec((own, 2 * own), lambda g: (0, 0)),
        ]
        + [pl.BlockSpec(memory_space=pl.ANY)] * len(after),
        out_specs=(
            pl.BlockSpec((n_span, MESH_X * PAIRS, 2 * zl), lambda g: (0, g, 0)),
            pl.BlockSpec(DONE.shape, lambda g: (0, 0)),
        ),
        compiler_params=pltpu.CompilerParams(vmem_limit_bytes=VMEM_BYTES),
        cost_estimate=lasting(4),
        name="packed_source",
    )(binary, dref, species, laplacian, perm, *after)


def unpack_kernel(has_tail, recv_ref, perm_ref, *refs):
    out_ref = refs[-1]
    n_span = recv_ref.shape[0]
    per_step, _, zl, _ = out_ref.shape
    perm = perm_ref[...]

    def turned(tile):
        top, rest = split_terms(tile)
        both = jnp.concatenate([top, rest], axis=0)
        return lax.dot_general(
            both, perm, (((0,), (0,)), ((), ())), preferred_element_type=f32
        )

    def blocks():
        pairs = per_step // 2
        for k in range(pairs):
            tile = jnp.concatenate(
                [recv_ref[q, pl.ds(k, MESH_X, stride=pairs), :] for q in range(n_span)], axis=0
            )
            result = turned(tile)
            out_ref[2 * k, 0] = result[:zl]
            out_ref[2 * k + 1, 0] = result[zl:]

    def tail():
        half = MESH_X // 2
        sides = []
        for q in range(n_span):
            block = recv_ref[q, :half, :]
            sides += [block, pltpu.roll(block, zl, 1)]
        out_ref[0, 0] = turned(jnp.concatenate(sides, axis=0))[:zl]

    by_step(has_tail, blocks, tail)


def unpacked(s, part, recv, perm2, shape, before):
    n_nodes, n_species, zl, own = shape
    n_span, _, width = recv.shape
    step = 2 * PAIRS
    begin, steps, _ = part_blocks(n_nodes, part)
    operands = [recv, perm2] + ([] if before is None else [before])
    return pl.pallas_call(
        functools.partial(unpack_kernel, part > 0),
        grid=(steps,),
        out_shape=jax.ShapeDtypeStruct(shape, f32),
        in_specs=[
            pl.BlockSpec((n_span, MESH_X * PAIRS, width), lambda g: (0, g, 0)),
            pl.BlockSpec((2 * own, own), lambda g: (0, 0)),
        ]
        + ([] if before is None else [pl.BlockSpec(memory_space=pl.ANY)]),
        out_specs=pl.BlockSpec((step, 1, zl, own), lambda g: (g + begin, s, 0, 0)),
        input_output_aliases={} if before is None else {2: 0},
        compiler_params=pltpu.CompilerParams(vmem_limit_bytes=VMEM_BYTES),
        cost_estimate=lasting(0.1),
        name="unpacked",
    )(*operands)


def left_product(matrix, values):
    rows = matrix.shape[0] // 2
    top, rest = split_terms(values)
    both = jnp.dot(matrix, top, preferred_element_type=f32)
    return both[:rows] + both[rows:] + jnp.dot(matrix[:rows], rest, preferred_element_type=f32)


def right_product(values, top_ref, rest_ref):
    rows = values.shape[0]
    top, rest = split_terms(values)
    both = jnp.dot(jnp.concatenate([top, rest], axis=0), top_ref[...], preferred_element_type=f32)
    return both[:rows] + both[rows:] + jnp.dot(top, rest_ref[...], preferred_element_type=f32)


def chunk_rows(index, size):
    return pl.ds(pl.multiple_of(index * size, size), size)


def send_traces(trace_ref, pick_ref, up_ref, down_ref):
    top, rest = split_terms(trace_ref[...])
    out = jnp.dot(pick_ref[...], top, preferred_element_type=f32)
    out = out + jnp.dot(pick_ref[...], rest, preferred_element_type=f32)
    half = up_ref.shape[0]
    up_ref[...] = out[:half]
    down_ref[...] = out[half:]


def sent_block(early_ref, late_ref, g, before, i):
    if g < before:
        return early_ref, chunk_rows(g * MESH_X + i, PAIRS)
    return late_ref, chunk_rows((g - before) * MESH_X + i, PAIRS)


def sent_parts(refs):
    if len(refs) == 2:
        return refs
    rows = refs[0].shape[1]
    first = (rows // (MESH_X * PAIRS)) // 2 * MESH_X * PAIRS
    return refs[0].at[:, pl.ds(0, first), :], refs[0].at[:, pl.ds(first, rows - first), :]


def start_kernel(*refs):
    *sent, top_ref, rest_ref, diag_ref, eigen_ref, edge_ref, pick_ref = refs[:-6]
    w_ref, trace_ref, up_ref, down_ref, x, ends = refs[-6:]
    early_ref, late_ref = sent_parts(sent)
    n_span, rows, width = late_ref.shape
    half = MESH_X // 2
    tail = rows - half
    before = early_ref.shape[1] // (MESH_X * PAIRS)
    groups = before + tail // (MESH_X * PAIRS)
    first = lax.broadcasted_iota(jnp.int32, (8, x.shape[1]), 0) == 0
    for tile in range(n_span // 2):
        lanes = slice(tile * LANES, (tile + 1) * LANES)
        left, right = half_swap(late_ref[2 * tile, tail:, :], late_ref[2 * tile + 1, tail:, :])
        ends[:half, lanes] = left
        ends[half:, lanes] = right

    def quad(c, carry):
        for ii in range(QUAD):
            i = c * QUAD + ii
            for tile in range(n_span // 2):
                lanes = slice(tile * LANES, (tile + 1) * LANES)
                for g in range(groups):
                    ref, block = sent_block(early_ref, late_ref, g, before, i)
                    left, right = half_swap(ref[2 * tile, block, :], ref[2 * tile + 1, block, :])
                    base = ii * NODE_ROWS + g * PAIRS
                    x[base : base + PAIRS, lanes] = left
                    base += groups * PAIRS
                    x[base : base + PAIRS, lanes] = right
            base = ii * NODE_ROWS + 2 * groups * PAIRS
            x[base : base + 8, :] = jnp.where(first, ends[pl.ds(i, 1), :], 0.0)
        y = right_product(x[...], top_ref, rest_ref)
        for p in range(QUAD // 2):
            part = slice(p * 2 * NODE_ROWS, (p + 1) * 2 * NODE_ROWS)
            w = left_product(eigen_ref[...], y[part])
            pair = c * (QUAD // 2) + p
            w_ref[chunk_rows(pair, 2 * NODE_ROWS), :] = w
            trace_ref[chunk_rows(pair, 2 * TRACE_ROWS), :] = left_product(
                edge_ref[...], w * diag_ref[...]
            )
        return carry

    lax.fori_loop(0, MESH_X // QUAD, quad, 0, unroll=True)
    send_traces(trace_ref, pick_ref, up_ref, down_ref)


def fill_sources(trace_ref, above_ref, below_ref, top, rest):
    row = 0
    for ref in (trace_ref, above_ref, below_ref):
        block = slice(row, row + ref.shape[0])
        top[block], rest[block] = split_terms(ref[...])
        row += ref.shape[0]


def met_traces(link_ref, top, rest, met):
    met[...] = jnp.dot(link_ref[...], top[...], preferred_element_type=f32) + jnp.dot(
        link_ref[...], rest[...], preferred_element_type=f32
    )


def sweep_kernel(sweep_id, rounds_ref, diag_ref, link_ref, pick_ref, inner_ref, edge_ref, *refs):
    begun = sweep_id > 1
    start_ref, trace_ref, above_ref, below_ref = refs[:4]
    held_ref = refs[4] if begun else None
    kept_ref, tout_ref, up_ref, down_ref, top, rest, gathered = refs[5 if begun else 4 :]
    fill_sources(trace_ref, above_ref, below_ref, top, rest)
    met_traces(link_ref, top, rest, gathered)
    going = rounds_ref[...] > sweep_id

    def quad(c, carry):
        rows = chunk_rows(c, QUAD * TRACE_ROWS)
        met = gathered[rows, :]
        kept_ref[rows, :] = jnp.where(going, met, held_ref[rows, :] if begun else 0.0)
        for p in range(QUAD // 2):
            part = met[p * 2 * TRACE_ROWS : (p + 1) * 2 * TRACE_ROWS]
            field = left_product(inner_ref[...], part) * diag_ref[...]
            rows = chunk_rows(c * (QUAD // 2) + p, 2 * TRACE_ROWS)
            tout_ref[rows, :] = start_ref[rows, :] + left_product(edge_ref[...], field)
        return carry

    lax.fori_loop(0, MESH_X // QUAD, quad, 0, unroll=True)
    send_traces(tout_ref, pick_ref, up_ref, down_ref)


def finish_kernel(
    sweep_id, rounds_ref, diag_ref, link_ref, inner_ref, nodal_ref, trace_ref, above_ref,
    below_ref, held_ref, w_ref, top_ref, rest_ref, *refs,
):
    *sent, top, rest, gathered, modal, ends = refs
    early_ref, late_ref = sent_parts(sent)
    n_span, rows, width = late_ref.shape
    half = MESH_X // 2
    tail = rows - half
    before = early_ref.shape[1] // (MESH_X * PAIRS)
    groups = before + tail // (MESH_X * PAIRS)
    fill_sources(trace_ref, above_ref, below_ref, top, rest)
    met_traces(link_ref, top, rest, gathered)
    going = rounds_ref[...] > sweep_id

    def quad(c, carry):
        rows = chunk_rows(c, QUAD * TRACE_ROWS)
        kept = jnp.where(going, gathered[rows, :], held_ref[rows, :])
        for p in range(QUAD // 2):
            part = kept[p * 2 * TRACE_ROWS : (p + 1) * 2 * TRACE_ROWS]
            rows = chunk_rows(c * (QUAD // 2) + p, 2 * NODE_ROWS)
            field = (w_ref[rows, :] + left_product(inner_ref[...], part)) * diag_ref[...]
            modal[p * 2 * NODE_ROWS : (p + 1) * 2 * NODE_ROWS] = left_product(
                nodal_ref[...], field
            )
        z = right_product(modal[...], top_ref, rest_ref)
        for ii in range(QUAD):
            i = c * QUAD + ii
            for tile in range(n_span // 2):
                lanes = slice(tile * LANES, (tile + 1) * LANES)
                for g in range(groups):
                    base = ii * NODE_ROWS + g * PAIRS
                    later = base + groups * PAIRS
                    left, right = half_swap(
                        z[base : base + PAIRS, lanes], z[later : later + PAIRS, lanes]
                    )
                    ref, block = sent_block(early_ref, late_ref, g, before, i)
                    ref[2 * tile, block, :] = left
                    ref[2 * tile + 1, block, :] = right
            base = ii * NODE_ROWS + 2 * groups * PAIRS
            ends[pl.ds(i, 1), :] = z[base : base + 1]
        return carry

    lax.fori_loop(0, MESH_X // QUAD, quad, 0, unroll=True)
    for tile in range(n_span // 2):
        lanes = slice(tile * LANES, (tile + 1) * LANES)
        left, right = half_swap(ends[:half, lanes], ends[half:, lanes])
        late_ref[2 * tile, tail:, :] = left
        late_ref[2 * tile + 1, tail:, :] = right


def vmem_call(kernel, name, out_shape, scratch, micros, operands, after):
    count, extra = len(operands), len(after)

    def ordered(*refs):
        last = count + extra + len(out_shape)
        refs[last][...] = jnp.zeros_like(refs[last])
        kernel(*refs[:count], *refs[count + extra : last], *refs[last + 1 :])

    vmem = pl.BlockSpec(memory_space=pltpu.VMEM)
    return pl.pallas_call(
        ordered,
        out_shape=tuple(out_shape) + (DONE,),
        in_specs=[vmem] * count + [pl.BlockSpec(memory_space=pl.ANY)] * extra,
        out_specs=tuple([vmem] * (len(out_shape) + 1)),
        scratch_shapes=scratch,
        compiler_params=pltpu.CompilerParams(vmem_limit_bytes=VMEM_BYTES),
        cost_estimate=lasting(micros),
        name=name,
    )(*operands, *after)


def stacked_terms(values):
    return jnp.concatenate(outer_split(values), axis=0)


def twice(matrix):
    zero = jnp.zeros_like(matrix)
    return jnp.concatenate(
        [jnp.concatenate([matrix, zero], axis=1), jnp.concatenate([zero, matrix], axis=1)], axis=0
    )


def nodal_matrices(basis):
    m = basis.shape[0]
    n_nodes = m * m
    kron_basis = (basis[:, None, :, None] * basis[None, :, None, :]).reshape(n_nodes, n_nodes)
    order = np.concatenate(
        [np.arange(0, n_nodes - 1, 2), np.arange(1, n_nodes - 1, 2), [n_nodes - 1]]
    )
    edges = np.array(edge_lists(m)).T.reshape(-1)
    full, edge = NODE_ROWS - n_nodes, TRACE_ROWS - edges.size
    nodal = jnp.pad(kron_basis[order], ((0, full), (0, full)))
    traces = jnp.pad(kron_basis[edges], ((0, edge), (0, full)))
    return [
        stacked_terms(twice(matrix)) for matrix in (nodal.T, traces, coupling * traces.T, nodal)
    ]


def solve_stages(n_sweeps, arrived, sent_shapes, rounds_row, diag, link, pick, matrices, forward, backward):
    eigen, edge, inner, nodal = matrices
    planes = forward[0].shape[0]
    w_shape = jax.ShapeDtypeStruct((MESH_X * NODE_ROWS, planes), f32)
    trace = jax.ShapeDtypeStruct((MESH_X * TRACE_ROWS, planes), f32)
    side = jax.ShapeDtypeStruct((MESH_X * SIDE, planes), f32)
    sources = pltpu.VMEM((link.shape[1], planes), bf16)
    gathered = pltpu.VMEM(trace.shape, f32)
    quad = pltpu.VMEM((QUAD * NODE_ROWS, planes), f32)
    ends = pltpu.VMEM((MESH_X, planes), f32)
    axes = ("span", "elem")
    n_span, n_elem = lax.axis_size("span"), lax.axis_size("elem")

    def exchange(up, down):
        below = lax.ppermute(up, axes, ring_route(n_span, n_elem, 1))
        above = lax.ppermute(down, axes, ring_route(n_span, n_elem, -1))
        return above, below

    after = yield None
    w, start, up, down, mark = vmem_call(
        start_kernel,
        "start_solve",
        [w_shape, trace, side, side],
        [quad, ends],
        16,
        arrived + [forward[0], forward[1], diag, eigen, edge, pick],
        after,
    )
    traces, held = start, []
    for sweep_id in range(1, n_sweeps):
        above, below = exchange(up, down)
        after = yield mark, None
        kept, traces, up, down, mark = vmem_call(
            functools.partial(sweep_kernel, sweep_id),
            "sweep_solve",
            [trace, trace, side, side],
            [sources, sources, gathered],
            10,
            [rounds_row, diag, link, pick, inner, edge, start, traces, above, below] + held,
            after,
        )
        held = [kept]
    above, below = exchange(up, down)
    after = yield mark, None
    *result, mark = vmem_call(
        functools.partial(finish_kernel, n_sweeps),
        "finish_solve",
        [jax.ShapeDtypeStruct(shape, f32) for shape in sent_shapes],
        [sources, sources, gathered, quad, ends],
        17,
        [rounds_row, diag, link, inner, nodal, traces, above, below, kept, w]
        + [backward[0], backward[1]],
        after,
    )
    yield mark, result


def transform_terms(planes):
    modes = np.tile(np.arange(planes // 2), 2)
    angles = np.arange(planes)[:, None] * modes[None, :] % planes * (2 * np.pi / planes)
    real = np.arange(planes)[None, :] < planes // 2
    table = np.where(real, np.cos(angles), -np.sin(angles))
    weights = np.where(modes == 0, 1.0, 2.0)

    def terms(values):
        top = values.astype(bf16)
        return top, (values - top.astype(np.float64)).astype(bf16)

    return terms(table / planes), terms((table * weights[None, :]).T)


def outer_split(values):
    top = lax.reduce_precision(values, exponent_bits=8, mantissa_bits=7)
    return top.astype(bf16), (values - top).astype(bf16)


def row_body(species, laplacian, binary, dref, stiff_eig, basis, rounds, adjacency, edge_map):
    n_nodes, n_species, zl, own = species.shape
    n_span = lax.axis_size("span")
    n_elem = lax.axis_size("elem")
    planes = zl * n_span
    n_modes = planes // 2
    perm, perm2, base, step, send = mesh_tables(adjacency, edge_map, n_span, n_elem)

    def across(sent):
        return lax.all_to_all(sent, "span", split_axis=0, concat_axis=0, tiled=True)

    link, pick = link_matrices(base, step, send, own)
    matrices = nodal_matrices(basis)
    forward, backward = transform_terms(planes)
    col_mode = jnp.tile(jnp.arange(n_modes, dtype=jnp.int32), 2)
    wavenumber = col_mode.astype(f32) * (8.0 / planes)
    shifts = 1.0 / dref[:, None] + (wavenumber * wavenumber)[None, :]
    eig_sum = (stiff_eig[:, None] + stiff_eig[None, :]).reshape(n_nodes)
    eig_sum = jnp.tile(jnp.pad(eig_sum, (0, NODE_ROWS - n_nodes)), 2)
    diag = 1.0 / (shifts[:, None, :] + eig_sum[None, :, None])
    rounds_row = jnp.tile(rounds, 2).reshape(1, planes)

    in_parts = [(WHOLE,) if FIRST_WHOLE and s == 0 else (0, 1) for s in range(n_species)]
    out_parts = [(WHOLE,) if s + 1 == n_species else (0, 1) for s in range(n_species)]
    steps, count = [], 0
    arrived_by, slots, back_slots = [], [], []
    for parts, slot_list in ((in_parts, slots), (out_parts, back_slots)):
        for group in parts:
            slot_list.append(range(count, count + len(group)))
            count += len(group)
    in_count = slots[-1][-1] + 1
    for s in range(n_species):
        for slot, part in zip(slots[s], in_parts[s]):
            early = min(slot - 2, slots[0][-1] - 1) if slot < 3 else slots[0][-1] - 1
            steps.append((early if slot else -2, 2, slot, s, ("pack", part)))
        first = slots[s][-1]
        for stage in range(N_SWEEPS + 1):
            steps.append((first + stage, 0, s, s, ("solve", stage)))
        for slot, part in zip(back_slots[s], out_parts[s]):
            steps.append((slot, 1, slot, s, ("unpack", part)))
    moved, waiting, solves, mark = [], [], [], []
    updated, last = None, -2
    for arrival, _, _, s, (kind, index) in sorted(steps):
        if arrival > last and waiting:
            moved.append(across(released(waiting.pop(0), mark + moved[-1:])))
        last = arrival
        after = mark + (moved[arrival : arrival + 1] if arrival >= 0 else [])
        if kind == "pack":
            sent, done = packed_source(
                s, index, species, laplacian, binary, dref, perm, n_span, after
            )
            waiting.append(sent)
            mark = [done]
        elif kind == "solve":
            if index == 0:
                shapes = [
                    (n_span, part_blocks(n_nodes, part)[2], 2 * zl) for part in out_parts[s]
                ]
                solves.append(
                    solve_stages(
                        N_SWEEPS, [moved[slot] for slot in slots[s]], shapes, rounds_row, diag[s],
                        link, pick, matrices, forward, backward,
                    )
                )
                next(solves[s])
            done, result = solves[s].send(after)
            mark = [done]
            if result is not None:
                waiting += result
        else:
            updated = unpacked(s, index, moved[arrival], perm2, species.shape, updated)
    return updated


def released(block, after):
    def kernel(*refs):
        pass

    anywhere = pl.BlockSpec(memory_space=pl.ANY)
    return pl.pallas_call(
        kernel,
        out_shape=jax.ShapeDtypeStruct(block.shape, block.dtype),
        in_specs=[anywhere] * (1 + len(after)),
        out_specs=anywhere,
        input_output_aliases={0: 0},
        name="released",
    )(block, *after)


def from_behind(block, axis, distance):
    devices = range(lax.axis_size(axis))
    route = [((i - distance) % len(devices), i) for i in devices]
    return lax.ppermute(block, axis, route)


def edge_matrix(per_side):
    edge_table = np.zeros((4, per_side, per_side * per_side), np.float32)
    for edge_id, node_list in enumerate(edge_lists(per_side)):
        for i, node_id in enumerate(node_list):
            edge_table[edge_id, i, node_id] = 1.0
    return edge_table


def mixture_source(species, laplacian, binary, dref):
    n_species = species.shape[1]
    bath_share = 1.0 - jnp.sum(species, axis=1)
    source_parts = []
    for s in range(n_species):
        resistance = bath_share / binary[s, n_species]
        for j in range(n_species):
            if j != s:
                resistance = resistance + species[:, j] / binary[s, j]
        mixture = (1.0 - species[:, s]) / resistance
        source_parts.append((species[:, s] + (mixture - dref[s]) * laplacian[:, s]) / dref[s])
    return jnp.stack(source_parts, axis=1)


def block_inverse(values, kron_basis, inverse_diag):
    n_nodes = values.shape[0]
    inner_part = (
        jnp.dot(kron_basis.T, values.reshape(n_nodes, -1), precision=highest).reshape(values.shape)
        * inverse_diag
    )
    return jnp.dot(kron_basis, inner_part.reshape(n_nodes, -1), precision=highest).reshape(
        values.shape
    )


def transform_tables(col_mode, col_part, planes):
    plane_ids = jnp.arange(planes, dtype=jnp.int32)
    phase_id = plane_ids[:, None] * col_mode[None, :] % planes
    angles = phase_id.astype(jnp.float32) * (two_pi / planes)
    trig_table = jnp.where(col_part[None, :] == 0, jnp.cos(angles), -jnp.sin(angles))
    weights = jnp.where(col_mode == 0, 1.0, 2.0).astype(jnp.float32)
    return (trig_table / planes, (trig_table * weights[None, :]).T)


def body(species, laplacian, binary, dref, stiff_eig, basis, rounds, adjacency, edge_map):
    per_side = basis.shape[0]
    n_nodes = per_side * per_side
    n_span = lax.axis_size("span")
    n_elem = lax.axis_size("elem")
    planes = species.shape[2] * n_span
    n_modes = planes // 2
    per_device = n_modes // n_span
    half_tile = per_device // 2
    own_count = adjacency.shape[0]
    source = mixture_source(species, laplacian, binary, dref)
    assign = jnp.arange(n_modes, dtype=jnp.int32).reshape(n_span, per_device)
    tile_count = 1
    col_mode = jnp.broadcast_to(
        assign.reshape(n_span, 2, 1, half_tile), (n_span, 2, 2, half_tile)
    ).reshape(planes)
    col_part = jnp.broadcast_to(
        jnp.arange(2, dtype=jnp.int32).reshape(1, 1, 2, 1), (n_span, 2, 2, half_tile)
    ).reshape(planes)
    forward, backward = transform_tables(col_mode, col_part, planes)
    source_swapped = jnp.transpose(source, (0, 1, 3, 2))
    coeffs = jnp.einsum(
        "nsez,zr->nser",
        lax.all_to_all(source_swapped, "span", split_axis=2, concat_axis=3, tiled=True),
        forward,
        precision=highest,
    )
    exchanged = lax.all_to_all(coeffs, "span", split_axis=3, concat_axis=2, tiled=True)
    modal_rhs = jnp.transpose(exchanged, (0, 1, 3, 2))
    columns = 2 * per_device
    my_modes = lax.dynamic_slice_in_dim(col_mode, lax.axis_index("span") * columns, columns)
    my_rounds = rounds[my_modes]
    wavenumber = my_modes.astype(jnp.float32) * (8.0 / planes)
    shifts = 1.0 / dref[:, None] + (wavenumber * wavenumber)[None, :]
    eig_sum = (stiff_eig[:, None] + stiff_eig[None, :]).reshape(n_nodes)
    inverse_diag = 1.0 / (shifts[None, :, :, None] + eig_sum[:, None, None, None])
    kron_basis = (basis[:, None, :, None] * basis[None, :, None, :]).reshape(n_nodes, n_nodes)
    flat_index = np.array(edge_lists(per_side)).reshape(-1)
    scatter_table = jnp.asarray(edge_matrix(per_side))
    owners = adjacency // own_count
    offset = (owners - lax.axis_index("elem") + n_elem) % n_elem
    local_id = adjacency % own_count
    flat_adj = adjacency.reshape(-1)
    flat_offset = offset.reshape(-1)
    earlier = flat_adj[None, :] < flat_adj[:, None]
    from_prev = flat_offset == n_elem - 1
    from_next = flat_offset == 1
    rank_prev = jnp.sum((earlier & from_prev[None, :]).astype(jnp.int32), axis=1)
    rank_next = jnp.sum((earlier & from_next[None, :]).astype(jnp.int32), axis=1)
    position = jnp.where(
        from_prev,
        own_count + rank_prev,
        jnp.where(from_next, own_count + MESH_X + rank_next, local_id.reshape(-1)),
    ).reshape(adjacency.shape)
    slot_ids = jnp.arange(MESH_X, dtype=jnp.int32)
    faces_next = jnp.any(offset == 1, axis=1)
    faces_prev = jnp.any(offset == n_elem - 1, axis=1)
    slot_next = jnp.cumsum(faces_next.astype(jnp.int32)) - 1
    slot_prev = jnp.cumsum(faces_prev.astype(jnp.int32)) - 1
    pick_next = (faces_next[:, None] & (slot_next[:, None] == slot_ids[None, :])).astype(
        jnp.float32
    )
    pick_prev = (faces_prev[:, None] & (slot_prev[:, None] == slot_ids[None, :])).astype(
        jnp.float32
    )

    def gather_pool(traces):
        send_up = jnp.einsum("ktsce,ea->ktsca", traces, pick_next, precision=highest)
        send_down = jnp.einsum("ktsce,ea->ktsca", traces, pick_prev, precision=highest)
        from_before = from_behind(send_up, "elem", 1)
        from_after = from_behind(send_down, "elem", -1)
        return jnp.concatenate([traces, from_before, from_after], axis=4)

    def couple(modal_field):
        traces = modal_field[flat_index].reshape((4, per_side) + modal_field.shape[1:])
        across = gather_pool(traces)[edge_map, :, :, :, position][:, :, ::-1]
        return jnp.einsum("jtn,ejtsc->nsce", scatter_table, across, precision=highest)

    tile_modes = assign.reshape(n_span, tile_count, per_device // tile_count)
    sweep_bound = jnp.max(rounds[tile_modes[:, 0].reshape(-1)])
    initial = block_inverse(modal_rhs, kron_basis, inverse_diag)

    def sweep_once(sweep_id, modal_field):
        proposal = block_inverse(
            modal_rhs + coupling * couple(modal_field), kron_basis, inverse_diag
        )
        return jnp.where(sweep_id < my_rounds[:, None], proposal, modal_field)

    solved = lax.fori_loop(1, sweep_bound, sweep_once, initial)
    solution_swapped = jnp.transpose(solved, (0, 1, 3, 2))
    values = jnp.einsum(
        "nser,rz->nsez",
        lax.all_to_all(solution_swapped, "span", split_axis=2, concat_axis=3, tiled=True),
        backward,
        precision=highest,
    )
    returned = lax.all_to_all(values, "span", split_axis=3, concat_axis=2, tiled=True)
    return jnp.transpose(returned, (0, 1, 3, 2))


def solution(mesh):
    n_span, n_elem = mesh.shape["span"], mesh.shape["elem"]

    def chosen_body(species, *rest):
        zl, own = species.shape[2:]
        by_rows = n_span * MESH_X == own and 2 * zl == LANES == own and n_elem > 2
        by_rows = by_rows and species.shape[0] == SIDE * SIDE
        return (row_body if by_rows else body)(species, *rest)

    return jax.shard_map(
        chosen_body,
        mesh=mesh,
        in_specs=(
            P(None, None, "span", "elem"),
            P(None, None, "span", "elem"),
            P(),
            P(),
            P(),
            P(),
            P(),
            P("elem", None),
            P("elem", None),
        ),
        out_specs=P(None, None, "span", "elem"),
        check_vma=False,
    )
```

```python
import functools

import jax
import jax.numpy as jnp
import numpy as np
from jax import lax
from jax.experimental import pallas as pl
from jax.experimental.pallas import tpu as pltpu
from jax.sharding import PartitionSpec as P

MESH_X = 16
LANES = 128
SIDE = 9
PAIRS = 8
QUAD = 4
NODE_ROWS = 88
TRACE_ROWS = 40
N_SWEEPS = 3
WHOLE = 2
COST_SCALE = 5
FIRST_WHOLE = True
DONE = jax.ShapeDtypeStruct((8, LANES), jnp.float32)
VMEM_BYTES = 60 * 1024 * 1024
UNPACK_BYTES = 48 * 1024 * 1024


coupling = 0.2
highest = lax.Precision.HIGHEST
two_pi = 6.283185307179586
f32 = jnp.float32
bf16 = jnp.bfloat16


def edge_lists(per_side):
    last_node = per_side - 1
    bottom = [i for i in range(per_side)]
    right_edge = [i * per_side + last_node for i in range(per_side)]
    top_edge = [last_node * per_side + last_node - i for i in range(per_side)]
    left_edge = [(last_node - i) * per_side for i in range(per_side)]
    return [bottom, right_edge, top_edge, left_edge]


def row_orders(n_span):
    even = [r ^ (r >> 1 & 1) for r in range(n_span)]
    odd = [r ^ int(2 * r >= n_span) for r in range(n_span)][::-1]
    return [even, odd]


def ring_route(n_span, n_elem, step):
    orders = row_orders(n_span)
    places = [orders[p % 2][r] * n_elem + p for p in range(n_elem) for r in range(n_span)]
    count = len(places)
    return [(places[g], places[(g + step) % count]) for g in range(count)]


def lasting(micros):
    return pl.CostEstimate(flops=int(micros * COST_SCALE * 1150000000), bytes_accessed=0, transcendentals=0)


def split_terms(values):
    top = values.astype(bf16)
    return top, (values - top.astype(f32)).astype(bf16)


def half_swap(first, second):
    low = lax.broadcasted_iota(jnp.int32, first.shape, 1) < LANES // 2
    left = jnp.where(low, first, pltpu.roll(second, LANES // 2, 1))
    right = jnp.where(low, pltpu.roll(first, LANES // 2, 1), second)
    return left, right


def tables_kernel(
    n_span, n_elem, adj_ref, map_ref, perm_ref, perm2_ref, base_ref, step_ref, send_ref
):
    own = adj_ref.shape[1]
    span_id, elem_id = lax.axis_index("span"), lax.axis_index("elem")
    lane = lax.broadcasted_iota(jnp.int32, (own, own), 1).astype(f32)
    sub = lax.broadcasted_iota(jnp.int32, (own, own), 0).astype(f32)
    eye = (lane == sub).astype(f32)
    first_own = (elem_id * own).astype(f32)
    first_next = (lax.rem(elem_id + 1, n_elem) * own).astype(f32)
    first_prev = (lax.rem(elem_id + n_elem - 1, n_elem) * own).astype(f32)

    def column(row):
        return jnp.sum(eye * row, axis=1, keepdims=True)

    def inside(ids, first):
        return (ids >= first) & (ids < first + own)

    adj_row = [adj_ref[j : j + 1, :].astype(f32) for j in range(4)]
    map_row = [map_ref[j : j + 1, :].astype(f32) for j in range(4)]
    meets = [(sub == adj_row[j] - first_own).astype(f32) for j in range(4)]
    near = (eye + meets[0] + meets[1] + meets[2] + meets[3]).astype(bf16)
    prev_row = jnp.zeros((1, own), f32)
    next_row = jnp.zeros((1, own), f32)
    for j in range(4):
        prev_row = prev_row + jnp.where(inside(adj_row[j], first_prev), adj_row[j] + 1.0, 0.0)
        next_row = next_row + jnp.where(inside(adj_row[j], first_next), adj_row[j] + 1.0, 0.0)
    prev_col, next_col = column(prev_row), column(next_row)
    reached = jnp.broadcast_to((prev_col > 0).astype(f32), (own, own))
    row_col = 1.0 - reached
    for _ in range(n_span - 2):
        reached = jnp.minimum(
            jnp.dot(near, reached.astype(bf16), preferred_element_type=f32), 1.0
        )
        row_col = row_col + 1.0 - reached
    row_row = jnp.sum(eye * row_col, axis=0, keepdims=True)
    same = row_col == row_row
    pos_col = jnp.sum((same & (lane < sub)).astype(f32), axis=1, keepdims=True)
    pos_row = jnp.sum((same & (sub < lane)).astype(f32), axis=0, keepdims=True)
    odd = lax.rem(elem_id, 2) == 1
    orders = row_orders(n_span)
    slot_row = jnp.zeros_like(row_row)
    for r in range(n_span):
        slot = jnp.where(odd, orders[1][r], orders[0][r]).astype(f32)
        slot_row = jnp.where(row_row == float(r), slot, slot_row)
    new_row = slot_row * float(MESH_X) + pos_row
    perm = (sub == new_row).astype(f32).astype(bf16)
    perm_ref[:, :own] = perm
    perm_ref[:, own:] = perm
    perm2_ref[:own] = perm
    perm2_ref[own:] = perm

    def rank(col, row):
        return jnp.sum(((col > 0) & (col < row)).astype(f32), axis=0, keepdims=True)

    rank_prev, rank_next = rank(prev_col, prev_row), rank(next_col, next_row)
    spot = lax.broadcasted_iota(jnp.int32, (MESH_X, own), 0).astype(f32)
    here = new_row == spot + (span_id * MESH_X).astype(f32)
    edge_up = jnp.zeros_like(row_row)
    edge_down = jnp.zeros_like(row_row)

    def chosen(values):
        picks = jnp.sum(jnp.where(here, values, 0.0), axis=1, keepdims=True)
        return jnp.broadcast_to(picks, (MESH_X, own))

    per_elem = float(TRACE_ROWS)
    per_row = MESH_X * per_elem
    side_rows = float(MESH_X * SIDE)
    for j in range(4):
        its_pos = jnp.sum(meets[j] * pos_col, axis=0, keepdims=True)
        its_row = jnp.sum(meets[j] * row_col, axis=0, keepdims=True)
        inner = inside(adj_row[j], first_own)
        ahead = inside(adj_row[j], first_next)
        behind = inside(adj_row[j], first_prev)
        up = ahead | (inner & (its_row == row_row + 1.0))
        down = behind | (inner & (its_row == row_row - 1.0))
        its_pos = jnp.where(ahead, rank_next, jnp.where(behind, rank_prev, its_pos))
        base = jnp.where(
            up,
            per_row + its_pos,
            jnp.where(down, per_row + side_rows + its_pos, its_pos * per_elem + map_row[j]),
        )
        edge_up = jnp.where(up, float(j), edge_up)
        edge_down = jnp.where(down, float(j), edge_down)
        rows = slice(j * MESH_X, (j + 1) * MESH_X)
        base_ref[rows] = chosen(base)
        step_ref[rows] = chosen(jnp.where(up | down, float(MESH_X), 4.0))
    send_ref[:MESH_X] = chosen(edge_up) + spot * per_elem
    send_ref[MESH_X:] = chosen(edge_down) + spot * per_elem


def mesh_tables(adjacency, edge_map, n_span, n_elem):
    own = adjacency.shape[0]
    return pl.pallas_call(
        functools.partial(tables_kernel, n_span, n_elem),
        out_shape=(
            jax.ShapeDtypeStruct((own, 2 * own), bf16),
            jax.ShapeDtypeStruct((2 * own, own), bf16),
            jax.ShapeDtypeStruct((4 * MESH_X, own), f32),
            jax.ShapeDtypeStruct((4 * MESH_X, own), f32),
            jax.ShapeDtypeStruct((2 * MESH_X, own), f32),
        ),
        in_specs=[
            pl.BlockSpec(memory_space=pltpu.VMEM),
            pl.BlockSpec(memory_space=pltpu.VMEM),
        ],
        out_specs=[pl.BlockSpec(memory_space=pltpu.VMEM)] * 5,
        cost_estimate=lasting(3),
        name="mesh_tables",
    )(adjacency.T, edge_map.T)


def link_kernel(
    base_ref, step_ref, send_ref, from_ref, turn_ref, skip_ref, out_ref, move_ref, link_ref, pick_ref
):
    def spread(table, values):
        return jnp.dot(table[...], values[...], precision=highest, preferred_element_type=f32)

    def fill(ref, wanted):
        for c in range(0, ref.shape[1], LANES):
            width = min(LANES, ref.shape[1] - c)
            lane = lax.broadcasted_iota(jnp.int32, wanted.shape, 1).astype(f32) + float(c)
            ref[:, c : c + width] = (wanted == lane).astype(f32).astype(bf16)[:, :width]

    fill(link_ref, spread(from_ref, base_ref) + turn_ref[...] * spread(from_ref, step_ref) + skip_ref[...])
    fill(pick_ref, spread(out_ref, send_ref) + move_ref[...])


def link_matrices(base, step, send, own):
    rows = MESH_X * TRACE_ROWS
    from_edge = np.zeros((rows, 4 * MESH_X), np.float32)
    turn = np.zeros((rows, own), np.float32)
    skip = np.full((rows, own), -1.0, np.float32)
    for i in range(MESH_X):
        for t in range(SIDE):
            for j in range(4):
                row = i * TRACE_ROWS + t * 4 + j
                from_edge[row, j * MESH_X + i] = 1.0
                turn[row] = SIDE - 1 - t
                skip[row] = 0.0
    side_rows = SIDE * MESH_X
    out_edge = np.zeros((2 * side_rows, 2 * MESH_X), np.float32)
    move = np.zeros((2 * side_rows, own), np.float32)
    for way in range(2):
        for t in range(SIDE):
            for i in range(MESH_X):
                row = way * side_rows + t * MESH_X + i
                out_edge[row, way * MESH_X + i] = 1.0
                move[row] = 4 * t
    vmem = pl.BlockSpec(memory_space=pltpu.VMEM)
    return pl.pallas_call(
        link_kernel,
        out_shape=(
            jax.ShapeDtypeStruct((rows, rows + 2 * side_rows), bf16),
            jax.ShapeDtypeStruct((2 * side_rows, rows), bf16),
        ),
        in_specs=[vmem] * 8,
        out_specs=[vmem] * 2,
        cost_estimate=lasting(4),
        name="link_matrices",
    )(base, step, send, from_edge, turn, skip, out_edge, move)


def source_kernel(s, part, binary_ref, dref_ref, species_ref, lap_ref, perm_ref, *refs):
    out_ref, done_ref = refs[-2:]
    done_ref[...] = jnp.zeros_like(done_ref)
    per_step, n_species, zl, own = species_ref.shape
    n_span = out_ref.shape[0]
    perm = perm_ref[...]

    def inverse(value):
        return 1.0 / jnp.full((8, own), value, f32)

    def wide(row):
        return jnp.broadcast_to(row[:1], (zl, own))

    scaled = [dref_ref[s] * inverse(binary_ref[s, j]) for j in range(n_species + 1)]
    bath = wide(scaled[n_species])
    other = [wide(scaled[j] - scaled[n_species]) for j in range(n_species)]
    inv_dref = wide(inverse(dref_ref[s]))

    def source(n):
        parts = [species_ref[n, j] for j in range(n_species)]
        resistance = bath - bath * parts[s]
        for j in range(n_species):
            if j != s:
                resistance = resistance + parts[j] * other[j]
        mixture = (1.0 - parts[s]) * pl.reciprocal(resistance, approx=False)
        return parts[s] * inv_dref + (mixture - 1.0) * lap_ref[n, 0]

    def turned(first, second):
        top, rest = split_terms(jnp.concatenate([first, second], axis=0))
        both = jnp.concatenate([top, rest], axis=1)
        return lax.dot_general(
            perm, both, (((1,), (1,)), ((), ())), preferred_element_type=f32
        )

    def blocks():
        pairs = per_step // 2
        for k in range(pairs):
            tile = turned(source(2 * k), source(2 * k + 1))
            for q in range(n_span):
                rows = block_rows(part, k, pairs)
                out_ref[q, rows, :] = tile[q * MESH_X : (q + 1) * MESH_X]

    def tail():
        value = source(0)
        tile = turned(value, value)
        half = MESH_X // 2
        low = lax.broadcasted_iota(jnp.int32, (half, 2 * zl), 1) < zl
        for q in range(n_span):
            block = tile[q * MESH_X : (q + 1) * MESH_X]
            out_ref[q, :half, :] = jnp.where(low, block[:half], block[half:])

    by_step(part > 0, blocks, tail)


def block_rows(part, k, pairs):
    if part == WHOLE:
        return slice(k * MESH_X, (k + 1) * MESH_X)
    return pl.ds(k, MESH_X, stride=pairs)


def by_step(has_tail, blocks, tail):
    if not has_tail:
        blocks()
        return
    last_step = pl.num_programs(0) - 1
    pl.when(pl.program_id(0) < last_step)(blocks)
    pl.when(pl.program_id(0) == last_step)(tail)


def part_blocks(n_nodes, part):
    groups = n_nodes // (2 * PAIRS)
    rows = MESH_X * PAIRS
    first = groups // 2
    if part == 0:
        return 0, first, first * rows
    if part == WHOLE:
        return 0, groups + 1, groups * rows + MESH_X // 2
    return first, groups - first + 1, (groups - first) * rows + MESH_X // 2


def packed_source(s, part, species, laplacian, binary, dref, perm, n_span, after):
    n_nodes, n_species, zl, own = species.shape
    step = 2 * PAIRS
    begin, steps, rows = part_blocks(n_nodes, part)
    return pl.pallas_call(
        functools.partial(source_kernel, s, part),
        grid=(steps,),
        out_shape=(jax.ShapeDtypeStruct((n_span, rows, 2 * zl), f32), DONE),
        in_specs=[
            pl.BlockSpec(memory_space=pltpu.SMEM),
            pl.BlockSpec(memory_space=pltpu.SMEM),
            pl.BlockSpec((step, n_species, zl, own), lambda g: (g + begin, 0, 0, 0)),
            pl.BlockSpec((step, 1, zl, own), lambda g: (g + begin, s, 0, 0)),
            pl.BlockSpec((own, 2 * own), lambda g: (0, 0)),
        ]
        + [pl.BlockSpec(memory_space=pl.ANY)] * len(after),
        out_specs=(
            pl.BlockSpec((n_span, MESH_X * PAIRS, 2 * zl), lambda g: (0, g, 0)),
            pl.BlockSpec(DONE.shape, lambda g: (0, 0)),
        ),
        compiler_params=pltpu.CompilerParams(vmem_limit_bytes=VMEM_BYTES),
        cost_estimate=lasting(4),
        name="packed_source",
    )(binary, dref, species, laplacian, perm, *after)


def unpack_kernel(part, recv_ref, perm_ref, *refs):
    out_ref = refs[-1]
    n_span = recv_ref.shape[0]
    per_step, _, zl, _ = out_ref.shape
    perm = perm_ref[...]

    def turned(tile):
        top, rest = split_terms(tile)
        both = jnp.concatenate([top, rest], axis=0)
        return lax.dot_general(
            both, perm, (((0,), (0,)), ((), ())), preferred_element_type=f32
        )

    def blocks():
        pairs = per_step // 2
        for k in range(pairs):
            tile = jnp.concatenate(
                [recv_ref[q, block_rows(part, k, pairs), :] for q in range(n_span)], axis=0
            )
            result = turned(tile)
            out_ref[2 * k, 0] = result[:zl]
            out_ref[2 * k + 1, 0] = result[zl:]

    def tail():
        half = MESH_X // 2
        sides = []
        for q in range(n_span):
            block = recv_ref[q, :half, :]
            sides += [block, pltpu.roll(block, zl, 1)]
        out_ref[0, 0] = turned(jnp.concatenate(sides, axis=0))[:zl]

    by_step(part > 0, blocks, tail)


def unpacked(s, part, recv, perm2, shape, before):
    n_nodes, n_species, zl, own = shape
    n_span, _, width = recv.shape
    step = 2 * PAIRS
    begin, steps, _ = part_blocks(n_nodes, part)
    operands = [recv, perm2] + ([] if before is None else [before])
    return pl.pallas_call(
        functools.partial(unpack_kernel, part),
        grid=(steps,),
        out_shape=jax.ShapeDtypeStruct(shape, f32),
        in_specs=[
            pl.BlockSpec((n_span, MESH_X * PAIRS, width), lambda g: (0, g, 0)),
            pl.BlockSpec((2 * own, own), lambda g: (0, 0)),
        ]
        + ([] if before is None else [pl.BlockSpec(memory_space=pl.ANY)]),
        out_specs=pl.BlockSpec((step, 1, zl, own), lambda g: (g + begin, s, 0, 0)),
        input_output_aliases={} if before is None else {2: 0},
        compiler_params=pltpu.CompilerParams(vmem_limit_bytes=UNPACK_BYTES),
        cost_estimate=lasting(0.1),
        name="unpacked",
    )(*operands)


def left_product(matrix, values):
    rows = matrix.shape[0] // 2
    top, rest = split_terms(values)
    both = jnp.dot(matrix, top, preferred_element_type=f32)
    return both[:rows] + both[rows:] + jnp.dot(matrix[:rows], rest, preferred_element_type=f32)


def right_product(values, top_ref, rest_ref):
    rows = values.shape[0]
    top, rest = split_terms(values)
    both = jnp.dot(jnp.concatenate([top, rest], axis=0), top_ref[...], preferred_element_type=f32)
    return both[:rows] + both[rows:] + jnp.dot(top, rest_ref[...], preferred_element_type=f32)


def chunk_rows(index, size):
    return pl.ds(pl.multiple_of(index * size, size), size)


def send_traces(trace_ref, pick_ref, up_ref, down_ref):
    top, rest = split_terms(trace_ref[...])
    out = jnp.dot(pick_ref[...], top, preferred_element_type=f32)
    out = out + jnp.dot(pick_ref[...], rest, preferred_element_type=f32)
    half = up_ref.shape[0]
    up_ref[...] = out[:half]
    down_ref[...] = out[half:]


def sent_block(sent, g, i):
    if len(sent) == 1:
        return sent[0], pl.ds(g * MESH_X * PAIRS + i, PAIRS, stride=MESH_X)
    before = sent[0].shape[1] // (MESH_X * PAIRS)
    if g < before:
        return sent[0], chunk_rows(g * MESH_X + i, PAIRS)
    return sent[1], chunk_rows((g - before) * MESH_X + i, PAIRS)


def sent_tail(sent):
    half = MESH_X // 2
    groups = sum(ref.shape[1] - half * (ref is sent[-1]) for ref in sent) // (MESH_X * PAIRS)
    return groups, sent[-1], sent[-1].shape[1] - half


def start_kernel(*refs):
    *sent, top_ref, rest_ref, diag_ref, eigen_ref, edge_ref, pick_ref = refs[:-6]
    w_ref, trace_ref, up_ref, down_ref, x, ends = refs[-6:]
    n_span = sent[0].shape[0]
    half = MESH_X // 2
    groups, late_ref, tail = sent_tail(sent)
    first = lax.broadcasted_iota(jnp.int32, (8, x.shape[1]), 0) == 0
    for tile in range(n_span // 2):
        lanes = slice(tile * LANES, (tile + 1) * LANES)
        left, right = half_swap(late_ref[2 * tile, tail:, :], late_ref[2 * tile + 1, tail:, :])
        ends[:half, lanes] = left
        ends[half:, lanes] = right

    def quad(c, carry):
        for ii in range(QUAD):
            i = c * QUAD + ii
            for tile in range(n_span // 2):
                lanes = slice(tile * LANES, (tile + 1) * LANES)
                for g in range(groups):
                    ref, block = sent_block(sent, g, i)
                    left, right = half_swap(ref[2 * tile, block, :], ref[2 * tile + 1, block, :])
                    base = ii * NODE_ROWS + g * PAIRS
                    x[base : base + PAIRS, lanes] = left
                    base += groups * PAIRS
                    x[base : base + PAIRS, lanes] = right
            base = ii * NODE_ROWS + 2 * groups * PAIRS
            x[base : base + 8, :] = jnp.where(first, ends[pl.ds(i, 1), :], 0.0)
        y = right_product(x[...], top_ref, rest_ref)
        for p in range(QUAD // 2):
            part = slice(p * 2 * NODE_ROWS, (p + 1) * 2 * NODE_ROWS)
            w = left_product(eigen_ref[...], y[part])
            pair = c * (QUAD // 2) + p
            w_ref[chunk_rows(pair, 2 * NODE_ROWS), :] = w
            trace_ref[chunk_rows(pair, 2 * TRACE_ROWS), :] = left_product(
                edge_ref[...], w * diag_ref[...]
            )
        return carry

    lax.fori_loop(0, MESH_X // QUAD, quad, 0, unroll=True)
    send_traces(trace_ref, pick_ref, up_ref, down_ref)


def fill_sources(trace_ref, above_ref, below_ref, top, rest):
    row = 0
    for ref in (trace_ref, above_ref, below_ref):
        block = slice(row, row + ref.shape[0])
        top[block], rest[block] = split_terms(ref[...])
        row += ref.shape[0]


def met_traces(link_ref, top, rest, met):
    met[...] = jnp.dot(link_ref[...], top[...], preferred_element_type=f32) + jnp.dot(
        link_ref[...], rest[...], preferred_element_type=f32
    )


def sweep_kernel(sweep_id, rounds_ref, diag_ref, link_ref, pick_ref, inner_ref, edge_ref, *refs):
    begun = sweep_id > 1
    start_ref, trace_ref, above_ref, below_ref = refs[:4]
    held_ref = refs[4] if begun else None
    kept_ref, tout_ref, up_ref, down_ref, top, rest, gathered = refs[5 if begun else 4 :]
    fill_sources(trace_ref, above_ref, below_ref, top, rest)
    met_traces(link_ref, top, rest, gathered)
    going = rounds_ref[...] > sweep_id

    def quad(c, carry):
        rows = chunk_rows(c, QUAD * TRACE_ROWS)
        met = gathered[rows, :]
        kept_ref[rows, :] = jnp.where(going, met, held_ref[rows, :] if begun else 0.0)
        for p in range(QUAD // 2):
            part = met[p * 2 * TRACE_ROWS : (p + 1) * 2 * TRACE_ROWS]
            field = left_product(inner_ref[...], part) * diag_ref[...]
            rows = chunk_rows(c * (QUAD // 2) + p, 2 * TRACE_ROWS)
            tout_ref[rows, :] = start_ref[rows, :] + left_product(edge_ref[...], field)
        return carry

    lax.fori_loop(0, MESH_X // QUAD, quad, 0, unroll=True)
    send_traces(tout_ref, pick_ref, up_ref, down_ref)


def finish_kernel(
    sweep_id, rounds_ref, diag_ref, link_ref, inner_ref, nodal_ref, trace_ref, above_ref,
    below_ref, held_ref, w_ref, top_ref, rest_ref, *refs,
):
    *sent, top, rest, gathered, modal, ends = refs
    n_span = sent[0].shape[0]
    half = MESH_X // 2
    groups, late_ref, tail = sent_tail(sent)
    fill_sources(trace_ref, above_ref, below_ref, top, rest)
    met_traces(link_ref, top, rest, gathered)
    going = rounds_ref[...] > sweep_id

    def quad(c, carry):
        rows = chunk_rows(c, QUAD * TRACE_ROWS)
        kept = jnp.where(going, gathered[rows, :], held_ref[rows, :])
        for p in range(QUAD // 2):
            part = kept[p * 2 * TRACE_ROWS : (p + 1) * 2 * TRACE_ROWS]
            rows = chunk_rows(c * (QUAD // 2) + p, 2 * NODE_ROWS)
            field = (w_ref[rows, :] + left_product(inner_ref[...], part)) * diag_ref[...]
            modal[p * 2 * NODE_ROWS : (p + 1) * 2 * NODE_ROWS] = left_product(
                nodal_ref[...], field
            )
        z = right_product(modal[...], top_ref, rest_ref)
        for ii in range(QUAD):
            i = c * QUAD + ii
            for tile in range(n_span // 2):
                lanes = slice(tile * LANES, (tile + 1) * LANES)
                for g in range(groups):
                    base = ii * NODE_ROWS + g * PAIRS
                    later = base + groups * PAIRS
                    left, right = half_swap(
                        z[base : base + PAIRS, lanes], z[later : later + PAIRS, lanes]
                    )
                    ref, block = sent_block(sent, g, i)
                    ref[2 * tile, block, :] = left
                    ref[2 * tile + 1, block, :] = right
            base = ii * NODE_ROWS + 2 * groups * PAIRS
            ends[pl.ds(i, 1), :] = z[base : base + 1]
        return carry

    lax.fori_loop(0, MESH_X // QUAD, quad, 0, unroll=True)
    for tile in range(n_span // 2):
        lanes = slice(tile * LANES, (tile + 1) * LANES)
        left, right = half_swap(ends[:half, lanes], ends[half:, lanes])
        late_ref[2 * tile, tail:, :] = left
        late_ref[2 * tile + 1, tail:, :] = right


def vmem_call(kernel, name, out_shape, scratch, micros, operands, after):
    count, extra = len(operands), len(after)

    def ordered(*refs):
        last = count + extra + len(out_shape)
        refs[last][...] = jnp.zeros_like(refs[last])
        kernel(*refs[:count], *refs[count + extra : last], *refs[last + 1 :])

    vmem = pl.BlockSpec(memory_space=pltpu.VMEM)
    return pl.pallas_call(
        ordered,
        out_shape=tuple(out_shape) + (DONE,),
        in_specs=[vmem] * count + [pl.BlockSpec(memory_space=pl.ANY)] * extra,
        out_specs=tuple([vmem] * (len(out_shape) + 1)),
        scratch_shapes=scratch,
        compiler_params=pltpu.CompilerParams(vmem_limit_bytes=VMEM_BYTES),
        cost_estimate=lasting(micros),
        name=name,
    )(*operands, *after)


def stacked_terms(values):
    return jnp.concatenate(outer_split(values), axis=0)


def twice(matrix):
    zero = jnp.zeros_like(matrix)
    return jnp.concatenate(
        [jnp.concatenate([matrix, zero], axis=1), jnp.concatenate([zero, matrix], axis=1)], axis=0
    )


def nodal_matrices(basis):
    m = basis.shape[0]
    n_nodes = m * m
    kron_basis = (basis[:, None, :, None] * basis[None, :, None, :]).reshape(n_nodes, n_nodes)
    order = np.concatenate(
        [np.arange(0, n_nodes - 1, 2), np.arange(1, n_nodes - 1, 2), [n_nodes - 1]]
    )
    edges = np.array(edge_lists(m)).T.reshape(-1)
    full, edge = NODE_ROWS - n_nodes, TRACE_ROWS - edges.size
    nodal = jnp.pad(kron_basis[order], ((0, full), (0, full)))
    traces = jnp.pad(kron_basis[edges], ((0, edge), (0, full)))
    return [
        stacked_terms(twice(matrix)) for matrix in (nodal.T, traces, coupling * traces.T, nodal)
    ]


def solve_stages(n_sweeps, arrived, sent_shapes, rounds_row, diag, link, pick, matrices, forward, backward):
    eigen, edge, inner, nodal = matrices
    planes = forward[0].shape[0]
    w_shape = jax.ShapeDtypeStruct((MESH_X * NODE_ROWS, planes), f32)
    trace = jax.ShapeDtypeStruct((MESH_X * TRACE_ROWS, planes), f32)
    side = jax.ShapeDtypeStruct((MESH_X * SIDE, planes), f32)
    sources = pltpu.VMEM((link.shape[1], planes), bf16)
    gathered = pltpu.VMEM(trace.shape, f32)
    quad = pltpu.VMEM((QUAD * NODE_ROWS, planes), f32)
    ends = pltpu.VMEM((MESH_X, planes), f32)
    axes = ("span", "elem")
    n_span, n_elem = lax.axis_size("span"), lax.axis_size("elem")

    def exchange(up, down):
        below = lax.ppermute(up, axes, ring_route(n_span, n_elem, 1))
        above = lax.ppermute(down, axes, ring_route(n_span, n_elem, -1))
        return above, below

    after = yield None
    w, start, up, down, mark = vmem_call(
        start_kernel,
        "start_solve",
        [w_shape, trace, side, side],
        [quad, ends],
        16,
        arrived + [forward[0], forward[1], diag, eigen, edge, pick],
        after,
    )
    traces, held = start, []
    for sweep_id in range(1, n_sweeps):
        above, below = exchange(up, down)
        after = yield mark, None
        kept, traces, up, down, mark = vmem_call(
            functools.partial(sweep_kernel, sweep_id),
            "sweep_solve",
            [trace, trace, side, side],
            [sources, sources, gathered],
            10,
            [rounds_row, diag, link, pick, inner, edge, start, traces, above, below] + held,
            after,
        )
        held = [kept]
    above, below = exchange(up, down)
    after = yield mark, None
    *result, mark = vmem_call(
        functools.partial(finish_kernel, n_sweeps),
        "finish_solve",
        [jax.ShapeDtypeStruct(shape, f32) for shape in sent_shapes],
        [sources, sources, gathered, quad, ends],
        17,
        [rounds_row, diag, link, inner, nodal, traces, above, below, kept, w]
        + [backward[0], backward[1]],
        after,
    )
    yield mark, result


def transform_terms(planes):
    modes = np.tile(np.arange(planes // 2), 2)
    angles = np.arange(planes)[:, None] * modes[None, :] % planes * (2 * np.pi / planes)
    real = np.arange(planes)[None, :] < planes // 2
    table = np.where(real, np.cos(angles), -np.sin(angles))
    weights = np.where(modes == 0, 1.0, 2.0)

    def terms(values):
        top = values.astype(bf16)
        return top, (values - top.astype(np.float64)).astype(bf16)

    return terms(table / planes), terms((table * weights[None, :]).T)


def outer_split(values):
    top = lax.reduce_precision(values, exponent_bits=8, mantissa_bits=7)
    return top.astype(bf16), (values - top).astype(bf16)


def row_body(species, laplacian, binary, dref, stiff_eig, basis, rounds, adjacency, edge_map):
    n_nodes, n_species, zl, own = species.shape
    n_span = lax.axis_size("span")
    n_elem = lax.axis_size("elem")
    planes = zl * n_span
    n_modes = planes // 2
    perm, perm2, base, step, send = mesh_tables(adjacency, edge_map, n_span, n_elem)

    def across(sent):
        return lax.all_to_all(sent, "span", split_axis=0, concat_axis=0, tiled=True)

    link, pick = link_matrices(base, step, send, own)
    matrices = nodal_matrices(basis)
    forward, backward = transform_terms(planes)
    col_mode = jnp.tile(jnp.arange(n_modes, dtype=jnp.int32), 2)
    wavenumber = col_mode.astype(f32) * (8.0 / planes)
    shifts = 1.0 / dref[:, None] + (wavenumber * wavenumber)[None, :]
    eig_sum = (stiff_eig[:, None] + stiff_eig[None, :]).reshape(n_nodes)
    eig_sum = jnp.tile(jnp.pad(eig_sum, (0, NODE_ROWS - n_nodes)), 2)
    diag = 1.0 / (shifts[:, None, :] + eig_sum[None, :, None])
    rounds_row = jnp.tile(rounds, 2).reshape(1, planes)

    in_parts = [(WHOLE,) if FIRST_WHOLE and s == 0 else (0, 1) for s in range(n_species)]
    out_parts = [(WHOLE,) if s + 1 == n_species else (0, 1) for s in range(n_species)]
    steps, count = [], 0
    arrived_by, slots, back_slots = [], [], []
    for parts, slot_list in ((in_parts, slots), (out_parts, back_slots)):
        for group in parts:
            slot_list.append(range(count, count + len(group)))
            count += len(group)
    in_count = slots[-1][-1] + 1
    for s in range(n_species):
        for slot, part in zip(slots[s], in_parts[s]):
            early = min(slot - 2, slots[0][-1] - 1) if slot < 3 else slots[0][-1] - 1
            steps.append((early if slot else -2, 2, slot, s, ("pack", part)))
        first = slots[s][-1]
        for stage in range(N_SWEEPS + 1):
            steps.append((first + stage, 0, s, s, ("solve", stage)))
        for slot, part in zip(back_slots[s], out_parts[s]):
            steps.append((slot, 1, slot, s, ("unpack", part)))
    moved, waiting, solves, mark = [], [], [], []
    updated, last = None, -2
    for arrival, _, _, s, (kind, index) in sorted(steps):
        if arrival > last and waiting:
            final = len(moved) + 1 == count
            moved.append(across(released(waiting.pop(0), mark + (moved[-1:] if final else []))))
        last = arrival
        after = mark + (moved[arrival : arrival + 1] if arrival >= 0 else [])
        if kind == "pack":
            sent, done = packed_source(
                s, index, species, laplacian, binary, dref, perm, n_span, after
            )
            waiting.append(sent)
            mark = [done]
        elif kind == "solve":
            if index == 0:
                shapes = [
                    (n_span, part_blocks(n_nodes, part)[2], 2 * zl) for part in out_parts[s]
                ]
                solves.append(
                    solve_stages(
                        N_SWEEPS, [moved[slot] for slot in slots[s]], shapes, rounds_row, diag[s],
                        link, pick, matrices, forward, backward,
                    )
                )
                next(solves[s])
            done, result = solves[s].send(after)
            mark = [done]
            if result is not None:
                waiting += result
        else:
            updated = unpacked(s, index, moved[arrival], perm2, species.shape, updated)
    return updated


def released(block, after):
    def kernel(*refs):
        pass

    anywhere = pl.BlockSpec(memory_space=pl.ANY)
    return pl.pallas_call(
        kernel,
        out_shape=jax.ShapeDtypeStruct(block.shape, block.dtype),
        in_specs=[anywhere] * (1 + len(after)),
        out_specs=anywhere,
        input_output_aliases={0: 0},
        name="released",
    )(block, *after)


def from_behind(block, axis, distance):
    devices = range(lax.axis_size(axis))
    route = [((i - distance) % len(devices), i) for i in devices]
    return lax.ppermute(block, axis, route)


def edge_matrix(per_side):
    edge_table = np.zeros((4, per_side, per_side * per_side), np.float32)
    for edge_id, node_list in enumerate(edge_lists(per_side)):
        for i, node_id in enumerate(node_list):
            edge_table[edge_id, i, node_id] = 1.0
    return edge_table


def mixture_source(species, laplacian, binary, dref):
    n_species = species.shape[1]
    bath_share = 1.0 - jnp.sum(species, axis=1)
    source_parts = []
    for s in range(n_species):
        resistance = bath_share / binary[s, n_species]
        for j in range(n_species):
            if j != s:
                resistance = resistance + species[:, j] / binary[s, j]
        mixture = (1.0 - species[:, s]) / resistance
        source_parts.append((species[:, s] + (mixture - dref[s]) * laplacian[:, s]) / dref[s])
    return jnp.stack(source_parts, axis=1)


def block_inverse(values, kron_basis, inverse_diag):
    n_nodes = values.shape[0]
    inner_part = (
        jnp.dot(kron_basis.T, values.reshape(n_nodes, -1), precision=highest).reshape(values.shape)
        * inverse_diag
    )
    return jnp.dot(kron_basis, inner_part.reshape(n_nodes, -1), precision=highest).reshape(
        values.shape
    )


def transform_tables(col_mode, col_part, planes):
    plane_ids = jnp.arange(planes, dtype=jnp.int32)
    phase_id = plane_ids[:, None] * col_mode[None, :] % planes
    angles = phase_id.astype(jnp.float32) * (two_pi / planes)
    trig_table = jnp.where(col_part[None, :] == 0, jnp.cos(angles), -jnp.sin(angles))
    weights = jnp.where(col_mode == 0, 1.0, 2.0).astype(jnp.float32)
    return (trig_table / planes, (trig_table * weights[None, :]).T)


def body(species, laplacian, binary, dref, stiff_eig, basis, rounds, adjacency, edge_map):
    per_side = basis.shape[0]
    n_nodes = per_side * per_side
    n_span = lax.axis_size("span")
    n_elem = lax.axis_size("elem")
    planes = species.shape[2] * n_span
    n_modes = planes // 2
    per_device = n_modes // n_span
    half_tile = per_device // 2
    own_count = adjacency.shape[0]
    source = mixture_source(species, laplacian, binary, dref)
    assign = jnp.arange(n_modes, dtype=jnp.int32).reshape(n_span, per_device)
    tile_count = 1
    col_mode = jnp.broadcast_to(
        assign.reshape(n_span, 2, 1, half_tile), (n_span, 2, 2, half_tile)
    ).reshape(planes)
    col_part = jnp.broadcast_to(
        jnp.arange(2, dtype=jnp.int32).reshape(1, 1, 2, 1), (n_span, 2, 2, half_tile)
    ).reshape(planes)
    forward, backward = transform_tables(col_mode, col_part, planes)
    source_swapped = jnp.transpose(source, (0, 1, 3, 2))
    coeffs = jnp.einsum(
        "nsez,zr->nser",
        lax.all_to_all(source_swapped, "span", split_axis=2, concat_axis=3, tiled=True),
        forward,
        precision=highest,
    )
    exchanged = lax.all_to_all(coeffs, "span", split_axis=3, concat_axis=2, tiled=True)
    modal_rhs = jnp.transpose(exchanged, (0, 1, 3, 2))
    columns = 2 * per_device
    my_modes = lax.dynamic_slice_in_dim(col_mode, lax.axis_index("span") * columns, columns)
    my_rounds = rounds[my_modes]
    wavenumber = my_modes.astype(jnp.float32) * (8.0 / planes)
    shifts = 1.0 / dref[:, None] + (wavenumber * wavenumber)[None, :]
    eig_sum = (stiff_eig[:, None] + stiff_eig[None, :]).reshape(n_nodes)
    inverse_diag = 1.0 / (shifts[None, :, :, None] + eig_sum[:, None, None, None])
    kron_basis = (basis[:, None, :, None] * basis[None, :, None, :]).reshape(n_nodes, n_nodes)
    flat_index = np.array(edge_lists(per_side)).reshape(-1)
    scatter_table = jnp.asarray(edge_matrix(per_side))
    owners = adjacency // own_count
    offset = (owners - lax.axis_index("elem") + n_elem) % n_elem
    local_id = adjacency % own_count
    flat_adj = adjacency.reshape(-1)
    flat_offset = offset.reshape(-1)
    earlier = flat_adj[None, :] < flat_adj[:, None]
    from_prev = flat_offset == n_elem - 1
    from_next = flat_offset == 1
    rank_prev = jnp.sum((earlier & from_prev[None, :]).astype(jnp.int32), axis=1)
    rank_next = jnp.sum((earlier & from_next[None, :]).astype(jnp.int32), axis=1)
    position = jnp.where(
        from_prev,
        own_count + rank_prev,
        jnp.where(from_next, own_count + MESH_X + rank_next, local_id.reshape(-1)),
    ).reshape(adjacency.shape)
    slot_ids = jnp.arange(MESH_X, dtype=jnp.int32)
    faces_next = jnp.any(offset == 1, axis=1)
    faces_prev = jnp.any(offset == n_elem - 1, axis=1)
    slot_next = jnp.cumsum(faces_next.astype(jnp.int32)) - 1
    slot_prev = jnp.cumsum(faces_prev.astype(jnp.int32)) - 1
    pick_next = (faces_next[:, None] & (slot_next[:, None] == slot_ids[None, :])).astype(
        jnp.float32
    )
    pick_prev = (faces_prev[:, None] & (slot_prev[:, None] == slot_ids[None, :])).astype(
        jnp.float32
    )

    def gather_pool(traces):
        send_up = jnp.einsum("ktsce,ea->ktsca", traces, pick_next, precision=highest)
        send_down = jnp.einsum("ktsce,ea->ktsca", traces, pick_prev, precision=highest)
        from_before = from_behind(send_up, "elem", 1)
        from_after = from_behind(send_down, "elem", -1)
        return jnp.concatenate([traces, from_before, from_after], axis=4)

    def couple(modal_field):
        traces = modal_field[flat_index].reshape((4, per_side) + modal_field.shape[1:])
        across = gather_pool(traces)[edge_map, :, :, :, position][:, :, ::-1]
        return jnp.einsum("jtn,ejtsc->nsce", scatter_table, across, precision=highest)

    tile_modes = assign.reshape(n_span, tile_count, per_device // tile_count)
    sweep_bound = jnp.max(rounds[tile_modes[:, 0].reshape(-1)])
    initial = block_inverse(modal_rhs, kron_basis, inverse_diag)

    def sweep_once(sweep_id, modal_field):
        proposal = block_inverse(
            modal_rhs + coupling * couple(modal_field), kron_basis, inverse_diag
        )
        return jnp.where(sweep_id < my_rounds[:, None], proposal, modal_field)

    solved = lax.fori_loop(1, sweep_bound, sweep_once, initial)
    solution_swapped = jnp.transpose(solved, (0, 1, 3, 2))
    values = jnp.einsum(
        "nser,rz->nsez",
        lax.all_to_all(solution_swapped, "span", split_axis=2, concat_axis=3, tiled=True),
        backward,
        precision=highest,
    )
    returned = lax.all_to_all(values, "span", split_axis=3, concat_axis=2, tiled=True)
    return jnp.transpose(returned, (0, 1, 3, 2))


def solution(mesh):
    n_span, n_elem = mesh.shape["span"], mesh.shape["elem"]

    def chosen_body(species, *rest):
        zl, own = species.shape[2:]
        by_rows = n_span * MESH_X == own and 2 * zl == LANES == own and n_elem > 2
        by_rows = by_rows and species.shape[0] == SIDE * SIDE
        return (row_body if by_rows else body)(species, *rest)

    return jax.shard_map(
        chosen_body,
        mesh=mesh,
        in_specs=(
            P(None, None, "span", "elem"),
            P(None, None, "span", "elem"),
            P(),
            P(),
            P(),
            P(),
            P(),
            P("elem", None),
            P("elem", None),
        ),
        out_specs=P(None, None, "span", "elem"),
        check_vma=False,
    )
```

```python
import functools

import jax
import jax.numpy as jnp
import numpy as np
from jax import lax
from jax.experimental import pallas as pl
from jax.experimental.pallas import tpu as pltpu
from jax.sharding import PartitionSpec as P

MESH_X = 16
LANES = 128
SIDE = 9
PAIRS = 8
QUAD = 4
NODE_ROWS = 88
TRACE_ROWS = 40
N_SWEEPS = 3
WHOLE = 2
COST_SCALE = 5
DONE = jax.ShapeDtypeStruct((8, LANES), jnp.float32)
VMEM_BYTES = 60 * 1024 * 1024
UNPACK_BYTES = 48 * 1024 * 1024


coupling = 0.2
highest = lax.Precision.HIGHEST
two_pi = 6.283185307179586
f32 = jnp.float32
bf16 = jnp.bfloat16


def edge_lists(per_side):
    last_node = per_side - 1
    bottom = [i for i in range(per_side)]
    right_edge = [i * per_side + last_node for i in range(per_side)]
    top_edge = [last_node * per_side + last_node - i for i in range(per_side)]
    left_edge = [(last_node - i) * per_side for i in range(per_side)]
    return [bottom, right_edge, top_edge, left_edge]


def row_orders(n_span):
    even = [r ^ (r >> 1 & 1) for r in range(n_span)]
    odd = [r ^ int(2 * r >= n_span) for r in range(n_span)][::-1]
    return [even, odd]


def ring_route(n_span, n_elem, step):
    orders = row_orders(n_span)
    places = [orders[p % 2][r] * n_elem + p for p in range(n_elem) for r in range(n_span)]
    count = len(places)
    return [(places[g], places[(g + step) % count]) for g in range(count)]


def lasting(micros):
    return pl.CostEstimate(flops=int(micros * COST_SCALE * 1150000000), bytes_accessed=0, transcendentals=0)


def split_terms(values):
    top = values.astype(bf16)
    return top, (values - top.astype(f32)).astype(bf16)


def half_swap(first, second):
    low = lax.broadcasted_iota(jnp.int32, first.shape, 1) < LANES // 2
    left = jnp.where(low, first, pltpu.roll(second, LANES // 2, 1))
    right = jnp.where(low, pltpu.roll(first, LANES // 2, 1), second)
    return left, right


def tables_kernel(
    n_span, n_elem, adj_ref, map_ref, perm_ref, perm2_ref, base_ref, step_ref, send_ref
):
    own = adj_ref.shape[1]
    span_id, elem_id = lax.axis_index("span"), lax.axis_index("elem")
    lane = lax.broadcasted_iota(jnp.int32, (own, own), 1).astype(f32)
    sub = lax.broadcasted_iota(jnp.int32, (own, own), 0).astype(f32)
    eye = (lane == sub).astype(f32)
    first_own = (elem_id * own).astype(f32)
    first_next = (lax.rem(elem_id + 1, n_elem) * own).astype(f32)
    first_prev = (lax.rem(elem_id + n_elem - 1, n_elem) * own).astype(f32)

    def column(row):
        return jnp.sum(eye * row, axis=1, keepdims=True)

    def inside(ids, first):
        return (ids >= first) & (ids < first + own)

    adj_row = [adj_ref[j : j + 1, :].astype(f32) for j in range(4)]
    map_row = [map_ref[j : j + 1, :].astype(f32) for j in range(4)]
    meets = [(sub == adj_row[j] - first_own).astype(f32) for j in range(4)]
    near = (eye + meets[0] + meets[1] + meets[2] + meets[3]).astype(bf16)
    prev_row = jnp.zeros((1, own), f32)
    next_row = jnp.zeros((1, own), f32)
    for j in range(4):
        prev_row = prev_row + jnp.where(inside(adj_row[j], first_prev), adj_row[j] + 1.0, 0.0)
        next_row = next_row + jnp.where(inside(adj_row[j], first_next), adj_row[j] + 1.0, 0.0)
    prev_col, next_col = column(prev_row), column(next_row)
    reached = jnp.broadcast_to((prev_col > 0).astype(f32), (own, own))
    row_col = 1.0 - reached
    for _ in range(n_span - 2):
        reached = jnp.minimum(
            jnp.dot(near, reached.astype(bf16), preferred_element_type=f32), 1.0
        )
        row_col = row_col + 1.0 - reached
    row_row = jnp.sum(eye * row_col, axis=0, keepdims=True)
    same = row_col == row_row
    pos_col = jnp.sum((same & (lane < sub)).astype(f32), axis=1, keepdims=True)
    pos_row = jnp.sum((same & (sub < lane)).astype(f32), axis=0, keepdims=True)
    odd = lax.rem(elem_id, 2) == 1
    orders = row_orders(n_span)
    slot_row = jnp.zeros_like(row_row)
    for r in range(n_span):
        slot = jnp.where(odd, orders[1][r], orders[0][r]).astype(f32)
        slot_row = jnp.where(row_row == float(r), slot, slot_row)
    new_row = slot_row * float(MESH_X) + pos_row
    perm = (sub == new_row).astype(f32).astype(bf16)
    perm_ref[:, :own] = perm
    perm_ref[:, own:] = perm
    perm2_ref[:own] = perm
    perm2_ref[own:] = perm

    def rank(col, row):
        return jnp.sum(((col > 0) & (col < row)).astype(f32), axis=0, keepdims=True)

    rank_prev, rank_next = rank(prev_col, prev_row), rank(next_col, next_row)
    spot = lax.broadcasted_iota(jnp.int32, (MESH_X, own), 0).astype(f32)
    here = new_row == spot + (span_id * MESH_X).astype(f32)
    edge_up = jnp.zeros_like(row_row)
    edge_down = jnp.zeros_like(row_row)

    def chosen(values):
        picks = jnp.sum(jnp.where(here, values, 0.0), axis=1, keepdims=True)
        return jnp.broadcast_to(picks, (MESH_X, own))

    per_elem = float(TRACE_ROWS)
    per_row = MESH_X * per_elem
    side_rows = float(MESH_X * SIDE)
    for j in range(4):
        its_pos = jnp.sum(meets[j] * pos_col, axis=0, keepdims=True)
        its_row = jnp.sum(meets[j] * row_col, axis=0, keepdims=True)
        inner = inside(adj_row[j], first_own)
        ahead = inside(adj_row[j], first_next)
        behind = inside(adj_row[j], first_prev)
        up = ahead | (inner & (its_row == row_row + 1.0))
        down = behind | (inner & (its_row == row_row - 1.0))
        its_pos = jnp.where(ahead, rank_next, jnp.where(behind, rank_prev, its_pos))
        base = jnp.where(
            up,
            per_row + its_pos,
            jnp.where(down, per_row + side_rows + its_pos, its_pos * per_elem + map_row[j]),
        )
        edge_up = jnp.where(up, float(j), edge_up)
        edge_down = jnp.where(down, float(j), edge_down)
        rows = slice(j * MESH_X, (j + 1) * MESH_X)
        base_ref[rows] = chosen(base)
        step_ref[rows] = chosen(jnp.where(up | down, float(MESH_X), 4.0))
    send_ref[:MESH_X] = chosen(edge_up) + spot * per_elem
    send_ref[MESH_X:] = chosen(edge_down) + spot * per_elem


def mesh_tables(adjacency, edge_map, n_span, n_elem):
    own = adjacency.shape[0]
    return pl.pallas_call(
        functools.partial(tables_kernel, n_span, n_elem),
        out_shape=(
            jax.ShapeDtypeStruct((own, 2 * own), bf16),
            jax.ShapeDtypeStruct((2 * own, own), bf16),
            jax.ShapeDtypeStruct((4 * MESH_X, own), f32),
            jax.ShapeDtypeStruct((4 * MESH_X, own), f32),
            jax.ShapeDtypeStruct((2 * MESH_X, own), f32),
        ),
        in_specs=[
            pl.BlockSpec(memory_space=pltpu.VMEM),
            pl.BlockSpec(memory_space=pltpu.VMEM),
        ],
        out_specs=[pl.BlockSpec(memory_space=pltpu.VMEM)] * 5,
        cost_estimate=lasting(3),
        name="mesh_tables",
    )(adjacency.T, edge_map.T)


def link_kernel(
    base_ref, step_ref, send_ref, from_ref, turn_ref, skip_ref, out_ref, move_ref, link_ref, pick_ref
):
    def spread(table, values):
        return jnp.dot(table[...], values[...], precision=highest, preferred_element_type=f32)

    def fill(ref, wanted):
        for c in range(0, ref.shape[1], LANES):
            width = min(LANES, ref.shape[1] - c)
            lane = lax.broadcasted_iota(jnp.int32, wanted.shape, 1).astype(f32) + float(c)
            ref[:, c : c + width] = (wanted == lane).astype(f32).astype(bf16)[:, :width]

    fill(link_ref, spread(from_ref, base_ref) + turn_ref[...] * spread(from_ref, step_ref) + skip_ref[...])
    fill(pick_ref, spread(out_ref, send_ref) + move_ref[...])


def link_matrices(base, step, send, own):
    rows = MESH_X * TRACE_ROWS
    from_edge = np.zeros((rows, 4 * MESH_X), np.float32)
    turn = np.zeros((rows, own), np.float32)
    skip = np.full((rows, own), -1.0, np.float32)
    for i in range(MESH_X):
        for t in range(SIDE):
            for j in range(4):
                row = i * TRACE_ROWS + t * 4 + j
                from_edge[row, j * MESH_X + i] = 1.0
                turn[row] = SIDE - 1 - t
                skip[row] = 0.0
    side_rows = SIDE * MESH_X
    out_edge = np.zeros((2 * side_rows, 2 * MESH_X), np.float32)
    move = np.zeros((2 * side_rows, own), np.float32)
    for way in range(2):
        for t in range(SIDE):
            for i in range(MESH_X):
                row = way * side_rows + t * MESH_X + i
                out_edge[row, way * MESH_X + i] = 1.0
                move[row] = 4 * t
    vmem = pl.BlockSpec(memory_space=pltpu.VMEM)
    return pl.pallas_call(
        link_kernel,
        out_shape=(
            jax.ShapeDtypeStruct((rows, rows + 2 * side_rows), bf16),
            jax.ShapeDtypeStruct((2 * side_rows, rows), bf16),
        ),
        in_specs=[vmem] * 8,
        out_specs=[vmem] * 2,
        cost_estimate=lasting(4),
        name="link_matrices",
    )(base, step, send, from_edge, turn, skip, out_edge, move)


def source_kernel(s, part, n_nodes, binary_ref, dref_ref, species_ref, lap_ref, perm_ref, *refs):
    out_ref, done_ref = refs[-2:]
    done_ref[...] = jnp.zeros_like(done_ref)
    per_step, n_species, zl, own = species_ref.shape
    n_span = out_ref.shape[0]
    perm = perm_ref[...]

    def inverse(value):
        return 1.0 / jnp.full((8, own), value, f32)

    def wide(row):
        return jnp.broadcast_to(row[:1], (zl, own))

    scaled = [dref_ref[s] * inverse(binary_ref[s, j]) for j in range(n_species + 1)]
    bath = wide(scaled[n_species])
    other = [wide(scaled[j] - scaled[n_species]) for j in range(n_species)]
    inv_dref = wide(inverse(dref_ref[s]))

    def source(n):
        parts = [species_ref[n, j] for j in range(n_species)]
        resistance = bath - bath * parts[s]
        for j in range(n_species):
            if j != s:
                resistance = resistance + parts[j] * other[j]
        mixture = (1.0 - parts[s]) * pl.reciprocal(resistance, approx=False)
        return parts[s] * inv_dref + (mixture - 1.0) * lap_ref[n, 0]

    def turned(first, second):
        top, rest = split_terms(jnp.concatenate([first, second], axis=0))
        both = jnp.concatenate([top, rest], axis=1)
        return lax.dot_general(
            perm, both, (((1,), (1,)), ((), ())), preferred_element_type=f32
        )

    def blocks(count=None):
        pairs = per_step // 2
        for k in range(pairs if count is None else count):
            tile = turned(source(2 * k), source(2 * k + 1))
            for q in range(n_span):
                rows = block_rows(part, k, pairs)
                out_ref[q, rows, :] = tile[q * MESH_X : (q + 1) * MESH_X]

    def tail():
        left = before_tail(n_nodes, per_step)
        blocks(left // 2)
        value = source(left)
        tile = turned(value, value)
        half = MESH_X // 2
        low = lax.broadcasted_iota(jnp.int32, (half, 2 * zl), 1) < zl
        for q in range(n_span):
            block = tile[q * MESH_X : (q + 1) * MESH_X]
            row = left // 2 * MESH_X
            out_ref[q, row : row + half, :] = jnp.where(low, block[:half], block[half:])

    by_step(part > 0, blocks, tail)


def block_rows(part, k, pairs):
    if part == WHOLE:
        return slice(k * MESH_X, (k + 1) * MESH_X)
    return pl.ds(k, MESH_X, stride=pairs)


def before_tail(n_nodes, per_step):
    return (n_nodes - 1) % per_step


def by_step(has_tail, blocks, tail):
    if not has_tail:
        blocks()
        return
    last_step = pl.num_programs(0) - 1
    pl.when(pl.program_id(0) < last_step)(blocks)
    pl.when(pl.program_id(0) == last_step)(tail)


def part_blocks(n_nodes, part):
    groups = n_nodes // (2 * PAIRS)
    rows = MESH_X * PAIRS
    first = groups // 2
    if part == 0:
        return 0, first, first * rows, PAIRS
    if part == WHOLE:
        return 0, -(-n_nodes // (4 * PAIRS)), groups * rows + MESH_X // 2, 2 * PAIRS
    return first, groups - first + 1, (groups - first) * rows + MESH_X // 2, PAIRS


def packed_source(s, part, species, laplacian, binary, dref, perm, n_span, after):
    n_nodes, n_species, zl, own = species.shape
    begin, steps, rows, pairs = part_blocks(n_nodes, part)
    step = 2 * pairs
    return pl.pallas_call(
        functools.partial(source_kernel, s, part, n_nodes),
        grid=(steps,),
        out_shape=(jax.ShapeDtypeStruct((n_span, rows, 2 * zl), f32), DONE),
        in_specs=[
            pl.BlockSpec(memory_space=pltpu.SMEM),
            pl.BlockSpec(memory_space=pltpu.SMEM),
            pl.BlockSpec((step, n_species, zl, own), lambda g: (g + begin, 0, 0, 0)),
            pl.BlockSpec((step, 1, zl, own), lambda g: (g + begin, s, 0, 0)),
            pl.BlockSpec((own, 2 * own), lambda g: (0, 0)),
        ]
        + [pl.BlockSpec(memory_space=pl.ANY)] * len(after),
        out_specs=(
            pl.BlockSpec((n_span, MESH_X * pairs, 2 * zl), lambda g: (0, g, 0)),
            pl.BlockSpec(DONE.shape, lambda g: (0, 0)),
        ),
        compiler_params=pltpu.CompilerParams(vmem_limit_bytes=VMEM_BYTES),
        cost_estimate=lasting(4),
        name="packed_source",
    )(binary, dref, species, laplacian, perm, *after)


def unpack_kernel(part, n_nodes, recv_ref, perm_ref, *refs):
    out_ref = refs[-1]
    n_span = recv_ref.shape[0]
    per_step, _, zl, _ = out_ref.shape
    perm = perm_ref[...]

    def turned(tile):
        top, rest = split_terms(tile)
        both = jnp.concatenate([top, rest], axis=0)
        return lax.dot_general(
            both, perm, (((0,), (0,)), ((), ())), preferred_element_type=f32
        )

    def blocks(count=None):
        pairs = per_step // 2
        for k in range(pairs if count is None else count):
            tile = jnp.concatenate(
                [recv_ref[q, block_rows(part, k, pairs), :] for q in range(n_span)], axis=0
            )
            result = turned(tile)
            out_ref[2 * k, 0] = result[:zl]
            out_ref[2 * k + 1, 0] = result[zl:]

    def tail():
        half = MESH_X // 2
        left = before_tail(n_nodes, per_step)
        blocks(left // 2)
        row = left // 2 * MESH_X
        sides = []
        for q in range(n_span):
            block = recv_ref[q, row : row + half, :]
            sides += [block, pltpu.roll(block, zl, 1)]
        out_ref[left, 0] = turned(jnp.concatenate(sides, axis=0))[:zl]

    by_step(part > 0, blocks, tail)


def unpacked(s, part, recv, perm2, shape, before):
    n_nodes, n_species, zl, own = shape
    n_span, _, width = recv.shape
    begin, steps, _, pairs = part_blocks(n_nodes, part)
    step = 2 * pairs
    operands = [recv, perm2] + ([] if before is None else [before])
    return pl.pallas_call(
        functools.partial(unpack_kernel, part, n_nodes),
        grid=(steps,),
        out_shape=jax.ShapeDtypeStruct(shape, f32),
        in_specs=[
            pl.BlockSpec((n_span, MESH_X * pairs, width), lambda g: (0, g, 0)),
            pl.BlockSpec((2 * own, own), lambda g: (0, 0)),
        ]
        + ([] if before is None else [pl.BlockSpec(memory_space=pl.ANY)]),
        out_specs=pl.BlockSpec((step, 1, zl, own), lambda g: (g + begin, s, 0, 0)),
        input_output_aliases={} if before is None else {2: 0},
        compiler_params=pltpu.CompilerParams(vmem_limit_bytes=UNPACK_BYTES),
        cost_estimate=lasting(0.1),
        name="unpacked",
    )(*operands)


def left_product(matrix, values):
    rows = matrix.shape[0] // 2
    top, rest = split_terms(values)
    both = jnp.dot(matrix, top, preferred_element_type=f32)
    return both[:rows] + both[rows:] + jnp.dot(matrix[:rows], rest, preferred_element_type=f32)


def right_product(values, top_ref, rest_ref):
    rows = values.shape[0]
    top, rest = split_terms(values)
    both = jnp.dot(jnp.concatenate([top, rest], axis=0), top_ref[...], preferred_element_type=f32)
    return both[:rows] + both[rows:] + jnp.dot(top, rest_ref[...], preferred_element_type=f32)


def chunk_rows(index, size):
    return pl.ds(pl.multiple_of(index * size, size), size)


def send_traces(trace_ref, pick_ref, up_ref, down_ref):
    top, rest = split_terms(trace_ref[...])
    out = jnp.dot(pick_ref[...], top, preferred_element_type=f32)
    out = out + jnp.dot(pick_ref[...], rest, preferred_element_type=f32)
    half = up_ref.shape[0]
    up_ref[...] = out[:half]
    down_ref[...] = out[half:]


def sent_block(sent, g, i):
    if len(sent) == 1:
        return sent[0], pl.ds(g * MESH_X * PAIRS + i, PAIRS, stride=MESH_X)
    before = sent[0].shape[1] // (MESH_X * PAIRS)
    if g < before:
        return sent[0], chunk_rows(g * MESH_X + i, PAIRS)
    return sent[1], chunk_rows((g - before) * MESH_X + i, PAIRS)


def sent_tail(sent):
    half = MESH_X // 2
    groups = sum(ref.shape[1] - half * (ref is sent[-1]) for ref in sent) // (MESH_X * PAIRS)
    return groups, sent[-1], sent[-1].shape[1] - half


def start_kernel(*refs):
    *sent, top_ref, rest_ref, diag_ref, eigen_ref, edge_ref, pick_ref = refs[:-6]
    w_ref, trace_ref, up_ref, down_ref, x, ends = refs[-6:]
    n_span = sent[0].shape[0]
    half = MESH_X // 2
    groups, late_ref, tail = sent_tail(sent)
    first = lax.broadcasted_iota(jnp.int32, (8, x.shape[1]), 0) == 0
    for tile in range(n_span // 2):
        lanes = slice(tile * LANES, (tile + 1) * LANES)
        left, right = half_swap(late_ref[2 * tile, tail:, :], late_ref[2 * tile + 1, tail:, :])
        ends[:half, lanes] = left
        ends[half:, lanes] = right

    def quad(c, carry):
        for ii in range(QUAD):
            i = c * QUAD + ii
            for tile in range(n_span // 2):
                lanes = slice(tile * LANES, (tile + 1) * LANES)
                for g in range(groups):
                    ref, block = sent_block(sent, g, i)
                    left, right = half_swap(ref[2 * tile, block, :], ref[2 * tile + 1, block, :])
                    base = ii * NODE_ROWS + g * PAIRS
                    x[base : base + PAIRS, lanes] = left
                    base += groups * PAIRS
                    x[base : base + PAIRS, lanes] = right
            base = ii * NODE_ROWS + 2 * groups * PAIRS
            x[base : base + 8, :] = jnp.where(first, ends[pl.ds(i, 1), :], 0.0)
        y = right_product(x[...], top_ref, rest_ref)
        for p in range(QUAD // 2):
            part = slice(p * 2 * NODE_ROWS, (p + 1) * 2 * NODE_ROWS)
            w = left_product(eigen_ref[...], y[part])
            pair = c * (QUAD // 2) + p
            w_ref[chunk_rows(pair, 2 * NODE_ROWS), :] = w
            trace_ref[chunk_rows(pair, 2 * TRACE_ROWS), :] = left_product(
                edge_ref[...], w * diag_ref[...]
            )
        return carry

    lax.fori_loop(0, MESH_X // QUAD, quad, 0, unroll=True)
    send_traces(trace_ref, pick_ref, up_ref, down_ref)


def fill_sources(trace_ref, above_ref, below_ref, top, rest):
    row = 0
    for ref in (trace_ref, above_ref, below_ref):
        block = slice(row, row + ref.shape[0])
        top[block], rest[block] = split_terms(ref[...])
        row += ref.shape[0]


def met_traces(link_ref, top, rest, met):
    met[...] = jnp.dot(link_ref[...], top[...], preferred_element_type=f32) + jnp.dot(
        link_ref[...], rest[...], preferred_element_type=f32
    )


def sweep_kernel(sweep_id, rounds_ref, diag_ref, link_ref, pick_ref, inner_ref, edge_ref, *refs):
    begun = sweep_id > 1
    start_ref, trace_ref, above_ref, below_ref = refs[:4]
    held_ref = refs[4] if begun else None
    kept_ref, tout_ref, up_ref, down_ref, top, rest, gathered = refs[5 if begun else 4 :]
    fill_sources(trace_ref, above_ref, below_ref, top, rest)
    met_traces(link_ref, top, rest, gathered)
    going = rounds_ref[...] > sweep_id

    def quad(c, carry):
        rows = chunk_rows(c, QUAD * TRACE_ROWS)
        met = gathered[rows, :]
        kept_ref[rows, :] = jnp.where(going, met, held_ref[rows, :] if begun else 0.0)
        for p in range(QUAD // 2):
            part = met[p * 2 * TRACE_ROWS : (p + 1) * 2 * TRACE_ROWS]
            field = left_product(inner_ref[...], part) * diag_ref[...]
            rows = chunk_rows(c * (QUAD // 2) + p, 2 * TRACE_ROWS)
            tout_ref[rows, :] = start_ref[rows, :] + left_product(edge_ref[...], field)
        return carry

    lax.fori_loop(0, MESH_X // QUAD, quad, 0, unroll=True)
    send_traces(tout_ref, pick_ref, up_ref, down_ref)


def finish_kernel(
    sweep_id, rounds_ref, diag_ref, link_ref, inner_ref, nodal_ref, trace_ref, above_ref,
    below_ref, held_ref, w_ref, top_ref, rest_ref, *refs,
):
    *sent, top, rest, gathered, modal, ends = refs
    n_span = sent[0].shape[0]
    half = MESH_X // 2
    groups, late_ref, tail = sent_tail(sent)
    fill_sources(trace_ref, above_ref, below_ref, top, rest)
    met_traces(link_ref, top, rest, gathered)
    going = rounds_ref[...] > sweep_id

    def quad(c, carry):
        rows = chunk_rows(c, QUAD * TRACE_ROWS)
        kept = jnp.where(going, gathered[rows, :], held_ref[rows, :])
        for p in range(QUAD // 2):
            part = kept[p * 2 * TRACE_ROWS : (p + 1) * 2 * TRACE_ROWS]
            rows = chunk_rows(c * (QUAD // 2) + p, 2 * NODE_ROWS)
            field = (w_ref[rows, :] + left_product(inner_ref[...], part)) * diag_ref[...]
            modal[p * 2 * NODE_ROWS : (p + 1) * 2 * NODE_ROWS] = left_product(
                nodal_ref[...], field
            )
        z = right_product(modal[...], top_ref, rest_ref)
        for ii in range(QUAD):
            i = c * QUAD + ii
            for tile in range(n_span // 2):
                lanes = slice(tile * LANES, (tile + 1) * LANES)
                for g in range(groups):
                    base = ii * NODE_ROWS + g * PAIRS
                    later = base + groups * PAIRS
                    left, right = half_swap(
                        z[base : base + PAIRS, lanes], z[later : later + PAIRS, lanes]
                    )
                    ref, block = sent_block(sent, g, i)
                    ref[2 * tile, block, :] = left
                    ref[2 * tile + 1, block, :] = right
            base = ii * NODE_ROWS + 2 * groups * PAIRS
            ends[pl.ds(i, 1), :] = z[base : base + 1]
        return carry

    lax.fori_loop(0, MESH_X // QUAD, quad, 0, unroll=True)
    for tile in range(n_span // 2):
        lanes = slice(tile * LANES, (tile + 1) * LANES)
        left, right = half_swap(ends[:half, lanes], ends[half:, lanes])
        late_ref[2 * tile, tail:, :] = left
        late_ref[2 * tile + 1, tail:, :] = right


def vmem_call(kernel, name, out_shape, scratch, micros, operands, after):
    count, extra = len(operands), len(after)

    def ordered(*refs):
        last = count + extra + len(out_shape)
        refs[last][...] = jnp.zeros_like(refs[last])
        kernel(*refs[:count], *refs[count + extra : last], *refs[last + 1 :])

    vmem = pl.BlockSpec(memory_space=pltpu.VMEM)
    return pl.pallas_call(
        ordered,
        out_shape=tuple(out_shape) + (DONE,),
        in_specs=[vmem] * count + [pl.BlockSpec(memory_space=pl.ANY)] * extra,
        out_specs=tuple([vmem] * (len(out_shape) + 1)),
        scratch_shapes=scratch,
        compiler_params=pltpu.CompilerParams(vmem_limit_bytes=VMEM_BYTES),
        cost_estimate=lasting(micros),
        name=name,
    )(*operands, *after)


def stacked_terms(values):
    return jnp.concatenate(outer_split(values), axis=0)


def twice(matrix):
    zero = jnp.zeros_like(matrix)
    return jnp.concatenate(
        [jnp.concatenate([matrix, zero], axis=1), jnp.concatenate([zero, matrix], axis=1)], axis=0
    )


def nodal_matrices(basis):
    m = basis.shape[0]
    n_nodes = m * m
    kron_basis = (basis[:, None, :, None] * basis[None, :, None, :]).reshape(n_nodes, n_nodes)
    order = np.concatenate(
        [np.arange(0, n_nodes - 1, 2), np.arange(1, n_nodes - 1, 2), [n_nodes - 1]]
    )
    edges = np.array(edge_lists(m)).T.reshape(-1)
    full, edge = NODE_ROWS - n_nodes, TRACE_ROWS - edges.size
    nodal = jnp.pad(kron_basis[order], ((0, full), (0, full)))
    traces = jnp.pad(kron_basis[edges], ((0, edge), (0, full)))
    return [
        stacked_terms(twice(matrix)) for matrix in (nodal.T, traces, coupling * traces.T, nodal)
    ]


def solve_stages(n_sweeps, arrived, sent_shapes, rounds_row, diag, link, pick, matrices, forward, backward):
    eigen, edge, inner, nodal = matrices
    planes = forward[0].shape[0]
    w_shape = jax.ShapeDtypeStruct((MESH_X * NODE_ROWS, planes), f32)
    trace = jax.ShapeDtypeStruct((MESH_X * TRACE_ROWS, planes), f32)
    side = jax.ShapeDtypeStruct((MESH_X * SIDE, planes), f32)
    sources = pltpu.VMEM((link.shape[1], planes), bf16)
    gathered = pltpu.VMEM(trace.shape, f32)
    quad = pltpu.VMEM((QUAD * NODE_ROWS, planes), f32)
    ends = pltpu.VMEM((MESH_X, planes), f32)
    axes = ("span", "elem")
    n_span, n_elem = lax.axis_size("span"), lax.axis_size("elem")

    def exchange(up, down):
        below = lax.ppermute(up, axes, ring_route(n_span, n_elem, 1))
        above = lax.ppermute(down, axes, ring_route(n_span, n_elem, -1))
        return above, below

    after = yield None
    w, start, up, down, mark = vmem_call(
        start_kernel,
        "start_solve",
        [w_shape, trace, side, side],
        [quad, ends],
        16,
        arrived + [forward[0], forward[1], diag, eigen, edge, pick],
        after,
    )
    traces, held = start, []
    for sweep_id in range(1, n_sweeps):
        above, below = exchange(up, down)
        after = yield mark, None
        kept, traces, up, down, mark = vmem_call(
            functools.partial(sweep_kernel, sweep_id),
            "sweep_solve",
            [trace, trace, side, side],
            [sources, sources, gathered],
            10,
            [rounds_row, diag, link, pick, inner, edge, start, traces, above, below] + held,
            after,
        )
        held = [kept]
    above, below = exchange(up, down)
    after = yield mark, None
    *result, mark = vmem_call(
        functools.partial(finish_kernel, n_sweeps),
        "finish_solve",
        [jax.ShapeDtypeStruct(shape, f32) for shape in sent_shapes],
        [sources, sources, gathered, quad, ends],
        17,
        [rounds_row, diag, link, inner, nodal, traces, above, below, kept, w]
        + [backward[0], backward[1]],
        after,
    )
    yield mark, result


def transform_terms(planes):
    modes = np.tile(np.arange(planes // 2), 2)
    angles = np.arange(planes)[:, None] * modes[None, :] % planes * (2 * np.pi / planes)
    real = np.arange(planes)[None, :] < planes // 2
    table = np.where(real, np.cos(angles), -np.sin(angles))
    weights = np.where(modes == 0, 1.0, 2.0)

    def terms(values):
        top = values.astype(bf16)
        return top, (values - top.astype(np.float64)).astype(bf16)

    return terms(table / planes), terms((table * weights[None, :]).T)


def outer_split(values):
    top = lax.reduce_precision(values, exponent_bits=8, mantissa_bits=7)
    return top.astype(bf16), (values - top).astype(bf16)


def row_body(species, laplacian, binary, dref, stiff_eig, basis, rounds, adjacency, edge_map):
    n_nodes, n_species, zl, own = species.shape
    n_span = lax.axis_size("span")
    n_elem = lax.axis_size("elem")
    planes = zl * n_span
    n_modes = planes // 2
    perm, perm2, base, step, send = mesh_tables(adjacency, edge_map, n_span, n_elem)

    def across(sent):
        return lax.all_to_all(sent, "span", split_axis=0, concat_axis=0, tiled=True)

    link, pick = link_matrices(base, step, send, own)
    matrices = nodal_matrices(basis)
    forward, backward = transform_terms(planes)
    col_mode = jnp.tile(jnp.arange(n_modes, dtype=jnp.int32), 2)
    wavenumber = col_mode.astype(f32) * (8.0 / planes)
    shifts = 1.0 / dref[:, None] + (wavenumber * wavenumber)[None, :]
    eig_sum = (stiff_eig[:, None] + stiff_eig[None, :]).reshape(n_nodes)
    eig_sum = jnp.tile(jnp.pad(eig_sum, (0, NODE_ROWS - n_nodes)), 2)
    diag = 1.0 / (shifts[:, None, :] + eig_sum[None, :, None])
    rounds_row = jnp.tile(rounds, 2).reshape(1, planes)

    in_parts = [(WHOLE,) if s == 0 else (0, 1) for s in range(n_species)]
    out_parts = [(WHOLE,) if s + 1 == n_species else (0, 1) for s in range(n_species)]
    steps, count = [], 0
    arrived_by, slots, back_slots = [], [], []
    for parts, slot_list in ((in_parts, slots), (out_parts, back_slots)):
        for group in parts:
            slot_list.append(range(count, count + len(group)))
            count += len(group)
    in_count = slots[-1][-1] + 1
    for s in range(n_species):
        for slot, part in zip(slots[s], in_parts[s]):
            early = min(slot - 2, slots[0][-1] - 1) if slot < 3 else slots[0][-1] - 1
            steps.append((early if slot else -2, 2, slot, s, ("pack", part)))
        first = slots[s][-1]
        for stage in range(N_SWEEPS + 1):
            steps.append((first + stage, 0, s, s, ("solve", stage)))
        for slot, part in zip(back_slots[s], out_parts[s]):
            steps.append((slot, 1, slot, s, ("unpack", part)))
    moved, waiting, solves, mark = [], [], [], []
    updated, last = None, -2
    for arrival, _, _, s, (kind, index) in sorted(steps):
        if arrival > last and waiting:
            final = len(moved) + 1 == count
            moved.append(across(released(waiting.pop(0), mark + ([moved[-1][0, :8]] if final else []))))
        last = arrival
        after = mark + (moved[arrival : arrival + 1] if arrival >= 0 else [])
        if kind == "pack":
            sent, done = packed_source(
                s, index, species, laplacian, binary, dref, perm, n_span, after
            )
            waiting.append(sent)
            mark = [done]
        elif kind == "solve":
            if index == 0:
                shapes = [
                    (n_span, part_blocks(n_nodes, part)[2], 2 * zl) for part in out_parts[s]
                ]
                solves.append(
                    solve_stages(
                        N_SWEEPS, [moved[slot] for slot in slots[s]], shapes, rounds_row, diag[s],
                        link, pick, matrices, forward, backward,
                    )
                )
                next(solves[s])
            done, result = solves[s].send(after)
            mark = [done]
            if result is not None:
                waiting += result
        else:
            updated = unpacked(s, index, moved[arrival], perm2, species.shape, updated)
    return updated


def released(block, after):
    def kernel(*refs):
        pass

    anywhere = pl.BlockSpec(memory_space=pl.ANY)
    return pl.pallas_call(
        kernel,
        out_shape=jax.ShapeDtypeStruct(block.shape, block.dtype),
        in_specs=[anywhere] * (1 + len(after)),
        out_specs=anywhere,
        input_output_aliases={0: 0},
        name="released",
    )(block, *after)


def from_behind(block, axis, distance):
    devices = range(lax.axis_size(axis))
    route = [((i - distance) % len(devices), i) for i in devices]
    return lax.ppermute(block, axis, route)


def edge_matrix(per_side):
    edge_table = np.zeros((4, per_side, per_side * per_side), np.float32)
    for edge_id, node_list in enumerate(edge_lists(per_side)):
        for i, node_id in enumerate(node_list):
            edge_table[edge_id, i, node_id] = 1.0
    return edge_table


def mixture_source(species, laplacian, binary, dref):
    n_species = species.shape[1]
    bath_share = 1.0 - jnp.sum(species, axis=1)
    source_parts = []
    for s in range(n_species):
        resistance = bath_share / binary[s, n_species]
        for j in range(n_species):
            if j != s:
                resistance = resistance + species[:, j] / binary[s, j]
        mixture = (1.0 - species[:, s]) / resistance
        source_parts.append((species[:, s] + (mixture - dref[s]) * laplacian[:, s]) / dref[s])
    return jnp.stack(source_parts, axis=1)


def block_inverse(values, kron_basis, inverse_diag):
    n_nodes = values.shape[0]
    inner_part = (
        jnp.dot(kron_basis.T, values.reshape(n_nodes, -1), precision=highest).reshape(values.shape)
        * inverse_diag
    )
    return jnp.dot(kron_basis, inner_part.reshape(n_nodes, -1), precision=highest).reshape(
        values.shape
    )


def transform_tables(col_mode, col_part, planes):
    plane_ids = jnp.arange(planes, dtype=jnp.int32)
    phase_id = plane_ids[:, None] * col_mode[None, :] % planes
    angles = phase_id.astype(jnp.float32) * (two_pi / planes)
    trig_table = jnp.where(col_part[None, :] == 0, jnp.cos(angles), -jnp.sin(angles))
    weights = jnp.where(col_mode == 0, 1.0, 2.0).astype(jnp.float32)
    return (trig_table / planes, (trig_table * weights[None, :]).T)


def body(species, laplacian, binary, dref, stiff_eig, basis, rounds, adjacency, edge_map):
    per_side = basis.shape[0]
    n_nodes = per_side * per_side
    n_span = lax.axis_size("span")
    n_elem = lax.axis_size("elem")
    planes = species.shape[2] * n_span
    n_modes = planes // 2
    per_device = n_modes // n_span
    half_tile = per_device // 2
    own_count = adjacency.shape[0]
    source = mixture_source(species, laplacian, binary, dref)
    assign = jnp.arange(n_modes, dtype=jnp.int32).reshape(n_span, per_device)
    tile_count = 1
    col_mode = jnp.broadcast_to(
        assign.reshape(n_span, 2, 1, half_tile), (n_span, 2, 2, half_tile)
    ).reshape(planes)
    col_part = jnp.broadcast_to(
        jnp.arange(2, dtype=jnp.int32).reshape(1, 1, 2, 1), (n_span, 2, 2, half_tile)
    ).reshape(planes)
    forward, backward = transform_tables(col_mode, col_part, planes)
    source_swapped = jnp.transpose(source, (0, 1, 3, 2))
    coeffs = jnp.einsum(
        "nsez,zr->nser",
        lax.all_to_all(source_swapped, "span", split_axis=2, concat_axis=3, tiled=True),
        forward,
        precision=highest,
    )
    exchanged = lax.all_to_all(coeffs, "span", split_axis=3, concat_axis=2, tiled=True)
    modal_rhs = jnp.transpose(exchanged, (0, 1, 3, 2))
    columns = 2 * per_device
    my_modes = lax.dynamic_slice_in_dim(col_mode, lax.axis_index("span") * columns, columns)
    my_rounds = rounds[my_modes]
    wavenumber = my_modes.astype(jnp.float32) * (8.0 / planes)
    shifts = 1.0 / dref[:, None] + (wavenumber * wavenumber)[None, :]
    eig_sum = (stiff_eig[:, None] + stiff_eig[None, :]).reshape(n_nodes)
    inverse_diag = 1.0 / (shifts[None, :, :, None] + eig_sum[:, None, None, None])
    kron_basis = (basis[:, None, :, None] * basis[None, :, None, :]).reshape(n_nodes, n_nodes)
    flat_index = np.array(edge_lists(per_side)).reshape(-1)
    scatter_table = jnp.asarray(edge_matrix(per_side))
    owners = adjacency // own_count
    offset = (owners - lax.axis_index("elem") + n_elem) % n_elem
    local_id = adjacency % own_count
    flat_adj = adjacency.reshape(-1)
    flat_offset = offset.reshape(-1)
    earlier = flat_adj[None, :] < flat_adj[:, None]
    from_prev = flat_offset == n_elem - 1
    from_next = flat_offset == 1
    rank_prev = jnp.sum((earlier & from_prev[None, :]).astype(jnp.int32), axis=1)
    rank_next = jnp.sum((earlier & from_next[None, :]).astype(jnp.int32), axis=1)
    position = jnp.where(
        from_prev,
        own_count + rank_prev,
        jnp.where(from_next, own_count + MESH_X + rank_next, local_id.reshape(-1)),
    ).reshape(adjacency.shape)
    slot_ids = jnp.arange(MESH_X, dtype=jnp.int32)
    faces_next = jnp.any(offset == 1, axis=1)
    faces_prev = jnp.any(offset == n_elem - 1, axis=1)
    slot_next = jnp.cumsum(faces_next.astype(jnp.int32)) - 1
    slot_prev = jnp.cumsum(faces_prev.astype(jnp.int32)) - 1
    pick_next = (faces_next[:, None] & (slot_next[:, None] == slot_ids[None, :])).astype(
        jnp.float32
    )
    pick_prev = (faces_prev[:, None] & (slot_prev[:, None] == slot_ids[None, :])).astype(
        jnp.float32
    )

    def gather_pool(traces):
        send_up = jnp.einsum("ktsce,ea->ktsca", traces, pick_next, precision=highest)
        send_down = jnp.einsum("ktsce,ea->ktsca", traces, pick_prev, precision=highest)
        from_before = from_behind(send_up, "elem", 1)
        from_after = from_behind(send_down, "elem", -1)
        return jnp.concatenate([traces, from_before, from_after], axis=4)

    def couple(modal_field):
        traces = modal_field[flat_index].reshape((4, per_side) + modal_field.shape[1:])
        across = gather_pool(traces)[edge_map, :, :, :, position][:, :, ::-1]
        return jnp.einsum("jtn,ejtsc->nsce", scatter_table, across, precision=highest)

    tile_modes = assign.reshape(n_span, tile_count, per_device // tile_count)
    sweep_bound = jnp.max(rounds[tile_modes[:, 0].reshape(-1)])
    initial = block_inverse(modal_rhs, kron_basis, inverse_diag)

    def sweep_once(sweep_id, modal_field):
        proposal = block_inverse(
            modal_rhs + coupling * couple(modal_field), kron_basis, inverse_diag
        )
        return jnp.where(sweep_id < my_rounds[:, None], proposal, modal_field)

    solved = lax.fori_loop(1, sweep_bound, sweep_once, initial)
    solution_swapped = jnp.transpose(solved, (0, 1, 3, 2))
    values = jnp.einsum(
        "nser,rz->nsez",
        lax.all_to_all(solution_swapped, "span", split_axis=2, concat_axis=3, tiled=True),
        backward,
        precision=highest,
    )
    returned = lax.all_to_all(values, "span", split_axis=3, concat_axis=2, tiled=True)
    return jnp.transpose(returned, (0, 1, 3, 2))


def solution(mesh):
    n_span, n_elem = mesh.shape["span"], mesh.shape["elem"]

    def chosen_body(species, *rest):
        zl, own = species.shape[2:]
        by_rows = n_span * MESH_X == own and 2 * zl == LANES == own and n_elem > 2
        by_rows = by_rows and species.shape[0] == SIDE * SIDE
        return (row_body if by_rows else body)(species, *rest)

    return jax.shard_map(
        chosen_body,
        mesh=mesh,
        in_specs=(
            P(None, None, "span", "elem"),
            P(None, None, "span", "elem"),
            P(),
            P(),
            P(),
            P(),
            P(),
            P("elem", None),
            P("elem", None),
        ),
        out_specs=P(None, None, "span", "elem"),
        check_vma=False,
    )
```

```python
import functools

import jax
import jax.numpy as jnp
import numpy as np
from jax import lax
from jax.experimental import pallas as pl
from jax.experimental.pallas import tpu as pltpu
from jax.sharding import PartitionSpec as P

MESH_X = 16
LANES = 128
SIDE = 9
PAIRS = 8
QUAD = 4
NODE_ROWS = 88
TRACE_ROWS = 40
N_SWEEPS = 3
WHOLE = 2
COST_SCALE = 5
DONE = jax.ShapeDtypeStruct((8, LANES), jnp.float32)
VMEM_BYTES = 60 * 1024 * 1024
UNPACK_BYTES = 48 * 1024 * 1024


coupling = 0.2
highest = lax.Precision.HIGHEST
two_pi = 6.283185307179586
f32 = jnp.float32
bf16 = jnp.bfloat16


def edge_lists(per_side):
    last_node = per_side - 1
    bottom = [i for i in range(per_side)]
    right_edge = [i * per_side + last_node for i in range(per_side)]
    top_edge = [last_node * per_side + last_node - i for i in range(per_side)]
    left_edge = [(last_node - i) * per_side for i in range(per_side)]
    return [bottom, right_edge, top_edge, left_edge]


def row_orders(n_span):
    even = [r ^ (r >> 1 & 1) for r in range(n_span)]
    odd = [r ^ int(2 * r >= n_span) for r in range(n_span)][::-1]
    return [even, odd]


def ring_route(n_span, n_elem, step):
    orders = row_orders(n_span)
    places = [orders[p % 2][r] * n_elem + p for p in range(n_elem) for r in range(n_span)]
    count = len(places)
    return [(places[g], places[(g + step) % count]) for g in range(count)]


def lasting(micros):
    return pl.CostEstimate(flops=int(micros * COST_SCALE * 1150000000), bytes_accessed=0, transcendentals=0)


def split_terms(values):
    top = values.astype(bf16)
    return top, (values - top.astype(f32)).astype(bf16)


def half_swap(first, second):
    low = lax.broadcasted_iota(jnp.int32, first.shape, 1) < LANES // 2
    left = jnp.where(low, first, pltpu.roll(second, LANES // 2, 1))
    right = jnp.where(low, pltpu.roll(first, LANES // 2, 1), second)
    return left, right


def tables_kernel(n_span, n_elem, order_only, *refs):
    adj_ref = refs[0]
    own = adj_ref.shape[1]
    span_id, elem_id = lax.axis_index("span"), lax.axis_index("elem")
    lane = lax.broadcasted_iota(jnp.int32, (own, own), 1).astype(f32)
    sub = lax.broadcasted_iota(jnp.int32, (own, own), 0).astype(f32)
    eye = (lane == sub).astype(f32)
    first_own = (elem_id * own).astype(f32)
    first_next = (lax.rem(elem_id + 1, n_elem) * own).astype(f32)
    first_prev = (lax.rem(elem_id + n_elem - 1, n_elem) * own).astype(f32)

    def column(row):
        return jnp.sum(eye * row, axis=1, keepdims=True)

    def inside(ids, first):
        return (ids >= first) & (ids < first + own)

    adj_row = [adj_ref[j : j + 1, :].astype(f32) for j in range(4)]
    meets = [(sub == adj_row[j] - first_own).astype(f32) for j in range(4)]
    near = (eye + meets[0] + meets[1] + meets[2] + meets[3]).astype(bf16)
    prev_row = jnp.zeros((1, own), f32)
    next_row = jnp.zeros((1, own), f32)
    for j in range(4):
        prev_row = prev_row + jnp.where(inside(adj_row[j], first_prev), adj_row[j] + 1.0, 0.0)
        next_row = next_row + jnp.where(inside(adj_row[j], first_next), adj_row[j] + 1.0, 0.0)
    prev_col, next_col = column(prev_row), column(next_row)
    reached = jnp.broadcast_to((prev_col > 0).astype(f32), (own, own))
    row_col = 1.0 - reached
    for _ in range(n_span - 2):
        reached = jnp.minimum(
            jnp.dot(near, reached.astype(bf16), preferred_element_type=f32), 1.0
        )
        row_col = row_col + 1.0 - reached
    row_row = jnp.sum(eye * row_col, axis=0, keepdims=True)
    same = row_col == row_row
    pos_col = jnp.sum((same & (lane < sub)).astype(f32), axis=1, keepdims=True)
    pos_row = jnp.sum((same & (sub < lane)).astype(f32), axis=0, keepdims=True)
    odd = lax.rem(elem_id, 2) == 1
    orders = row_orders(n_span)
    slot_row = jnp.zeros_like(row_row)
    for r in range(n_span):
        slot = jnp.where(odd, orders[1][r], orders[0][r]).astype(f32)
        slot_row = jnp.where(row_row == float(r), slot, slot_row)
    new_row = slot_row * float(MESH_X) + pos_row
    perm = (sub == new_row).astype(f32).astype(bf16)
    if order_only:
        refs[1][:, :own] = perm
        refs[1][:, own:] = perm
        return
    map_ref = refs[1]
    map_row = [map_ref[j : j + 1, :].astype(f32) for j in range(4)]
    perm2_ref, base_ref, step_ref, send_ref = refs[-4:]
    perm2_ref[:own] = perm
    perm2_ref[own:] = perm

    def rank(col, row):
        return jnp.sum(((col > 0) & (col < row)).astype(f32), axis=0, keepdims=True)

    rank_prev, rank_next = rank(prev_col, prev_row), rank(next_col, next_row)
    spot = lax.broadcasted_iota(jnp.int32, (MESH_X, own), 0).astype(f32)
    here = new_row == spot + (span_id * MESH_X).astype(f32)
    edge_up = jnp.zeros_like(row_row)
    edge_down = jnp.zeros_like(row_row)

    def chosen(values):
        picks = jnp.sum(jnp.where(here, values, 0.0), axis=1, keepdims=True)
        return jnp.broadcast_to(picks, (MESH_X, own))

    per_elem = float(TRACE_ROWS)
    per_row = MESH_X * per_elem
    side_rows = float(MESH_X * SIDE)
    for j in range(4):
        its_pos = jnp.sum(meets[j] * pos_col, axis=0, keepdims=True)
        its_row = jnp.sum(meets[j] * row_col, axis=0, keepdims=True)
        inner = inside(adj_row[j], first_own)
        ahead = inside(adj_row[j], first_next)
        behind = inside(adj_row[j], first_prev)
        up = ahead | (inner & (its_row == row_row + 1.0))
        down = behind | (inner & (its_row == row_row - 1.0))
        its_pos = jnp.where(ahead, rank_next, jnp.where(behind, rank_prev, its_pos))
        base = jnp.where(
            up,
            per_row + its_pos,
            jnp.where(down, per_row + side_rows + its_pos, its_pos * per_elem + map_row[j]),
        )
        edge_up = jnp.where(up, float(j), edge_up)
        edge_down = jnp.where(down, float(j), edge_down)
        rows = slice(j * MESH_X, (j + 1) * MESH_X)
        base_ref[rows] = chosen(base)
        step_ref[rows] = chosen(jnp.where(up | down, float(MESH_X), 4.0))
    send_ref[:MESH_X] = chosen(edge_up) + spot * per_elem
    send_ref[MESH_X:] = chosen(edge_down) + spot * per_elem


def element_order(adjacency, n_span, n_elem):
    own = adjacency.shape[0]
    vmem = pl.BlockSpec(memory_space=pltpu.VMEM)
    return pl.pallas_call(
        functools.partial(tables_kernel, n_span, n_elem, True),
        out_shape=jax.ShapeDtypeStruct((own, 2 * own), bf16),
        in_specs=[vmem],
        out_specs=vmem,
        cost_estimate=lasting(2),
        name="element_order",
    )(adjacency.T)


def mesh_tables(adjacency, edge_map, n_span, n_elem, after):
    own = adjacency.shape[0]
    vmem = pl.BlockSpec(memory_space=pltpu.VMEM)
    return pl.pallas_call(
        functools.partial(tables_kernel, n_span, n_elem, False),
        out_shape=(
            jax.ShapeDtypeStruct((2 * own, own), bf16),
            jax.ShapeDtypeStruct((4 * MESH_X, own), f32),
            jax.ShapeDtypeStruct((4 * MESH_X, own), f32),
            jax.ShapeDtypeStruct((2 * MESH_X, own), f32),
        ),
        in_specs=[vmem] * 2 + [pl.BlockSpec(memory_space=pl.ANY)] * len(after),
        out_specs=[vmem] * 4,
        cost_estimate=lasting(3),
        name="mesh_tables",
    )(adjacency.T, edge_map.T, *after)


def link_kernel(
    base_ref, step_ref, send_ref, from_ref, turn_ref, skip_ref, out_ref, move_ref, link_ref, pick_ref
):
    def spread(table, values):
        return jnp.dot(table[...], values[...], precision=highest, preferred_element_type=f32)

    def fill(ref, wanted):
        for c in range(0, ref.shape[1], LANES):
            width = min(LANES, ref.shape[1] - c)
            lane = lax.broadcasted_iota(jnp.int32, wanted.shape, 1).astype(f32) + float(c)
            ref[:, c : c + width] = (wanted == lane).astype(f32).astype(bf16)[:, :width]

    fill(link_ref, spread(from_ref, base_ref) + turn_ref[...] * spread(from_ref, step_ref) + skip_ref[...])
    fill(pick_ref, spread(out_ref, send_ref) + move_ref[...])


def link_matrices(base, step, send, own):
    rows = MESH_X * TRACE_ROWS
    from_edge = np.zeros((rows, 4 * MESH_X), np.float32)
    turn = np.zeros((rows, own), np.float32)
    skip = np.full((rows, own), -1.0, np.float32)
    for i in range(MESH_X):
        for t in range(SIDE):
            for j in range(4):
                row = i * TRACE_ROWS + t * 4 + j
                from_edge[row, j * MESH_X + i] = 1.0
                turn[row] = SIDE - 1 - t
                skip[row] = 0.0
    side_rows = SIDE * MESH_X
    out_edge = np.zeros((2 * side_rows, 2 * MESH_X), np.float32)
    move = np.zeros((2 * side_rows, own), np.float32)
    for way in range(2):
        for t in range(SIDE):
            for i in range(MESH_X):
                row = way * side_rows + t * MESH_X + i
                out_edge[row, way * MESH_X + i] = 1.0
                move[row] = 4 * t
    vmem = pl.BlockSpec(memory_space=pltpu.VMEM)
    return pl.pallas_call(
        link_kernel,
        out_shape=(
            jax.ShapeDtypeStruct((rows, rows + 2 * side_rows), bf16),
            jax.ShapeDtypeStruct((2 * side_rows, rows), bf16),
        ),
        in_specs=[vmem] * 8,
        out_specs=[vmem] * 2,
        cost_estimate=lasting(4),
        name="link_matrices",
    )(base, step, send, from_edge, turn, skip, out_edge, move)


def source_kernel(s, part, n_nodes, binary_ref, dref_ref, species_ref, lap_ref, perm_ref, *refs):
    out_ref, done_ref = refs[-2:]
    done_ref[...] = jnp.zeros_like(done_ref)
    per_step, n_species, zl, own = species_ref.shape
    n_span = out_ref.shape[0]
    perm = perm_ref[...]

    def inverse(value):
        return 1.0 / jnp.full((8, own), value, f32)

    def wide(row):
        return jnp.broadcast_to(row[:1], (zl, own))

    scaled = [dref_ref[s] * inverse(binary_ref[s, j]) for j in range(n_species + 1)]
    bath = wide(scaled[n_species])
    other = [wide(scaled[j] - scaled[n_species]) for j in range(n_species)]
    inv_dref = wide(inverse(dref_ref[s]))

    def source(n):
        parts = [species_ref[n, j] for j in range(n_species)]
        resistance = bath - bath * parts[s]
        for j in range(n_species):
            if j != s:
                resistance = resistance + parts[j] * other[j]
        mixture = (1.0 - parts[s]) * pl.reciprocal(resistance, approx=False)
        return parts[s] * inv_dref + (mixture - 1.0) * lap_ref[n, 0]

    def turned(first, second):
        top, rest = split_terms(jnp.concatenate([first, second], axis=0))
        both = jnp.concatenate([top, rest], axis=1)
        return lax.dot_general(
            perm, both, (((1,), (1,)), ((), ())), preferred_element_type=f32
        )

    def blocks(count=None):
        pairs = per_step // 2
        for k in range(pairs if count is None else count):
            tile = turned(source(2 * k), source(2 * k + 1))
            for q in range(n_span):
                rows = block_rows(part, k, pairs)
                out_ref[q, rows, :] = tile[q * MESH_X : (q + 1) * MESH_X]

    def tail():
        left = before_tail(n_nodes, per_step)
        blocks(left // 2)
        value = source(left)
        tile = turned(value, value)
        half = MESH_X // 2
        low = lax.broadcasted_iota(jnp.int32, (half, 2 * zl), 1) < zl
        for q in range(n_span):
            block = tile[q * MESH_X : (q + 1) * MESH_X]
            row = left // 2 * MESH_X
            out_ref[q, row : row + half, :] = jnp.where(low, block[:half], block[half:])

    by_step(part > 0, blocks, tail)


def block_rows(part, k, pairs):
    if part == WHOLE:
        return slice(k * MESH_X, (k + 1) * MESH_X)
    return pl.ds(k, MESH_X, stride=pairs)


def before_tail(n_nodes, per_step):
    return (n_nodes - 1) % per_step


def by_step(has_tail, blocks, tail):
    if not has_tail:
        blocks()
        return
    last_step = pl.num_programs(0) - 1
    pl.when(pl.program_id(0) < last_step)(blocks)
    pl.when(pl.program_id(0) == last_step)(tail)


def part_blocks(n_nodes, part):
    groups = n_nodes // (2 * PAIRS)
    rows = MESH_X * PAIRS
    first = groups // 2
    if part == 0:
        return 0, first, first * rows, PAIRS
    if part == WHOLE:
        return 0, -(-n_nodes // (4 * PAIRS)), groups * rows + MESH_X // 2, 2 * PAIRS
    return first, groups - first + 1, (groups - first) * rows + MESH_X // 2, PAIRS


def packed_source(s, part, species, laplacian, binary, dref, perm, n_span, after):
    n_nodes, n_species, zl, own = species.shape
    begin, steps, rows, pairs = part_blocks(n_nodes, part)
    step = 2 * pairs
    return pl.pallas_call(
        functools.partial(source_kernel, s, part, n_nodes),
        grid=(steps,),
        out_shape=(jax.ShapeDtypeStruct((n_span, rows, 2 * zl), f32), DONE),
        in_specs=[
            pl.BlockSpec(memory_space=pltpu.SMEM),
            pl.BlockSpec(memory_space=pltpu.SMEM),
            pl.BlockSpec((step, n_species, zl, own), lambda g: (g + begin, 0, 0, 0)),
            pl.BlockSpec((step, 1, zl, own), lambda g: (g + begin, s, 0, 0)),
            pl.BlockSpec((own, 2 * own), lambda g: (0, 0)),
        ]
        + [pl.BlockSpec(memory_space=pl.ANY)] * len(after),
        out_specs=(
            pl.BlockSpec((n_span, MESH_X * pairs, 2 * zl), lambda g: (0, g, 0)),
            pl.BlockSpec(DONE.shape, lambda g: (0, 0)),
        ),
        compiler_params=pltpu.CompilerParams(vmem_limit_bytes=VMEM_BYTES),
        cost_estimate=lasting(4),
        name="packed_source",
    )(binary, dref, species, laplacian, perm, *after)


def unpack_kernel(part, n_nodes, recv_ref, perm_ref, *refs):
    out_ref = refs[-1]
    n_span = recv_ref.shape[0]
    per_step, _, zl, _ = out_ref.shape
    perm = perm_ref[...]

    def turned(tile):
        top, rest = split_terms(tile)
        both = jnp.concatenate([top, rest], axis=0)
        return lax.dot_general(
            both, perm, (((0,), (0,)), ((), ())), preferred_element_type=f32
        )

    def blocks(count=None):
        pairs = per_step // 2
        for k in range(pairs if count is None else count):
            tile = jnp.concatenate(
                [recv_ref[q, block_rows(part, k, pairs), :] for q in range(n_span)], axis=0
            )
            result = turned(tile)
            out_ref[2 * k, 0] = result[:zl]
            out_ref[2 * k + 1, 0] = result[zl:]

    def tail():
        half = MESH_X // 2
        left = before_tail(n_nodes, per_step)
        blocks(left // 2)
        row = left // 2 * MESH_X
        sides = []
        for q in range(n_span):
            block = recv_ref[q, row : row + half, :]
            sides += [block, pltpu.roll(block, zl, 1)]
        out_ref[left, 0] = turned(jnp.concatenate(sides, axis=0))[:zl]

    by_step(part > 0, blocks, tail)


def unpacked(s, part, recv, perm2, shape, before):
    n_nodes, n_species, zl, own = shape
    n_span, _, width = recv.shape
    begin, steps, _, pairs = part_blocks(n_nodes, part)
    step = 2 * pairs
    operands = [recv, perm2] + ([] if before is None else [before])
    return pl.pallas_call(
        functools.partial(unpack_kernel, part, n_nodes),
        grid=(steps,),
        out_shape=jax.ShapeDtypeStruct(shape, f32),
        in_specs=[
            pl.BlockSpec((n_span, MESH_X * pairs, width), lambda g: (0, g, 0)),
            pl.BlockSpec((2 * own, own), lambda g: (0, 0)),
        ]
        + ([] if before is None else [pl.BlockSpec(memory_space=pl.ANY)]),
        out_specs=pl.BlockSpec((step, 1, zl, own), lambda g: (g + begin, s, 0, 0)),
        input_output_aliases={} if before is None else {2: 0},
        compiler_params=pltpu.CompilerParams(vmem_limit_bytes=UNPACK_BYTES),
        cost_estimate=lasting(0.1),
        name="unpacked",
    )(*operands)


def left_product(matrix, values):
    rows = matrix.shape[0] // 2
    top, rest = split_terms(values)
    both = jnp.dot(matrix, top, preferred_element_type=f32)
    return both[:rows] + both[rows:] + jnp.dot(matrix[:rows], rest, preferred_element_type=f32)


def right_product(values, top_ref, rest_ref):
    rows = values.shape[0]
    top, rest = split_terms(values)
    both = jnp.dot(jnp.concatenate([top, rest], axis=0), top_ref[...], preferred_element_type=f32)
    return both[:rows] + both[rows:] + jnp.dot(top, rest_ref[...], preferred_element_type=f32)


def chunk_rows(index, size):
    return pl.ds(pl.multiple_of(index * size, size), size)


def send_traces(trace_ref, pick_ref, up_ref, down_ref):
    top, rest = split_terms(trace_ref[...])
    out = jnp.dot(pick_ref[...], top, preferred_element_type=f32)
    out = out + jnp.dot(pick_ref[...], rest, preferred_element_type=f32)
    half = up_ref.shape[0]
    up_ref[...] = out[:half]
    down_ref[...] = out[half:]


def sent_block(sent, g, i):
    if len(sent) == 1:
        return sent[0], pl.ds(g * MESH_X * PAIRS + i, PAIRS, stride=MESH_X)
    before = sent[0].shape[1] // (MESH_X * PAIRS)
    if g < before:
        return sent[0], chunk_rows(g * MESH_X + i, PAIRS)
    return sent[1], chunk_rows((g - before) * MESH_X + i, PAIRS)


def sent_tail(sent):
    half = MESH_X // 2
    groups = sum(ref.shape[1] - half * (ref is sent[-1]) for ref in sent) // (MESH_X * PAIRS)
    return groups, sent[-1], sent[-1].shape[1] - half


def start_kernel(*refs):
    *sent, top_ref, rest_ref, diag_ref, eigen_ref, edge_ref, pick_ref = refs[:-6]
    w_ref, trace_ref, up_ref, down_ref, x, ends = refs[-6:]
    n_span = sent[0].shape[0]
    half = MESH_X // 2
    groups, late_ref, tail = sent_tail(sent)
    first = lax.broadcasted_iota(jnp.int32, (8, x.shape[1]), 0) == 0
    for tile in range(n_span // 2):
        lanes = slice(tile * LANES, (tile + 1) * LANES)
        left, right = half_swap(late_ref[2 * tile, tail:, :], late_ref[2 * tile + 1, tail:, :])
        ends[:half, lanes] = left
        ends[half:, lanes] = right

    def quad(c, carry):
        for ii in range(QUAD):
            i = c * QUAD + ii
            for tile in range(n_span // 2):
                lanes = slice(tile * LANES, (tile + 1) * LANES)
                for g in range(groups):
                    ref, block = sent_block(sent, g, i)
                    left, right = half_swap(ref[2 * tile, block, :], ref[2 * tile + 1, block, :])
                    base = ii * NODE_ROWS + g * PAIRS
                    x[base : base + PAIRS, lanes] = left
                    base += groups * PAIRS
                    x[base : base + PAIRS, lanes] = right
            base = ii * NODE_ROWS + 2 * groups * PAIRS
            x[base : base + 8, :] = jnp.where(first, ends[pl.ds(i, 1), :], 0.0)
        y = right_product(x[...], top_ref, rest_ref)
        for p in range(QUAD // 2):
            part = slice(p * 2 * NODE_ROWS, (p + 1) * 2 * NODE_ROWS)
            w = left_product(eigen_ref[...], y[part])
            pair = c * (QUAD // 2) + p
            w_ref[chunk_rows(pair, 2 * NODE_ROWS), :] = w
            trace_ref[chunk_rows(pair, 2 * TRACE_ROWS), :] = left_product(
                edge_ref[...], w * diag_ref[...]
            )
        return carry

    lax.fori_loop(0, MESH_X // QUAD, quad, 0, unroll=True)
    send_traces(trace_ref, pick_ref, up_ref, down_ref)


def fill_sources(trace_ref, above_ref, below_ref, top, rest):
    row = 0
    for ref in (trace_ref, above_ref, below_ref):
        block = slice(row, row + ref.shape[0])
        top[block], rest[block] = split_terms(ref[...])
        row += ref.shape[0]


def met_traces(link_ref, top, rest, met):
    met[...] = jnp.dot(link_ref[...], top[...], preferred_element_type=f32) + jnp.dot(
        link_ref[...], rest[...], preferred_element_type=f32
    )


def sweep_kernel(sweep_id, rounds_ref, diag_ref, link_ref, pick_ref, inner_ref, edge_ref, *refs):
    begun = sweep_id > 1
    start_ref, trace_ref, above_ref, below_ref = refs[:4]
    held_ref = refs[4] if begun else None
    kept_ref, tout_ref, up_ref, down_ref, top, rest, gathered = refs[5 if begun else 4 :]
    fill_sources(trace_ref, above_ref, below_ref, top, rest)
    met_traces(link_ref, top, rest, gathered)
    going = rounds_ref[...] > sweep_id

    def quad(c, carry):
        rows = chunk_rows(c, QUAD * TRACE_ROWS)
        met = gathered[rows, :]
        kept_ref[rows, :] = jnp.where(going, met, held_ref[rows, :] if begun else 0.0)
        for p in range(QUAD // 2):
            part = met[p * 2 * TRACE_ROWS : (p + 1) * 2 * TRACE_ROWS]
            field = left_product(inner_ref[...], part) * diag_ref[...]
            rows = chunk_rows(c * (QUAD // 2) + p, 2 * TRACE_ROWS)
            tout_ref[rows, :] = start_ref[rows, :] + left_product(edge_ref[...], field)
        return carry

    lax.fori_loop(0, MESH_X // QUAD, quad, 0, unroll=True)
    send_traces(tout_ref, pick_ref, up_ref, down_ref)


def finish_kernel(
    sweep_id, rounds_ref, diag_ref, link_ref, inner_ref, nodal_ref, trace_ref, above_ref,
    below_ref, held_ref, w_ref, top_ref, rest_ref, *refs,
):
    *sent, top, rest, gathered, modal, ends = refs
    n_span = sent[0].shape[0]
    half = MESH_X // 2
    groups, late_ref, tail = sent_tail(sent)
    fill_sources(trace_ref, above_ref, below_ref, top, rest)
    met_traces(link_ref, top, rest, gathered)
    going = rounds_ref[...] > sweep_id

    def quad(c, carry):
        rows = chunk_rows(c, QUAD * TRACE_ROWS)
        kept = jnp.where(going, gathered[rows, :], held_ref[rows, :])
        for p in range(QUAD // 2):
            part = kept[p * 2 * TRACE_ROWS : (p + 1) * 2 * TRACE_ROWS]
            rows = chunk_rows(c * (QUAD // 2) + p, 2 * NODE_ROWS)
            field = (w_ref[rows, :] + left_product(inner_ref[...], part)) * diag_ref[...]
            modal[p * 2 * NODE_ROWS : (p + 1) * 2 * NODE_ROWS] = left_product(
                nodal_ref[...], field
            )
        z = right_product(modal[...], top_ref, rest_ref)
        for ii in range(QUAD):
            i = c * QUAD + ii
            for tile in range(n_span // 2):
                lanes = slice(tile * LANES, (tile + 1) * LANES)
                for g in range(groups):
                    base = ii * NODE_ROWS + g * PAIRS
                    later = base + groups * PAIRS
                    left, right = half_swap(
                        z[base : base + PAIRS, lanes], z[later : later + PAIRS, lanes]
                    )
                    ref, block = sent_block(sent, g, i)
                    ref[2 * tile, block, :] = left
                    ref[2 * tile + 1, block, :] = right
            base = ii * NODE_ROWS + 2 * groups * PAIRS
            ends[pl.ds(i, 1), :] = z[base : base + 1]
        return carry

    lax.fori_loop(0, MESH_X // QUAD, quad, 0, unroll=True)
    for tile in range(n_span // 2):
        lanes = slice(tile * LANES, (tile + 1) * LANES)
        left, right = half_swap(ends[:half, lanes], ends[half:, lanes])
        late_ref[2 * tile, tail:, :] = left
        late_ref[2 * tile + 1, tail:, :] = right


def vmem_call(kernel, name, out_shape, scratch, micros, operands, after):
    count, extra = len(operands), len(after)

    def ordered(*refs):
        last = count + extra + len(out_shape)
        refs[last][...] = jnp.zeros_like(refs[last])
        kernel(*refs[:count], *refs[count + extra : last], *refs[last + 1 :])

    vmem = pl.BlockSpec(memory_space=pltpu.VMEM)
    return pl.pallas_call(
        ordered,
        out_shape=tuple(out_shape) + (DONE,),
        in_specs=[vmem] * count + [pl.BlockSpec(memory_space=pl.ANY)] * extra,
        out_specs=tuple([vmem] * (len(out_shape) + 1)),
        scratch_shapes=scratch,
        compiler_params=pltpu.CompilerParams(vmem_limit_bytes=VMEM_BYTES),
        cost_estimate=lasting(micros),
        name=name,
    )(*operands, *after)


def stacked_terms(values):
    return jnp.concatenate(outer_split(values), axis=0)


def twice(matrix):
    zero = jnp.zeros_like(matrix)
    return jnp.concatenate(
        [jnp.concatenate([matrix, zero], axis=1), jnp.concatenate([zero, matrix], axis=1)], axis=0
    )


def nodal_matrices(basis):
    m = basis.shape[0]
    n_nodes = m * m
    kron_basis = (basis[:, None, :, None] * basis[None, :, None, :]).reshape(n_nodes, n_nodes)
    order = np.concatenate(
        [np.arange(0, n_nodes - 1, 2), np.arange(1, n_nodes - 1, 2), [n_nodes - 1]]
    )
    edges = np.array(edge_lists(m)).T.reshape(-1)
    full, edge = NODE_ROWS - n_nodes, TRACE_ROWS - edges.size
    nodal = jnp.pad(kron_basis[order], ((0, full), (0, full)))
    traces = jnp.pad(kron_basis[edges], ((0, edge), (0, full)))
    return [
        stacked_terms(twice(matrix)) for matrix in (nodal.T, traces, coupling * traces.T, nodal)
    ]


def solve_stages(n_sweeps, arrived, sent_shapes, rounds_row, diag, link, pick, matrices, forward, backward):
    eigen, edge, inner, nodal = matrices
    planes = forward[0].shape[0]
    w_shape = jax.ShapeDtypeStruct((MESH_X * NODE_ROWS, planes), f32)
    trace = jax.ShapeDtypeStruct((MESH_X * TRACE_ROWS, planes), f32)
    side = jax.ShapeDtypeStruct((MESH_X * SIDE, planes), f32)
    sources = pltpu.VMEM((link.shape[1], planes), bf16)
    gathered = pltpu.VMEM(trace.shape, f32)
    quad = pltpu.VMEM((QUAD * NODE_ROWS, planes), f32)
    ends = pltpu.VMEM((MESH_X, planes), f32)
    axes = ("span", "elem")
    n_span, n_elem = lax.axis_size("span"), lax.axis_size("elem")

    def exchange(up, down):
        below = lax.ppermute(up, axes, ring_route(n_span, n_elem, 1))
        above = lax.ppermute(down, axes, ring_route(n_span, n_elem, -1))
        return above, below

    after = yield None
    w, start, up, down, mark = vmem_call(
        start_kernel,
        "start_solve",
        [w_shape, trace, side, side],
        [quad, ends],
        16,
        arrived + [forward[0], forward[1], diag, eigen, edge, pick],
        after,
    )
    traces, held = start, []
    for sweep_id in range(1, n_sweeps):
        above, below = exchange(up, down)
        after = yield mark, None
        kept, traces, up, down, mark = vmem_call(
            functools.partial(sweep_kernel, sweep_id),
            "sweep_solve",
            [trace, trace, side, side],
            [sources, sources, gathered],
            10,
            [rounds_row, diag, link, pick, inner, edge, start, traces, above, below] + held,
            after,
        )
        held = [kept]
    above, below = exchange(up, down)
    after = yield mark, None
    *result, mark = vmem_call(
        functools.partial(finish_kernel, n_sweeps),
        "finish_solve",
        [jax.ShapeDtypeStruct(shape, f32) for shape in sent_shapes],
        [sources, sources, gathered, quad, ends],
        17,
        [rounds_row, diag, link, inner, nodal, traces, above, below, kept, w]
        + [backward[0], backward[1]],
        after,
    )
    yield mark, result


def transform_terms(planes):
    modes = np.tile(np.arange(planes // 2), 2)
    angles = np.arange(planes)[:, None] * modes[None, :] % planes * (2 * np.pi / planes)
    real = np.arange(planes)[None, :] < planes // 2
    table = np.where(real, np.cos(angles), -np.sin(angles))
    weights = np.where(modes == 0, 1.0, 2.0)

    def terms(values):
        top = values.astype(bf16)
        return top, (values - top.astype(np.float64)).astype(bf16)

    return terms(table / planes), terms((table * weights[None, :]).T)


def outer_split(values):
    top = lax.reduce_precision(values, exponent_bits=8, mantissa_bits=7)
    return top.astype(bf16), (values - top).astype(bf16)


def row_body(species, laplacian, binary, dref, stiff_eig, basis, rounds, adjacency, edge_map):
    n_nodes, n_species, zl, own = species.shape
    n_span = lax.axis_size("span")
    n_elem = lax.axis_size("elem")
    planes = zl * n_span
    n_modes = planes // 2
    perm = element_order(adjacency, n_span, n_elem)

    def across(sent):
        return lax.all_to_all(sent, "span", split_axis=0, concat_axis=0, tiled=True)

    matrices = nodal_matrices(basis)
    forward, backward = transform_terms(planes)
    col_mode = jnp.tile(jnp.arange(n_modes, dtype=jnp.int32), 2)
    wavenumber = col_mode.astype(f32) * (8.0 / planes)
    shifts = 1.0 / dref[:, None] + (wavenumber * wavenumber)[None, :]
    eig_sum = (stiff_eig[:, None] + stiff_eig[None, :]).reshape(n_nodes)
    eig_sum = jnp.tile(jnp.pad(eig_sum, (0, NODE_ROWS - n_nodes)), 2)
    diag = 1.0 / (shifts[:, None, :] + eig_sum[None, :, None])
    rounds_row = jnp.tile(rounds, 2).reshape(1, planes)

    in_parts = [(WHOLE,) if s == 0 else (0, 1) for s in range(n_species)]
    out_parts = [(WHOLE,) if s + 1 == n_species else (0, 1) for s in range(n_species)]
    steps, count = [], 0
    arrived_by, slots, back_slots = [], [], []
    for parts, slot_list in ((in_parts, slots), (out_parts, back_slots)):
        for group in parts:
            slot_list.append(range(count, count + len(group)))
            count += len(group)
    in_count = slots[-1][-1] + 1
    for s in range(n_species):
        for slot, part in zip(slots[s], in_parts[s]):
            early = min(slot - 2, slots[0][-1] - 1) if slot < 3 else slots[0][-1] - 1
            steps.append((early if slot else -2, 2, slot, s, ("pack", part)))
        first = slots[s][-1]
        for stage in range(N_SWEEPS + 1):
            steps.append((first + stage, 0, s, s, ("solve", stage)))
        for slot, part in zip(back_slots[s], out_parts[s]):
            steps.append((slot, 1, slot, s, ("unpack", part)))
    moved, waiting, solves, mark = [], [], [], []
    updated, last = None, -2
    for arrival, _, _, s, (kind, index) in sorted(steps):
        if arrival > last and waiting:
            final = len(moved) + 1 == count
            moved.append(across(released(waiting.pop(0), mark + ([moved[-1][0, :8]] if final else []))))
        last = arrival
        after = mark + (moved[arrival : arrival + 1] if arrival >= 0 else [])
        if kind == "pack":
            sent, done = packed_source(
                s, index, species, laplacian, binary, dref, perm, n_span, after
            )
            waiting.append(sent)
            mark = [done]
            if arrival < -1:
                perm2, *ends = mesh_tables(adjacency, edge_map, n_span, n_elem, mark)
                link, pick = link_matrices(*ends, own)
        elif kind == "solve":
            if index == 0:
                shapes = [
                    (n_span, part_blocks(n_nodes, part)[2], 2 * zl) for part in out_parts[s]
                ]
                solves.append(
                    solve_stages(
                        N_SWEEPS, [moved[slot] for slot in slots[s]], shapes, rounds_row, diag[s],
                        link, pick, matrices, forward, backward,
                    )
                )
                next(solves[s])
            done, result = solves[s].send(after)
            mark = [done]
            if result is not None:
                waiting += result
        else:
            updated = unpacked(s, index, moved[arrival], perm2, species.shape, updated)
    return updated


def released(block, after):
    def kernel(*refs):
        pass

    anywhere = pl.BlockSpec(memory_space=pl.ANY)
    return pl.pallas_call(
        kernel,
        out_shape=jax.ShapeDtypeStruct(block.shape, block.dtype),
        in_specs=[anywhere] * (1 + len(after)),
        out_specs=anywhere,
        input_output_aliases={0: 0},
        name="released",
    )(block, *after)


def from_behind(block, axis, distance):
    devices = range(lax.axis_size(axis))
    route = [((i - distance) % len(devices), i) for i in devices]
    return lax.ppermute(block, axis, route)


def edge_matrix(per_side):
    edge_table = np.zeros((4, per_side, per_side * per_side), np.float32)
    for edge_id, node_list in enumerate(edge_lists(per_side)):
        for i, node_id in enumerate(node_list):
            edge_table[edge_id, i, node_id] = 1.0
    return edge_table


def mixture_source(species, laplacian, binary, dref):
    n_species = species.shape[1]
    bath_share = 1.0 - jnp.sum(species, axis=1)
    source_parts = []
    for s in range(n_species):
        resistance = bath_share / binary[s, n_species]
        for j in range(n_species):
            if j != s:
                resistance = resistance + species[:, j] / binary[s, j]
        mixture = (1.0 - species[:, s]) / resistance
        source_parts.append((species[:, s] + (mixture - dref[s]) * laplacian[:, s]) / dref[s])
    return jnp.stack(source_parts, axis=1)


def block_inverse(values, kron_basis, inverse_diag):
    n_nodes = values.shape[0]
    inner_part = (
        jnp.dot(kron_basis.T, values.reshape(n_nodes, -1), precision=highest).reshape(values.shape)
        * inverse_diag
    )
    return jnp.dot(kron_basis, inner_part.reshape(n_nodes, -1), precision=highest).reshape(
        values.shape
    )


def transform_tables(col_mode, col_part, planes):
    plane_ids = jnp.arange(planes, dtype=jnp.int32)
    phase_id = plane_ids[:, None] * col_mode[None, :] % planes
    angles = phase_id.astype(jnp.float32) * (two_pi / planes)
    trig_table = jnp.where(col_part[None, :] == 0, jnp.cos(angles), -jnp.sin(angles))
    weights = jnp.where(col_mode == 0, 1.0, 2.0).astype(jnp.float32)
    return (trig_table / planes, (trig_table * weights[None, :]).T)


def body(species, laplacian, binary, dref, stiff_eig, basis, rounds, adjacency, edge_map):
    per_side = basis.shape[0]
    n_nodes = per_side * per_side
    n_span = lax.axis_size("span")
    n_elem = lax.axis_size("elem")
    planes = species.shape[2] * n_span
    n_modes = planes // 2
    per_device = n_modes // n_span
    half_tile = per_device // 2
    own_count = adjacency.shape[0]
    source = mixture_source(species, laplacian, binary, dref)
    assign = jnp.arange(n_modes, dtype=jnp.int32).reshape(n_span, per_device)
    tile_count = 1
    col_mode = jnp.broadcast_to(
        assign.reshape(n_span, 2, 1, half_tile), (n_span, 2, 2, half_tile)
    ).reshape(planes)
    col_part = jnp.broadcast_to(
        jnp.arange(2, dtype=jnp.int32).reshape(1, 1, 2, 1), (n_span, 2, 2, half_tile)
    ).reshape(planes)
    forward, backward = transform_tables(col_mode, col_part, planes)
    source_swapped = jnp.transpose(source, (0, 1, 3, 2))
    coeffs = jnp.einsum(
        "nsez,zr->nser",
        lax.all_to_all(source_swapped, "span", split_axis=2, concat_axis=3, tiled=True),
        forward,
        precision=highest,
    )
    exchanged = lax.all_to_all(coeffs, "span", split_axis=3, concat_axis=2, tiled=True)
    modal_rhs = jnp.transpose(exchanged, (0, 1, 3, 2))
    columns = 2 * per_device
    my_modes = lax.dynamic_slice_in_dim(col_mode, lax.axis_index("span") * columns, columns)
    my_rounds = rounds[my_modes]
    wavenumber = my_modes.astype(jnp.float32) * (8.0 / planes)
    shifts = 1.0 / dref[:, None] + (wavenumber * wavenumber)[None, :]
    eig_sum = (stiff_eig[:, None] + stiff_eig[None, :]).reshape(n_nodes)
    inverse_diag = 1.0 / (shifts[None, :, :, None] + eig_sum[:, None, None, None])
    kron_basis = (basis[:, None, :, None] * basis[None, :, None, :]).reshape(n_nodes, n_nodes)
    flat_index = np.array(edge_lists(per_side)).reshape(-1)
    scatter_table = jnp.asarray(edge_matrix(per_side))
    owners = adjacency // own_count
    offset = (owners - lax.axis_index("elem") + n_elem) % n_elem
    local_id = adjacency % own_count
    flat_adj = adjacency.reshape(-1)
    flat_offset = offset.reshape(-1)
    earlier = flat_adj[None, :] < flat_adj[:, None]
    from_prev = flat_offset == n_elem - 1
    from_next = flat_offset == 1
    rank_prev = jnp.sum((earlier & from_prev[None, :]).astype(jnp.int32), axis=1)
    rank_next = jnp.sum((earlier & from_next[None, :]).astype(jnp.int32), axis=1)
    position = jnp.where(
        from_prev,
        own_count + rank_prev,
        jnp.where(from_next, own_count + MESH_X + rank_next, local_id.reshape(-1)),
    ).reshape(adjacency.shape)
    slot_ids = jnp.arange(MESH_X, dtype=jnp.int32)
    faces_next = jnp.any(offset == 1, axis=1)
    faces_prev = jnp.any(offset == n_elem - 1, axis=1)
    slot_next = jnp.cumsum(faces_next.astype(jnp.int32)) - 1
    slot_prev = jnp.cumsum(faces_prev.astype(jnp.int32)) - 1
    pick_next = (faces_next[:, None] & (slot_next[:, None] == slot_ids[None, :])).astype(
        jnp.float32
    )
    pick_prev = (faces_prev[:, None] & (slot_prev[:, None] == slot_ids[None, :])).astype(
        jnp.float32
    )

    def gather_pool(traces):
        send_up = jnp.einsum("ktsce,ea->ktsca", traces, pick_next, precision=highest)
        send_down = jnp.einsum("ktsce,ea->ktsca", traces, pick_prev, precision=highest)
        from_before = from_behind(send_up, "elem", 1)
        from_after = from_behind(send_down, "elem", -1)
        return jnp.concatenate([traces, from_before, from_after], axis=4)

    def couple(modal_field):
        traces = modal_field[flat_index].reshape((4, per_side) + modal_field.shape[1:])
        across = gather_pool(traces)[edge_map, :, :, :, position][:, :, ::-1]
        return jnp.einsum("jtn,ejtsc->nsce", scatter_table, across, precision=highest)

    tile_modes = assign.reshape(n_span, tile_count, per_device // tile_count)
    sweep_bound = jnp.max(rounds[tile_modes[:, 0].reshape(-1)])
    initial = block_inverse(modal_rhs, kron_basis, inverse_diag)

    def sweep_once(sweep_id, modal_field):
        proposal = block_inverse(
            modal_rhs + coupling * couple(modal_field), kron_basis, inverse_diag
        )
        return jnp.where(sweep_id < my_rounds[:, None], proposal, modal_field)

    solved = lax.fori_loop(1, sweep_bound, sweep_once, initial)
    solution_swapped = jnp.transpose(solved, (0, 1, 3, 2))
    values = jnp.einsum(
        "nser,rz->nsez",
        lax.all_to_all(solution_swapped, "span", split_axis=2, concat_axis=3, tiled=True),
        backward,
        precision=highest,
    )
    returned = lax.all_to_all(values, "span", split_axis=3, concat_axis=2, tiled=True)
    return jnp.transpose(returned, (0, 1, 3, 2))


def solution(mesh):
    n_span, n_elem = mesh.shape["span"], mesh.shape["elem"]

    def chosen_body(species, *rest):
        zl, own = species.shape[2:]
        by_rows = n_span * MESH_X == own and 2 * zl == LANES == own and n_elem > 2
        by_rows = by_rows and species.shape[0] == SIDE * SIDE
        return (row_body if by_rows else body)(species, *rest)

    return jax.shard_map(
        chosen_body,
        mesh=mesh,
        in_specs=(
            P(None, None, "span", "elem"),
            P(None, None, "span", "elem"),
            P(),
            P(),
            P(),
            P(),
            P(),
            P("elem", None),
            P("elem", None),
        ),
        out_specs=P(None, None, "span", "elem"),
        check_vma=False,
    )
```
